32 devices in a mesh: dp: 8 (over y, x, core), tensor: 4 (over z).
Axes of the slice: x: 2, y: 2, z: 4, core: 2. Of those that a mesh axis runs over, the one named last changes fastest.
Arguments:
- tokens: bfloat16 [25088, 1024], P(('dp', 'tensor')), may hold values from -6 to 6
- cotangent: bfloat16 [25088, 1024], P(('dp', 'tensor')), may hold values from -6 to 6
- norm_first: float32 [1024], replicated, may hold values from 0.1 to 1.9
- norm_second: float32 [1024], replicated, may hold values from 0.1 to 1.9
- entry_weight: bfloat16 [1024, 3, 1024], P('dp', None, 'tensor'), may hold values from -0.1875 to 0.1875
- output_weight: bfloat16 [1024, 1024], P('dp', 'tensor'), may hold values from -4 to 4
- expand_weight: bfloat16 [1024, 4096], P('dp', 'tensor'), may hold values from -0.1875 to 0.1875
- shrink_weight: bfloat16 [1024, 4096], P('dp', 'tensor'), may hold values from -0.09375 to 0.09375
- entry_down: bfloat16 [8, 1024, 16], replicated, may hold values from -0.1875 to 0.1875
- entry_up: bfloat16 [8, 16, 3, 1024], P(None, None, None, 'tensor'), may hold values from -1 to 1
- output_down: bfloat16 [8, 1024, 16], P(None, 'tensor'), may hold values from -4 to 4
- output_up: bfloat16 [8, 16, 1024], replicated, may hold values from -1.5 to 1.5
- expand_down: bfloat16 [8, 1024, 16], replicated, may hold values from -0.1875 to 0.1875
- expand_up: bfloat16 [8, 16, 4096], P(None, None, 'tensor'), may hold values from -1 to 1
- shrink_down: bfloat16 [8, 4096, 16], P(None, 'tensor'), may hold values from -0.09375 to 0.09375
- shrink_up: bfloat16 [8, 16, 1024], replicated, may hold values from -1 to 1
- adapter_choice: int32 [16], P('dp'), may hold values from 0 to 7
- clip_count: int32 [8], P('dp'), may hold values from 1 to 2, as said below
Outputs:
- mixed: bfloat16 [25088, 1024], P(('dp', 'tensor'))
- token_grad: bfloat16 [25088, 1024], P(('dp', 'tensor'))
- entry_down_grad: float32 [8, 1024, 16], replicated
- entry_up_grad: float32 [8, 16, 3, 1024], P(None, None, None, 'tensor')
- output_down_grad: float32 [8, 1024, 16], P(None, 'tensor')
- output_up_grad: float32 [8, 16, 1024], replicated
- expand_down_grad: float32 [8, 1024, 16], replicated
- expand_up_grad: float32 [8, 16, 4096], P(None, None, 'tensor')
- shrink_down_grad: float32 [8, 4096, 16], P(None, 'tensor')
- shrink_up_grad: float32 [8, 16, 1024], replicated
The draws below stay inside these ranges and needn't reach their ends.
Inputs may be any that keep to these rules, and one draw needn't show every extreme that they name: The first clip_count[i] of the 2 slots of dp index i hold clips, the rest are empty; some index has all 2 slots live.
All inputs are finite; a program needn't handle non-finite values.
Results may differ from the reference program's by a relative error of at most 0.02.
Values may be sent and summed in bfloat16 or wider, within the bound.
A program may use at most 256 MiB of HBM per device.

```python
import jax
import jax.numpy as jnp
from jax import lax

D = 1024
HEADS = 16
HEAD_DIM = 64
FF = 4096
RANK = 16
ADAPTERS = 8
L = 1568
CAP = 2
SLOTS = 16
TOKENS = 25088
N_DP = 8
N_TENSOR = 4


def draw_clip_count(key, part):
    key = jax.random.fold_in(key, 7)
    first_key, second_key = jax.random.split(key)
    counts = jax.random.randint(first_key, (N_DP,), 1, CAP + 1)
    fullest = jax.random.randint(second_key, (), 0, N_DP)
    return jnp.where(lax.iota(jnp.int32, N_DP) == fullest, CAP, counts).astype(jnp.int32)


def with_ends(entries, stream_key, smallest, top_value):
    longest = entries.shape.index(max(entries.shape))
    spots = []
    for shift in (0, 1):
        where = [jax.random.randint(jax.random.fold_in(stream_key, axis), (), 0, length) for axis, length in enumerate(entries.shape)]
        where[longest] = (where[longest] + shift) % entries.shape[longest]
        spots.append(tuple(where))
    return entries.at[spots[0]].set(smallest).at[spots[1]].set(top_value)


def level_of(stream_key, shape, shards, low, largest):
    def one(dim, parts):
        steps = jax.random.uniform(jax.random.fold_in(jax.random.fold_in(stream_key, 6), dim), (parts,), jnp.float32, low / len(shards), largest / len(shards))
        return jnp.repeat(jnp.exp(steps), shape[dim] // parts).reshape((-1,) + (1,) * (len(shape) - dim - 1))

    level = one(*shards[0])
    for cut in shards[1:]:
        level = level * one(*cut)
    return level


def noise(stream_key, extent, scale, most, cuts=(), kind=jnp.bfloat16):
    entries = scale * jax.random.normal(stream_key, extent, jnp.float32)
    if cuts:
        entries = entries * level_of(stream_key, extent, cuts, -0.22, 0.18)
    return jnp.clip(entries, -most, most).astype(kind)


def setup_inputs(seed: int = 0) -> dict:
    keys = jax.random.split(jax.random.key(seed), 19)
    tokens = noise(keys[0], (TOKENS, D), 1.0, 6.0, ((0, 32),))
    cotangent = noise(keys[1], (TOKENS, D), 1.0, 6.0, ((0, 32),))
    norm_first = jnp.clip(1.0 + 0.18 * jax.random.normal(keys[2], (D,), jnp.float32), 0.1, 1.9)
    norm_second = jnp.clip(1.0 + 0.18 * jax.random.normal(keys[3], (D,), jnp.float32), 0.1, 1.9)
    entry_weight = noise(keys[4], (D, 3, D), D ** -0.5, 0.1875, ((0, 8), (2, 4)))
    output_weight = noise(keys[5], (D, D), (max(1, 4 * D // L)) ** -0.5, 4.0, ((0, 8), (1, 4)))
    expand_weight = noise(keys[6], (D, FF), D ** -0.5, 0.1875, ((0, 8), (1, 4)))
    shrink_weight = noise(keys[7], (D, FF), FF ** -0.5, 0.09375, ((0, 8), (1, 4)))
    entry_down = noise(keys[8], (ADAPTERS, D, RANK), D ** -0.5, 0.1875)
    entry_up = noise(keys[9], (ADAPTERS, RANK, 3, D), (2 * RANK) ** -0.5, 1.0, ((3, 4),))
    output_down = noise(keys[10], (ADAPTERS, D, RANK), (max(1, 4 * D // L)) ** -0.5, 4.0, ((1, 4),))
    output_up = noise(keys[11], (ADAPTERS, RANK, D), RANK ** -0.5, 1.5)
    expand_down = noise(keys[12], (ADAPTERS, D, RANK), D ** -0.5, 0.1875)
    expand_up = noise(keys[13], (ADAPTERS, RANK, FF), (2 * RANK) ** -0.5, 1.0, ((2, 4),))
    shrink_down = noise(keys[14], (ADAPTERS, FF, RANK), FF ** -0.5, 0.09375, ((1, 4),))
    shrink_up = noise(keys[15], (ADAPTERS, RANK, D), (2 * RANK) ** -0.5, 1.0)
    adapter_choice = with_ends(jax.random.randint(keys[16], (SLOTS,), 0, ADAPTERS), jax.random.fold_in(keys[16], 1), 0, ADAPTERS - 1).astype(jnp.int32)
    clip_count = draw_clip_count(jax.random.fold_in(keys[18], 71), 0)
    return dict(tokens=tokens, cotangent=cotangent, norm_first=norm_first, norm_second=norm_second, entry_weight=entry_weight, output_weight=output_weight, expand_weight=expand_weight, shrink_weight=shrink_weight, entry_down=entry_down, entry_up=entry_up, output_down=output_down, output_up=output_up, expand_down=expand_down, expand_up=expand_up, shrink_down=shrink_down, shrink_up=shrink_up, adapter_choice=adapter_choice, clip_count=clip_count)


highest_precision = lax.Precision.HIGHEST

@jax.custom_vjp
def low(v):
    return lax.optimization_barrier(v.astype(jnp.bfloat16)).astype(jnp.float32)

@jax.custom_vjp
def low_back(v):
    return v

def low_keep(v):
    return (low(v), None)

def low_pass(kept, grad):
    return (grad,)

def back_keep(v):
    return (v, None)

def back_low(kept, grad):
    return (low(grad),)
low.defvjp(low_keep, low_pass)
low_back.defvjp(back_keep, back_low)

def normalize(values):
    centre = lax.optimization_barrier(jnp.mean(values, axis=-1, keepdims=True))
    shifted = values - centre
    spread = lax.optimization_barrier(jnp.mean(shifted * shifted, axis=-1, keepdims=True))
    return shifted * lax.rsqrt(spread + 1e-05)

def grouped_branch(rows, weight, down_map, up_map):
    groups = N_TENSOR
    width = rows.shape[1]
    group_width = width // groups
    length = rows.shape[0]
    row_groups = rows.reshape(length, groups, group_width)
    paths = jnp.einsum('tgi,gir->gtr', row_groups, down_map.reshape(groups, group_width, down_map.shape[1]), precision=highest_precision)
    terms = jnp.einsum('tgi,ogi->gto', row_groups, weight.reshape(weight.shape[0], groups, group_width), precision=highest_precision)
    terms = terms + jnp.einsum('gtr,ro->gto', paths, up_map, precision=highest_precision)
    return lax.optimization_barrier(jnp.sum(low(terms), axis=0))

def clip_layer(inputs, frozen, chosen):
    norm_first, norm_second, entry_weight, output_weight, expand_weight, shrink_weight = frozen
    entry_down, entry_up, output_down, output_up, expand_down, expand_up, shrink_down, shrink_up = chosen
    length = inputs.shape[0]
    normed = low(normalize(inputs) * norm_first)
    entry_lowrank_path = jnp.dot(normed, entry_down, precision=highest_precision)
    projected_rows = jnp.einsum('td,dje->tje', normed, entry_weight, precision=highest_precision)
    projected_rows = projected_rows + jnp.einsum('tr,rje->tje', entry_lowrank_path, entry_up, precision=highest_precision)
    projected_rows = low(low_back(projected_rows))
    queries = projected_rows[:, 0].reshape(length, HEADS, HEAD_DIM)
    keys_all = projected_rows[:, 1].reshape(length, HEADS, HEAD_DIM)
    values_all = projected_rows[:, 2].reshape(length, HEADS, HEAD_DIM)
    scores = low_back(jnp.einsum('qhd,khd->hqk', queries, keys_all, precision=highest_precision) * HEAD_DIM ** (-0.5))
    probs_low = low(jax.nn.softmax(scores, axis=-1))
    attended = jnp.einsum('hqk,khd->qhd', probs_low, values_all, precision=highest_precision).reshape(length, D)
    attended = low(low_back(attended))
    branch = grouped_branch(attended, output_weight, output_down, output_up)
    middle = inputs + low_back(branch)
    second = low(normalize(middle) * norm_second)
    expand_lowrank_path = jnp.dot(second, expand_down, precision=highest_precision)
    hidden_activation = jnp.dot(second, expand_weight, precision=highest_precision) + jnp.dot(expand_lowrank_path, expand_up, precision=highest_precision)
    hidden_activation = low_back(hidden_activation)
    activated = low(jax.nn.gelu(hidden_activation, approximate=False))
    branch_two = grouped_branch(activated, shrink_weight, shrink_down, shrink_up)
    return middle + low_back(branch_two)

def reference(tokens, cotangent, norm_first, norm_second, entry_weight, output_weight, expand_weight, shrink_weight, entry_down, entry_up, output_down, output_up, expand_down, expand_up, shrink_down, shrink_up, adapter_choice, clip_count):
    slot_count = adapter_choice.shape[0]
    capacity = slot_count // N_DP
    frozen = (norm_first.astype(jnp.float32), norm_second.astype(jnp.float32), entry_weight.astype(jnp.float32), output_weight.astype(jnp.float32), expand_weight.astype(jnp.float32), shrink_weight.astype(jnp.float32))
    adapters = tuple((table.astype(jnp.float32) for table in (entry_down, entry_up, output_down, output_up, expand_down, expand_up, shrink_down, shrink_up)))
    inputs = tokens.astype(jnp.float32).reshape(slot_count, L, D)
    position = jnp.arange(slot_count, dtype=jnp.int32)
    alive_flag = (position % capacity < clip_count[position // capacity]).astype(jnp.float32)

    def forward(inputs, adapters):

        def advance(running, element):
            clip_inputs, choice_index, flag_value = element
            chosen = tuple((table[choice_index] for table in adapters))
            result = jax.checkpoint(clip_layer)(clip_inputs, frozen, chosen)
            return (running, result * flag_value)
        _, results = lax.scan(advance, jnp.zeros((), jnp.float32), (inputs, adapter_choice, alive_flag))
        return results
    results, pullback = jax.vjp(forward, inputs, adapters)
    input_grad, gradients = pullback(cotangent.astype(jnp.float32).reshape(slot_count, L, D))
    mixed = results.reshape(slot_count * L, D).astype(jnp.bfloat16)
    token_grad = input_grad.reshape(slot_count * L, D).astype(jnp.bfloat16)
    return (mixed, token_grad, gradients[0], gradients[1], gradients[2], gradients[3], gradients[4], gradients[5], gradients[6], gradients[7])
```

```python
import functools

import jax
import jax.numpy as jnp
from jax import lax
from jax.experimental import pallas as pl
from jax.experimental.pallas import tpu as pltpu
from jax.sharding import PartitionSpec as P

HEAD_DIM = 64
PAIR = 2 * HEAD_DIM
RANK = 16
LOG2E = 1.4426950408889634
LN2 = 0.6931471805599453
F32, BF = jnp.float32, jnp.bfloat16
VMEM_LIMIT = 60 * 2**20


def dot(a, b, ca, cb):
    return lax.dot_general(a, b, (((ca,), (cb,)), ((), ())), preferred_element_type=F32)


def params(**more):
    return pltpu.CompilerParams(vmem_limit_bytes=VMEM_LIMIT, **more)


def merge_rows(block):
    return block.reshape(block.shape[0] * block.shape[1], block.shape[2])


def norm_parts(values):
    centre = jnp.mean(values, axis=-1, keepdims=True)
    shifted = values - centre
    scale = lax.rsqrt(jnp.mean(shifted * shifted, axis=-1, keepdims=True) + 1e-05)
    return shifted * scale, scale


def norm_back(hat, scale, gain, grad):
    inner = grad * gain
    mean_one = jnp.mean(inner, axis=-1, keepdims=True)
    mean_two = jnp.mean(inner * hat, axis=-1, keepdims=True)
    return scale * (inner - mean_one - hat * mean_two)


def entry_kernel(
    tok_ref, gain_ref, w_ref, down_ref, up_ref, q_ref, k_ref, v_ref, normed_ref, inner_t_ref, inner_ref
):
    @pl.when(pl.program_id(0) == 0)
    def _():
        hat, _ = norm_parts(tok_ref[...].astype(F32))
        normed = (hat * gain_ref[...]).astype(BF)
        normed_ref[...] = normed
        inner_ref[...] = dot(normed, down_ref[...], 1, 1).astype(BF)
        inner_t_ref[...] = dot(down_ref[...], normed, 1, 1).astype(BF)

    normed = normed_ref[...]
    inner = inner_ref[...]
    for which, (out, scale) in enumerate(((q_ref, HEAD_DIM**-0.5 * LOG2E), (k_ref, None), (v_ref, None))):
        part = dot(normed, merge_rows(w_ref[:, which]), 1, 0) + dot(inner, up_ref[which], 1, 0)
        if scale is not None:
            part = part * scale
        out[...] = part.astype(BF)


def entry_forward(tok, gain, w, down, up):
    rows, width = tok.shape
    n_dp, n_t, _, depth, cols = w.shape
    whole = lambda shape: pl.BlockSpec(shape, lambda i: (0,) * len(shape))
    return pl.pallas_call(
        entry_kernel,
        grid=(n_t,),
        in_specs=[
            whole((rows, width)),
            whole((1, width)),
            pl.BlockSpec((n_dp, None, 3, depth, cols), lambda i: (0, i, 0, 0, 0)),
            whole((RANK, width)),
            pl.BlockSpec((None, 3, RANK, cols), lambda i: (i, 0, 0, 0)),
        ],
        out_specs=[pl.BlockSpec((rows, cols), lambda i: (0, i))] * 3
        + [whole((rows, width)), whole((RANK, rows))],
        out_shape=[jax.ShapeDtypeStruct((rows, width), BF)] * 4 + [jax.ShapeDtypeStruct((RANK, rows), BF)],
        scratch_shapes=[pltpu.VMEM((rows, RANK), BF)],
        compiler_params=params(),
        name="entry_forward",
    )(tok, gain, w, down, up)


def head_masks(shape):
    lane = lax.broadcasted_iota(jnp.int32, shape, 1)
    return lane < HEAD_DIM, lane >= HEAD_DIM


def ones_lanes(rows, count):
    lane = lax.broadcasted_iota(jnp.int32, (rows, PAIR), 1)
    return jnp.where(lane < count, 1.0, 0.0).astype(BF)


def attend_kernel(q_ref, k_ref, v_ref, o_ref, lse_ref):
    rows = q_ref.shape[0]
    keys = k_ref[...]
    length = keys.shape[0]
    values = jnp.concatenate([v_ref[...], ones_lanes(length, 1)], axis=1)
    queries = q_ref[...]
    zero = jnp.zeros_like(queries)
    outs, sums = [], []
    for mask in head_masks(queries.shape):
        scores = dot(jnp.where(mask, queries, zero), keys, 1, 1)
        top = jnp.max(scores, axis=1, keepdims=True)
        probs = jnp.exp2(scores - top).astype(BF)
        mixed = dot(probs, values, 1, 0)
        total = mixed[:, PAIR : PAIR + 1]
        outs.append(mixed[:, :PAIR] / total)
        sums.append(top + jnp.log2(total))
    first, _ = head_masks((rows, PAIR))
    o_ref[...] = jnp.where(first, outs[0], outs[1]).astype(BF)
    lse_ref[...] = jnp.where(first, sums[0], sums[1])


def attention_forward(q, k, v):
    rows, width = q.shape
    length = k.shape[0]
    pair = lambda n: pl.BlockSpec((n, PAIR), lambda h: (0, h))
    return pl.pallas_call(
        attend_kernel,
        grid=(width // PAIR,),
        in_specs=[pair(rows), pair(length), pair(length)],
        out_specs=[pair(rows), pair(rows)],
        out_shape=[jax.ShapeDtypeStruct((rows, width), BF), jax.ShapeDtypeStruct((rows, width), F32)],
        compiler_params=params(),
        name="attention_forward",
    )(q, k, v)


def split_lanes(column):
    column = -column
    high = column.astype(BF)
    rest = column - high.astype(F32)
    mid = rest.astype(BF)
    low = (rest - mid.astype(F32)).astype(BF)
    lane = lax.broadcasted_iota(jnp.int32, (column.shape[0], PAIR), 1)
    zero = jnp.zeros((column.shape[0], PAIR), BF)
    return jnp.where(lane == 0, high, jnp.where(lane == 1, mid, jnp.where(lane == 2, low, zero)))


def attend_back_kernel(q_ref, k_ref, v_ref, o_ref, lse_ref, do_ref, dq_ref, dk_ref, dv_ref):
    rows = q_ref.shape[0]
    keys = k_ref[...]
    length = keys.shape[0]
    ones = ones_lanes(length, 3)
    keys_more = jnp.concatenate([keys, ones], axis=1)
    values_more = jnp.concatenate([v_ref[...], ones], axis=1)
    queries, grad = q_ref[...], do_ref[...]
    zero = jnp.zeros_like(queries)
    product = grad.astype(F32) * o_ref[...].astype(F32)
    d_queries, d_keys, d_values = [], 0.0, 0.0
    for head, mask in enumerate(head_masks(queries.shape)):
        query = jnp.where(mask, queries, zero)
        grad_head = jnp.where(mask, grad, zero)
        lse = lse_ref[:, head * HEAD_DIM : head * HEAD_DIM + 1]
        delta = jnp.sum(jnp.where(mask, product, 0.0), axis=1, keepdims=True)
        probs = jnp.exp2(dot(jnp.concatenate([query, split_lanes(lse)], axis=1), keys_more, 1, 1))
        slope = dot(jnp.concatenate([grad_head, split_lanes(delta)], axis=1), values_more, 1, 1)
        score_grad = (probs * slope).astype(BF)
        d_queries.append(dot(score_grad, keys, 1, 0))
        d_values = d_values + dot(grad_head, probs.astype(BF), 0, 0)
        d_keys = d_keys + dot(query, score_grad, 0, 0)
    first, _ = head_masks((rows, PAIR))
    dq_ref[...] = (jnp.where(first, d_queries[0], d_queries[1]) * HEAD_DIM**-0.5).astype(BF)
    dk_ref[...] = (d_keys * LN2).T.astype(BF)
    dv_ref[...] = d_values.T.astype(BF)


def attention_backward(q, k, v, o, lse, do):
    rows, width = q.shape
    length = k.shape[0]
    pair = lambda n: pl.BlockSpec((n, PAIR), lambda h: (0, h))
    return pl.pallas_call(
        attend_back_kernel,
        grid=(width // PAIR,),
        in_specs=[pair(rows), pair(length), pair(length), pair(rows), pair(rows), pair(rows)],
        out_specs=[pair(rows), pair(length), pair(length)],
        out_shape=[
            jax.ShapeDtypeStruct((rows, width), BF),
            jax.ShapeDtypeStruct((length, width), BF),
            jax.ShapeDtypeStruct((length, width), BF),
        ],
        compiler_params=params(),
        name="attention_backward",
    )(q, k, v, o, lse, do)


def gelu_parts(hidden):
    share = 0.5 * (1.0 + lax.erf(hidden * 0.7071067811865476))
    density = jnp.exp(-0.5 * hidden * hidden) * 0.3989422804014327
    return hidden * share, share + hidden * density


def middle_kernel(
    alive_ref, x_ref, att_ref, cot_ref, gain_ref, wo_ref, we_ref, ws_ref,
    o_down_ref, o_up_ref, e_down_ref, e_up_ref, s_down_ref, s_up_ref,
    mixed_ref, mgrad_ref, agrad_ref, od_g_ref, ou_g_ref, ed_g_ref, eu_g_ref, sd_g_ref, su_g_ref,
    middle_ref, second_ref, dy_ref, acc2_ref, acc3_ref, einner_ref, einner_t_ref, sback_ref, sback_t_ref,
    sinner_ref, eback_ref, oinner_ref,
):
    step = pl.program_id(0)
    alive = alive_ref[0]
    n_t = wo_ref.shape[1]
    cols = wo_ref.shape[3]

    @pl.when(step == 0)
    def _():
        branch, inner = 0.0, 0.0
        for t in range(n_t):
            att = att_ref[:, t * cols : (t + 1) * cols]
            branch = branch + dot(att, merge_rows(wo_ref[:, t]), 1, 1)
            inner = inner + dot(att, o_down_ref[t], 1, 1)
        inner = inner.astype(BF)
        oinner_ref[...] = inner
        middle = x_ref[...].astype(F32) + (branch + dot(inner, o_up_ref[...], 1, 0))
        middle_ref[...] = middle
        hat, _ = norm_parts(middle)
        second = (hat * gain_ref[...]).astype(BF)
        second_ref[...] = second
        dy = (cot_ref[...].astype(F32) * alive).astype(BF)
        dy_ref[...] = dy
        einner_ref[...] = dot(second, e_down_ref[...], 1, 1).astype(BF)
        einner_t_ref[...] = dot(e_down_ref[...], second, 1, 1).astype(BF)
        sback_ref[...] = dot(dy, s_up_ref[...], 1, 1).astype(BF)
        sback_t_ref[...] = dot(s_up_ref[...], dy, 1, 1).astype(BF)
        acc2_ref[...] = jnp.zeros_like(acc2_ref)
        acc3_ref[...] = jnp.zeros_like(acc3_ref)
        sinner_ref[...] = jnp.zeros_like(sinner_ref)
        eback_ref[...] = jnp.zeros_like(eback_ref)

    we, ws = merge_rows(we_ref[...]), merge_rows(ws_ref[...])
    e_up, s_down = e_up_ref[...], s_down_ref[...]
    hidden = dot(second_ref[...], we, 1, 0) + dot(einner_ref[...], e_up, 1, 0)
    value, slope = gelu_parts(hidden)
    act = value.astype(BF)
    acc2_ref[...] += dot(act, ws, 1, 1)
    sinner_ref[...] += dot(act, s_down, 1, 1)
    act_grad = dot(dy_ref[...], ws, 1, 0) + dot(sback_ref[...], s_down, 1, 0)
    hid_grad = (act_grad * slope).astype(BF)
    acc3_ref[...] += dot(hid_grad, we, 1, 1)
    eback_ref[...] += dot(hid_grad, e_up, 1, 1)
    sd_g_ref[...] = dot(sback_t_ref[...], act, 1, 0)
    eu_g_ref[...] = dot(einner_t_ref[...], hid_grad, 1, 0)

    @pl.when(step == pl.num_programs(0) - 1)
    def _():
        s_inner, e_back = sinner_ref[...].astype(BF), eback_ref[...].astype(BF)
        middle = middle_ref[...]
        mixed_ref[...] = (alive * (middle + (acc2_ref[...] + dot(s_inner, s_up_ref[...], 1, 0)))).astype(BF)
        su_g_ref[...] = dot(s_inner, dy_ref[...], 0, 0)
        ed_g_ref[...] = dot(e_back, second_ref[...], 0, 0)
        second_grad = acc3_ref[...] + dot(e_back, e_down_ref[...], 1, 0)
        hat, scale = norm_parts(middle)
        mgrad = cot_ref[...].astype(F32) * alive + norm_back(hat, scale, gain_ref[...], second_grad)
        mgrad_ref[...] = mgrad
        low = mgrad.astype(BF)
        o_back = dot(low, o_up_ref[...], 1, 1).astype(BF)
        for t in range(n_t):
            agrad_ref[:, t * cols : (t + 1) * cols] = (
                dot(low, merge_rows(wo_ref[:, t]), 1, 0) + dot(o_back, o_down_ref[t], 1, 0)
            ).astype(BF)
        od_g_ref[...] = dot(o_back, att_ref[...], 0, 0)
        ou_g_ref[...] = dot(oinner_ref[...], low, 0, 0)


def middle_both_ways(alive, x, att, cot, gain, wo, we, ws, o_down, o_up, e_down, e_up, s_down, s_up):
    rows, width = x.shape
    n_dp, n_t, depth, hid = we.shape
    sub = max(1, hid // 512)
    step_cols = hid // sub
    whole = lambda shape: pl.BlockSpec(shape, lambda i: (0,) * len(shape))
    chunk = pl.BlockSpec((n_dp, None, depth, step_cols), lambda i: (0, i // sub, 0, i % sub))
    thin = pl.BlockSpec((None, RANK, step_cols), lambda i: (i // sub, 0, i % sub))
    ff = n_t * hid
    return pl.pallas_call(
        middle_kernel,
        grid=(n_t * sub,),
        in_specs=[
            pl.BlockSpec(memory_space=pltpu.SMEM),
            whole((rows, width)), whole((rows, width)), whole((rows, width)), whole((1, width)),
            whole(wo.shape), chunk, chunk,
            whole(o_down.shape), whole((RANK, width)), whole((RANK, width)), thin, thin, whole((RANK, width)),
        ],
        out_specs=[
            whole((rows, width)), whole((rows, width)), whole((rows, width)),
            whole((RANK, width)), whole((RANK, width)), whole((RANK, width)),
            pl.BlockSpec((RANK, step_cols), lambda i: (0, i)), pl.BlockSpec((RANK, step_cols), lambda i: (0, i)),
            whole((RANK, width)),
        ],
        out_shape=[
            jax.ShapeDtypeStruct((rows, width), BF), jax.ShapeDtypeStruct((rows, width), F32),
            jax.ShapeDtypeStruct((rows, width), BF),
            jax.ShapeDtypeStruct((RANK, width), F32), jax.ShapeDtypeStruct((RANK, width), F32),
            jax.ShapeDtypeStruct((RANK, width), F32), jax.ShapeDtypeStruct((RANK, ff), F32),
            jax.ShapeDtypeStruct((RANK, ff), F32), jax.ShapeDtypeStruct((RANK, width), F32),
        ],
        scratch_shapes=[
            pltpu.VMEM((rows, width), F32), pltpu.VMEM((rows, width), BF), pltpu.VMEM((rows, width), BF),
            pltpu.VMEM((rows, width), F32), pltpu.VMEM((rows, width), F32),
            pltpu.VMEM((rows, RANK), BF), pltpu.VMEM((RANK, rows), BF),
            pltpu.VMEM((rows, RANK), BF), pltpu.VMEM((RANK, rows), BF),
            pltpu.VMEM((rows, RANK), F32), pltpu.VMEM((rows, RANK), F32), pltpu.VMEM((rows, RANK), BF),
        ],
        compiler_params=params(),
        name="middle_both_ways",
    )(alive, x, att, cot, gain, wo, we, ws, o_down, o_up, e_down, e_up, s_down, s_up)


def entry_back_kernel(
    tok_ref, gain_ref, mgrad_ref, normed_ref, inner_t_ref, dq_ref, dk_ref, dv_ref, dk2_ref, dv2_ref,
    w_ref, down_ref, up_ref, tgrad_ref, down_g_ref, up_g_ref, acc_ref, back_ref,
):
    @pl.when(pl.program_id(0) == 0)
    def _():
        acc_ref[...] = jnp.zeros_like(acc_ref)
        back_ref[...] = jnp.zeros_like(back_ref)

    acc, back = acc_ref[...], back_ref[...]
    add = lambda a, b: (a[...].astype(F32) + b[...].astype(F32)).astype(BF)
    for which, grad in enumerate((dq_ref[...], add(dk_ref, dk2_ref), add(dv_ref, dv2_ref))):
        acc = acc + dot(grad, merge_rows(w_ref[:, which]), 1, 1)
        back = back + dot(grad, up_ref[which], 1, 1)
        up_g_ref[which] = dot(inner_t_ref[...], grad, 1, 0)
    acc_ref[...] = acc
    back_ref[...] = back

    @pl.when(pl.program_id(0) == pl.num_programs(0) - 1)
    def _():
        back = back_ref[...].astype(BF)
        first_grad = acc_ref[...] + dot(back, down_ref[...], 1, 0)
        down_g_ref[...] = dot(back, normed_ref[...], 0, 0)
        hat, scale = norm_parts(tok_ref[...].astype(F32))
        tgrad_ref[...] = (mgrad_ref[...] + norm_back(hat, scale, gain_ref[...], first_grad)).astype(BF)


def entry_backward(tok, gain, mgrad, normed, inner_t, dq, dk, dv, dk2, dv2, w, down, up):
    rows, width = tok.shape
    n_dp, n_t, _, depth, cols = w.shape
    whole = lambda shape: pl.BlockSpec(shape, lambda i: (0,) * len(shape))
    return pl.pallas_call(
        entry_back_kernel,
        grid=(n_t,),
        in_specs=[
            whole((rows, width)), whole((1, width)), whole((rows, width)), whole((rows, width)),
            whole((RANK, rows)),
            *[pl.BlockSpec((rows, cols), lambda i: (0, i))] * 5,
            pl.BlockSpec((n_dp, None, 3, depth, cols), lambda i: (0, i, 0, 0, 0)),
            whole((RANK, width)),
            pl.BlockSpec((None, 3, RANK, cols), lambda i: (i, 0, 0, 0)),
        ],
        out_specs=[
            whole((rows, width)), whole((RANK, width)),
            pl.BlockSpec((None, 3, RANK, cols), lambda i: (i, 0, 0, 0)),
        ],
        out_shape=[
            jax.ShapeDtypeStruct((rows, width), BF), jax.ShapeDtypeStruct((RANK, width), F32),
            jax.ShapeDtypeStruct((n_t, 3, RANK, cols), F32),
        ],
        scratch_shapes=[pltpu.VMEM((rows, width), F32), pltpu.VMEM((rows, RANK), F32)],
        compiler_params=params(),
        name="entry_backward",
    )(tok, gain, mgrad, normed, inner_t, dq, dk, dv, dk2, dv2, w, down, up)


class Places:
    def __init__(self, n_dp, n_t, cap):
        self.n_dp, self.n_t, self.cap = n_dp, n_t, cap
        self.group = n_t // cap
        self.half = self.group // 2

    def swapped(self, dp, t):
        core, slot, j = dp % 2, t // self.group, t % self.group
        return dp - core + j // self.half, slot * self.group + core * self.half + j % self.half

    def swap_pairs(self):
        pairs = []
        for dp in range(self.n_dp):
            for t in range(self.n_t):
                to = self.swapped(dp, t)
                pairs.append((dp * self.n_t + t, to[0] * self.n_t + to[1]))
        return pairs

    def mate(self, dp, t, shift):
        core, j = dp % 2, t % self.group
        block = (core * self.half + j % self.half + shift) % self.group
        return dp - core + block // self.half, t - j % self.half + block % self.half

    def mate_pairs(self, shift):
        pairs = []
        for dp in range(self.n_dp):
            for t in range(self.n_t):
                to = self.mate(dp, t, shift)
                pairs.append((dp * self.n_t + t, to[0] * self.n_t + to[1]))
        return pairs

    def owner(self, dp, t):
        return self.swapped(dp, t)[0] * self.cap + t // self.group


BOTH = ("dp", "tensor")


def local(
    tokens, cotangent, norm_first, norm_second, entry_weight, output_weight, expand_weight, shrink_weight,
    entry_down, entry_up, output_down, output_up, expand_down, expand_up, shrink_down, shrink_up,
    adapter_choice, clip_count,
):
    n_dp, n_t, cap = lax.axis_size("dp"), lax.axis_size("tensor"), adapter_choice.shape[0]
    dp, t = lax.axis_index("dp"), lax.axis_index("tensor")
    places = Places(n_dp, n_t, cap)
    rows, width = tokens.shape
    adapters = entry_down.shape[0]
    cols, hid = output_weight.shape[1], expand_weight.shape[1]

    choices = lax.all_gather(adapter_choice, "dp", axis=0, tiled=True)
    counts = lax.all_gather(clip_count, "dp", axis=0, tiled=True)
    owner = places.owner(dp, t)
    mine = choices[owner]
    alive = (owner % cap < counts[owner // cap]).astype(F32).reshape(1)

    tok = lax.ppermute(tokens, BOTH, places.swap_pairs())
    cot = lax.ppermute(cotangent, BOTH, places.swap_pairs())
    gather = lambda w: lax.all_gather(w, BOTH, axis=0).reshape(n_dp, n_t, *w.shape)
    full_entry = gather(entry_weight.transpose(1, 0, 2))
    full_output = gather(output_weight)
    full_expand = gather(expand_weight)
    full_shrink = gather(shrink_weight)

    thin = jnp.concatenate(
        [
            entry_up.transpose(0, 2, 1, 3).reshape(adapters, 3 * RANK, cols).reshape(adapters, 3, RANK, cols)[:, 0],
            entry_up[:, :, 1],
            entry_up[:, :, 2],
            output_down.transpose(0, 2, 1),
            expand_up,
            shrink_down.transpose(0, 2, 1),
        ],
        axis=2,
    )
    owners = jnp.stack([places.owner(dp, jnp.int32(other)) for other in range(n_t)])
    sent = thin[choices[owners]]
    got = lax.all_to_all(sent, "tensor", 0, 0)
    up_entry = jnp.stack([got[:, :, i * cols : (i + 1) * cols] for i in range(3)], axis=1)
    down_output = got[:, :, 3 * cols : 4 * cols]
    up_expand = got[:, :, 4 * cols : 4 * cols + hid]
    down_shrink = got[:, :, 4 * cols + hid :]
    pick = lambda table: lax.dynamic_index_in_dim(table, mine, 0, keepdims=False)
    down_entry, up_output = pick(entry_down.transpose(0, 2, 1)), pick(output_up)
    down_expand, up_shrink = pick(expand_down.transpose(0, 2, 1)), pick(shrink_up)
    gain_first, gain_second = norm_first.reshape(1, width), norm_second.reshape(1, width)

    q, k, v, normed, inner_t = entry_forward(tok, gain_first, full_entry, down_entry, up_entry)
    shifts = range(1, places.group)
    k_all = jnp.concatenate([k] + [lax.ppermute(k, BOTH, places.mate_pairs(s)) for s in shifts], axis=0)
    v_all = jnp.concatenate([v] + [lax.ppermute(v, BOTH, places.mate_pairs(s)) for s in shifts], axis=0)
    att, lse = attention_forward(q, k_all, v_all)
    mixed, mgrad, agrad, od_g, ou_g, ed_g, eu_g, sd_g, su_g = middle_both_ways(
        alive, tok, att, cot, gain_second, full_output, full_expand, full_shrink,
        down_output, up_output, down_expand, up_expand, down_shrink, up_shrink,
    )
    dq, dk, dv = attention_backward(q, k_all, v_all, att, lse, agrad)

    def returned(grad):
        total = 0.0
        for s in shifts:
            part = lax.ppermute(grad[s * rows : (s + 1) * rows], BOTH, places.mate_pairs(places.group - s))
            total = total + part.astype(F32) if places.group > 2 else part
        return total.astype(BF)

    tgrad, edn_g, eup_g = entry_backward(
        tok, gain_first, mgrad, normed, inner_t, dq, dk[:rows], dv[:rows], returned(dk), returned(dv),
        full_entry, down_entry, up_entry,
    )
    mixed = lax.ppermute(mixed, BOTH, places.swap_pairs())
    token_grad = lax.ppermute(tgrad, BOTH, places.swap_pairs())

    all_owner = jnp.array([places.owner(d, o) for d in range(n_dp) for o in range(n_t)], jnp.int32)
    onehot = (choices[all_owner][:, None] == lax.iota(jnp.int32, adapters)[None]).astype(F32)
    whole = jnp.stack([edn_g, ou_g, ed_g, su_g])
    whole = lax.all_gather(whole.astype(BF), BOTH, axis=0)
    whole = jnp.einsum("sa,sgrd->gard", onehot.astype(BF), whole, preferred_element_type=F32)
    thin_g = jnp.concatenate(
        [
            eup_g[:, 0],
            eup_g[:, 1],
            eup_g[:, 2],
            od_g.reshape(RANK, n_t, cols).transpose(1, 0, 2),
            eu_g.reshape(RANK, n_t, hid).transpose(1, 0, 2),
            sd_g.reshape(RANK, n_t, hid).transpose(1, 0, 2),
        ],
        axis=2,
    )
    thin_g = lax.all_to_all(thin_g.astype(BF), "tensor", 0, 0)
    here = lax.dynamic_slice_in_dim(onehot, dp * n_t, n_t, 0).astype(BF)
    thin_g = jnp.einsum("sa,src->arc", here, thin_g, preferred_element_type=F32)
    thin_g = lax.psum(thin_g.astype(BF), "dp").astype(F32)
    entry_up_grad = jnp.stack([thin_g[:, :, i * cols : (i + 1) * cols] for i in range(3)], axis=2)
    return (
        mixed,
        token_grad,
        whole[0].transpose(0, 2, 1),
        entry_up_grad,
        thin_g[:, :, 3 * cols : 4 * cols].transpose(0, 2, 1),
        whole[1],
        whole[2].transpose(0, 2, 1),
        thin_g[:, :, 4 * cols : 4 * cols + hid],
        thin_g[:, :, 4 * cols + hid :].transpose(0, 2, 1),
        whole[3],
    )


def solution(mesh):
    in_specs = (
        P(BOTH, None), P(BOTH, None), P(), P(),
        P("dp", None, "tensor"), P("dp", "tensor"), P("dp", "tensor"), P("dp", "tensor"),
        P(), P(None, None, None, "tensor"), P(None, "tensor", None), P(),
        P(), P(None, None, "tensor"), P(None, "tensor", None), P(), P("dp"), P("dp"),
    )
    out_specs = (
        P(BOTH, None), P(BOTH, None), P(), P(None, None, None, "tensor"), P(None, "tensor", None), P(),
        P(), P(None, None, "tensor"), P(None, "tensor", None), P(),
    )
    return jax.shard_map(local, mesh=mesh, in_specs=in_specs, out_specs=out_specs, check_vma=False)
```

```python
import functools

import jax
import jax.numpy as jnp
from jax import lax
from jax.experimental import pallas as pl
from jax.experimental.pallas import tpu as pltpu
from jax.sharding import PartitionSpec as P

HEAD_DIM = 64
PAIR = 2 * HEAD_DIM
RANK = 16
LOG2E = 1.4426950408889634
LN2 = 0.6931471805599453
F32, BF = jnp.float32, jnp.bfloat16
VMEM_LIMIT = 60 * 2**20


def dot(a, b, ca, cb):
    return lax.dot_general(a, b, (((ca,), (cb,)), ((), ())), preferred_element_type=F32)


def params(**more):
    return pltpu.CompilerParams(vmem_limit_bytes=VMEM_LIMIT, **more)


def merge_rows(block):
    return block.reshape(block.shape[0] * block.shape[1], block.shape[2])


def norm_parts(values):
    centre = jnp.mean(values, axis=-1, keepdims=True)
    shifted = values - centre
    scale = lax.rsqrt(jnp.mean(shifted * shifted, axis=-1, keepdims=True) + 1e-05)
    return shifted * scale, scale


def norm_back(hat, scale, gain, grad):
    inner = grad * gain
    mean_one = jnp.mean(inner, axis=-1, keepdims=True)
    mean_two = jnp.mean(inner * hat, axis=-1, keepdims=True)
    return scale * (inner - mean_one - hat * mean_two)


MESH = pl.DeviceIdType.MESH
BOTH = ("dp", "tensor")
ANY = pl.BlockSpec(memory_space=pl.ANY)
IN_VMEM = pl.BlockSpec(memory_space=pltpu.VMEM)
IN_SMEM = pl.BlockSpec(memory_space=pltpu.SMEM)
DMA = pltpu.SemaphoreType.DMA


class Place:
    def __init__(self, n_dp, n_t, cap):
        self.n_dp, self.n_t, self.cap = n_dp, n_t, cap
        self.dp, self.t = lax.axis_index("dp"), lax.axis_index("tensor")
        self.core, self.q = self.dp % 2, self.dp // 2
        self.n_q, self.n_hi = n_dp // 2, n_dp // 4
        self.lo, self.hi = self.q % 2, self.q // 2
        self.group = n_t // cap
        self.half = self.group // 2
        self.slot, block = self.t // self.group, self.t % self.group
        self.high, self.low = block // self.half, block % self.half
        self.stays = self.core == self.high
        self.sibling = (self.dp + 1 - 2 * self.core, self.t)
        self.partner = (self.dp - self.core + self.high, self.t - block + self.core * self.half + self.low)

    def along(self, d):
        return (self.t + d) % self.n_t

    def column(self, d, cols):
        return pl.ds(pl.multiple_of(((self.t + self.n_t - d) % self.n_t) * cols, cols), cols)

    def lo_q(self):
        return self.q + 1 - 2 * self.lo

    def hi_q(self, m, lo=None):
        return ((self.hi + m) % self.n_hi) * 2 + (self.lo if lo is None else lo)

    def device(self, q, core=None, t=None):
        return (q * 2 + (self.core if core is None else core), self.t if t is None else t)

    def mate(self, shift):
        block = (self.core * self.half + self.low + shift) % self.group
        return (self.dp - self.core + block // self.half, self.t - self.low + block % self.half)

    def gather_peers(self):
        return (
            [(self.dp, self.along(d)) for d in range(1, self.n_t)]
            + [self.sibling, self.device(self.lo_q())]
            + [self.device(self.hi_q(m)) for m in range(1, self.n_hi)]
        )

    def other_core_peers(self):
        return [(self.sibling[0], self.along(d)) for d in range(1, self.n_t)]


def greet(peers):
    barrier = pltpu.get_barrier_semaphore()
    for peer in peers:
        pl.semaphore_signal(barrier, inc=1, device_id=peer, device_id_type=MESH)
    pl.semaphore_wait(barrier, len(peers))


def remote(src, dst, send, recv, device):
    return pltpu.make_async_remote_copy(
        src_ref=src, dst_ref=dst, send_sem=send, recv_sem=recv, device_id=device, device_id_type=MESH
    )


class Gather:
    @staticmethod
    def keys(n_hi, ds):
        found = []
        for d in ds:
            found += [("z", d)] if d else []
            found += [("x", d), ("s", d)]
            for m in range(1, n_hi):
                found += [("y", m, d), ("dy", m, d), ("dx", m, d)]
        return found

    @staticmethod
    def scratch(n_dp, ds):
        count = len(Gather.keys(n_dp // 4, ds))
        return [DMA((count,)), DMA((count,)), DMA((1,))]

    def __init__(self, place, source, full, ds, sems, spread=None, by_rows=True):
        self.place, self.source, self.full, self.ds = place, source, full, list(ds)
        self.send, self.recv, self.own = sems
        self.index = {k: i for i, k in enumerate(Gather.keys(place.n_hi, self.ds))}
        self.spread, self.by_rows = spread, by_rows
        self.ms = range(1, place.n_hi)

    def block(self, d, q, half=None):
        ref = self.full.at[self.ds.index(d), q, self.place.core]
        if half is None:
            return ref
        rows, cols = self.full.shape[-2:]
        if self.by_rows:
            return ref.at[pl.ds(half * (rows // 2), rows // 2)]
        first = cols // 2 // 128 * 128
        return ref.at[:, pl.ds(half * first, cols - first if half else first)]

    def copy(self, key):
        p, kind, d = self.place, key[0], key[-1]
        i = self.index[key]
        if kind == "z":
            src = self.source if self.spread is None else self.spread(d)
            dst, device = self.block(d, p.q), (p.dp, p.along(d))
        elif kind == "s":
            src = dst = self.full.at[self.ds.index(d), :, p.core]
            device = p.sibling
        elif kind in "xy":
            src = self.source if d == 0 else self.block(d, p.q)
            dst = self.block(d, p.q)
            device = p.device(p.lo_q() if kind == "x" else p.hi_q(key[1]))
        elif kind == "dy":
            src = dst = self.block(d, p.lo_q(), 0)
            device = p.device(p.hi_q(key[1]))
        else:
            src = dst = self.block(d, p.hi_q(p.n_hi - key[1]), 1)
            device = p.device(p.lo_q())
        return remote(src, dst, self.send.at[i], self.recv.at[i], device)

    def own_copy(self):
        return pltpu.make_async_copy(self.source, self.block(0, self.place.q), self.own.at[0])

    def start(self):
        for d in self.ds:
            if d:
                self.copy(("z", d)).start()
        if 0 in self.ds:
            self.relay(0)
            self.own_copy().start()

    def relay(self, d):
        if d:
            self.copy(("z", d)).wait_recv()
        self.copy(("x", d)).start()
        for m in self.ms:
            self.copy(("y", m, d)).start()

    def diag(self, d):
        self.copy(("x", d)).wait_recv()
        for m in self.ms:
            self.copy(("dy", m, d)).start()
        for m in self.ms:
            self.copy(("y", m, d)).wait_recv()
            self.copy(("dx", m, d)).start()

    def share(self, d):
        if d == 0:
            self.own_copy().wait()
        for m in self.ms:
            self.copy(("dy", m, d)).wait_recv()
            self.copy(("dx", m, d)).wait_recv()
        self.copy(("s", d)).start()

    def done(self, d):
        self.copy(("s", d)).wait_recv()

    def finish(self):
        for key in self.index:
            self.copy(key).wait_send()


def move(place, source, target, sems, kind, rows=None):
    if rows is not None:
        source, target = source.at[rows], target.at[rows]

    @pl.when(place.stays)
    def _():
        here = pltpu.make_async_copy(source, target, sems[2])
        here.start() if kind == "start" else here.wait()

    @pl.when(jnp.logical_not(place.stays))
    def _():
        there = remote(source, target, sems[0], sems[1], place.partner)
        there.start() if kind == "start" else there.wait()


def first_kernel(
    n_dp, n_t, cap,
    choice_ref, count_ref, tokens_ref, w_ref, gain_ref, ed_tab, ou_tab, xd_tab, su_tab, eu_tab, od_tab, xu_tab, sd_tab,
    q_ref, k_ref, v_ref, normed_ref, inner_t_ref, thin_ref, rep_ref, tok_out, k_far, v_far, w_full,
    tok, thin, thin_send, rep, stage, inner,
    g_send, g_recv, g_own, tok_sems, thin_sends, thin_recvs, rep_sems, stage_sems, kv_sends, kv_recvs, out_sem,
):
    p = Place(n_dp, n_t, cap)
    cols, hid = od_tab.shape[-1], xu_tab.shape[-1]
    greet(p.gather_peers() + p.other_core_peers())
    gather = Gather(p, w_ref, w_full, range(n_t), (g_send, g_recv, g_own))
    gather.start()
    swap_sems = [tok_sems.at[i] for i in range(3)]
    move(p, tokens_ref, tok, swap_sems, "start")

    for s in range(cap):
        a = choice_ref[s]
        for i in range(3):
            thin_send[s, :, i * cols : (i + 1) * cols] = eu_tab[a, i]
        thin_send[s, :, 3 * cols : 4 * cols] = od_tab[a]
        thin_send[s, :, 4 * cols : 4 * cols + hid] = xu_tab[a]
        thin_send[s, :, 4 * cols + hid :] = sd_tab[a]
    for s in range(cap):
        for low in range(p.half):
            to = s * p.group + p.core * p.half + low
            d = (to + n_t - p.t) % n_t
            for core in range(2):
                i = (s * p.half + low) * 2 + core
                mine = jnp.logical_and(core == p.core, to == p.t)

                @pl.when(jnp.logical_not(mine))
                def _():
                    remote(
                        thin_send.at[s], thin.at[d], thin_sends.at[i], thin_recvs.at[d], (p.dp - p.core + core, to)
                    ).start()

    @pl.when(p.stays)
    def _():
        a = choice_ref[p.slot]
        for i, table in enumerate((ed_tab, ou_tab, xd_tab, su_tab)):
            rep[i * RANK : (i + 1) * RANK] = table[a]
        row = lax.broadcasted_iota(jnp.int32, (RANK, rep.shape[1]), 0)
        alive = jnp.where(p.slot < count_ref[0], 1.0, 0.0)
        rep[4 * RANK :] = jnp.where(row < RANK // 2, alive, a.astype(F32)).astype(BF)
        remote(rep, rep, rep_sems.at[0], rep_sems.at[1], p.sibling).start()
        thin[0] = thin_send[p.slot]

    gather.diag(0)
    gather.relay(1)
    gather.share(0)
    for d in range(1, n_t - 1):
        gather.diag(d)
        gather.relay(d + 1)
        gather.share(d)

    @pl.when(jnp.logical_not(p.stays))
    def _():
        remote(rep, rep, rep_sems.at[0], rep_sems.at[1], p.sibling).wait_recv()
        remote(thin_send.at[0], thin.at[0], thin_sends.at[0], thin_recvs.at[0], p.sibling).wait_recv()

    for d in range(1, n_t):
        remote(thin_send.at[0], thin.at[d], thin_sends.at[0], thin_recvs.at[d], p.sibling).wait_recv()
    rep_ref[...] = rep[...]
    thin_ref[...] = thin[...]

    move(p, tokens_ref, tok, swap_sems, "wait")
    keep = pltpu.make_async_copy(tok, tok_out, out_sem)
    keep.start()
    hat, _ = norm_parts(tok[...].astype(F32))
    normed = (hat * gain_ref[...]).astype(BF)
    normed_ref[...] = normed
    down = rep[:RANK]
    inner[...] = dot(normed, down, 1, 1).astype(BF)
    inner_t_ref[...] = dot(down, normed, 1, 1).astype(BF)

    def load(d):
        return pltpu.make_async_copy(w_full.at[d], stage.at[d % 2], stage_sems.at[d % 2])

    depth = stage.shape[-2] // 3
    gather.done(0)
    load(0).start()
    sent = []
    for d in range(n_t):
        if d == n_t - 2:
            gather.diag(n_t - 1)
        load(d).wait()
        if d + 1 < n_t:
            if d + 1 == n_t - 1:
                gather.share(n_t - 1)
            gather.done(d + 1)
            load(d + 1).start()
        at = p.column(d, cols)
        normed = normed_ref[...]
        for which, out in ((1, k_ref), (2, v_ref), (0, q_ref)):
            weights = stage[d % 2, :, :, which * depth : (which + 1) * depth].reshape(n_dp * depth, cols)
            part = dot(normed, weights, 1, 0)
            part = part + dot(inner[...], thin[d, :, which * cols : (which + 1) * cols], 1, 0)
            if which == 0:
                part = part * (HEAD_DIM**-0.5 * LOG2E)
            out[:, at] = part.astype(BF)
            if which:
                far = (k_far, v_far)[which - 1]
                for m in range(1, p.group):
                    i = (d * 2 + which - 1) * (p.group - 1) + m - 1
                    copy = remote(
                        out.at[:, at], far.at[m - 1, :, at], kv_sends.at[i], kv_recvs.at[i], p.mate(m)
                    )
                    copy.start()
                    sent.append((i, far, m, d))

    for i, far, m, d in sent:
        at = p.column(d, cols)
        remote(k_ref.at[:, at], far.at[m - 1, :, at], kv_sends.at[i], kv_recvs.at[i], p.mate(m)).wait()
    gather.finish()

    @pl.when(p.stays)
    def _():
        remote(rep, rep, rep_sems.at[0], rep_sems.at[1], p.sibling).wait_send()

    for s in range(cap):
        for low in range(p.half):
            to = s * p.group + p.core * p.half + low
            for core in range(2):
                i = (s * p.half + low) * 2 + core
                mine = jnp.logical_and(core == p.core, to == p.t)

                @pl.when(jnp.logical_not(mine))
                def _():
                    remote(
                        thin_send.at[s], thin.at[0], thin_sends.at[i], thin_recvs.at[0], p.sibling
                    ).wait_send()

    keep.wait()


def first_part(cap, choice, count, tokens, w, gain, rep_tables, thin_tables):
    n_dp, n_t = lax.axis_size("dp"), lax.axis_size("tensor")
    rows, width = tokens.shape
    depth3, cols = w.shape
    group = n_t // cap
    thin_width = 4 * cols + 2 * thin_tables[2].shape[-1]
    shape = jax.ShapeDtypeStruct
    n_kv = n_t * 2 * (group - 1)
    return pl.pallas_call(
        functools.partial(first_kernel, n_dp, n_t, cap),
        in_specs=[IN_SMEM, IN_SMEM, ANY, ANY] + [IN_VMEM] * 9,
        out_specs=[IN_VMEM] * 7 + [ANY] * 4,
        out_shape=[shape((rows, width), BF)] * 4
        + [
            shape((RANK, rows), BF),
            shape((n_t, RANK, thin_width), BF),
            shape((5 * RANK, width), BF),
            shape((rows, width), BF),
            shape((group - 1, rows, width), BF),
            shape((group - 1, rows, width), BF),
            shape((n_t, n_dp // 2, 2, depth3, cols), BF),
        ],
        scratch_shapes=[
            pltpu.VMEM((rows, width), BF),
            pltpu.VMEM((n_t, RANK, thin_width), BF),
            pltpu.VMEM((cap, RANK, thin_width), BF),
            pltpu.VMEM((5 * RANK, width), BF),
            pltpu.VMEM((2, n_dp // 2, 2, depth3, cols), BF),
            pltpu.VMEM((rows, RANK), BF),
            *Gather.scratch(n_dp, range(n_t)),
            DMA((3,)), DMA((n_t,)), DMA((n_t,)), DMA((2,)), DMA((2,)), DMA((n_kv,)), DMA((n_kv,)), DMA(()),
        ],
        compiler_params=params(collective_id=0, has_side_effects=True),
        name="first_part",
    )(choice, count, tokens, w, gain, *rep_tables, *thin_tables)


def head_masks(shape):
    lane = lax.broadcasted_iota(jnp.int32, shape, 1)
    return lane < HEAD_DIM, lane >= HEAD_DIM


def ones_lanes(rows, count):
    lane = lax.broadcasted_iota(jnp.int32, (rows, PAIR), 1)
    return jnp.where(lane < count, 1.0, 0.0).astype(BF)


def with_far(near_ref, far_ref):
    return jnp.concatenate([near_ref[...]] + [far_ref[m] for m in range(far_ref.shape[0])], axis=0)


def attend(q_ref, k_ref, k_far, v_ref, v_far, o_ref, lse_ref):
    rows = q_ref.shape[0]
    keys = with_far(k_ref, k_far)
    length = keys.shape[0]
    values = jnp.concatenate([with_far(v_ref, v_far), ones_lanes(length, 1)], axis=1)
    queries = q_ref[...]
    zero = jnp.zeros_like(queries)
    outs, sums = [], []
    for mask in head_masks(queries.shape):
        scores = dot(jnp.where(mask, queries, zero), keys, 1, 1)
        top = jnp.max(scores, axis=1, keepdims=True)
        probs = jnp.exp2(scores - top).astype(BF)
        mixed = dot(probs, values, 1, 0)
        total = mixed[:, PAIR : PAIR + 1]
        outs.append(mixed[:, :PAIR] / total)
        sums.append(top + jnp.log2(total))
    first, _ = head_masks((rows, PAIR))
    o_ref[...] = jnp.where(first, outs[0], outs[1]).astype(BF)
    lse_ref[...] = jnp.where(first, sums[0], sums[1])


def attend_kernel(
    n_dp, n_t, cap,
    q_ref, k_ref, k_far, v_ref, v_far, wo_ref, we_ref, ws_ref, cot_ref,
    o_ref, lse_ref, wo_full, we_full, ws_full, cot_out, *sems,
):
    p = Place(n_dp, n_t, cap)
    step, steps = pl.program_id(0), pl.num_programs(0)
    early = list(range(n_t // 2))
    out_g = Gather(p, wo_ref, wo_full, range(n_t), sems[0:3])
    exp_g = Gather(p, we_ref, we_full, early, sems[3:6])
    shr_g = Gather(p, ws_ref, ws_full, early, sems[6:9])
    swap_sems = [sems[9].at[i] for i in range(3)]

    def starts():
        greet(p.gather_peers() + p.other_core_peers())
        for g in (exp_g, shr_g, out_g):
            g.start()
        move(p, cot_ref, cot_out, swap_sems, "start")

    events = [starts]
    both = (exp_g, shr_g)
    for d in range(n_t):
        if d in early:
            events.append(lambda d=d: [g.diag(d) for g in both])
        events.append(lambda d=d: out_g.diag(d))
        if d + 1 in early:
            events.append(lambda d=d: [g.relay(d + 1) for g in both])
        if d + 1 < n_t:
            events.append(lambda d=d: out_g.relay(d + 1))
        if d in early:
            events.append(lambda d=d: [g.share(d) for g in both])
        events.append(lambda d=d: out_g.share(d))
    places_left = 8
    for i in range(places_left):
        batch = events[:1] if i == 0 else events[1 + (len(events) - 1) * (i - 1) // 7 : 1 + (len(events) - 1) * i // 7]

        @pl.when(step == i)
        def _():
            for event in batch:
                event()

    attend(q_ref, k_ref, k_far, v_ref, v_far, o_ref, lse_ref)

    @pl.when(step == steps - 1)
    def _():
        for g in (exp_g, shr_g, out_g):
            for d in g.ds:
                g.done(d)
            g.finish()
        move(p, cot_ref, cot_out, swap_sems, "wait")


def attention_forward(cap, q, k, k_far, v, v_far, wo, we, ws, cot):
    n_dp, n_t = lax.axis_size("dp"), lax.axis_size("tensor")
    rows, width = q.shape
    pair = pl.BlockSpec((rows, PAIR), lambda h: (0, h))
    far = pl.BlockSpec((k_far.shape[0], rows, PAIR), lambda h: (0, 0, h))
    shape = jax.ShapeDtypeStruct
    early = n_t // 2
    full = lambda n, w: shape((n, n_dp // 2, 2, *w.shape), BF)
    return pl.pallas_call(
        functools.partial(attend_kernel, n_dp, n_t, cap),
        grid=(width // PAIR,),
        in_specs=[pair, pair, far, pair, far] + [ANY] * 4,
        out_specs=[pair, pair] + [ANY] * 4,
        out_shape=[
            shape((rows, width), BF), shape((rows, width), F32),
            full(n_t, wo), full(early, we), full(early, ws), shape((rows, width), BF),
        ],
        scratch_shapes=Gather.scratch(n_dp, range(n_t)) + Gather.scratch(n_dp, range(early)) * 2 + [DMA((3,))],
        compiler_params=params(collective_id=1, has_side_effects=True),
        name="attention_forward",
    )(q, k, k_far, v, v_far, wo, we, ws, cot)


def split_lanes(column):
    column = -column
    high = column.astype(BF)
    rest = column - high.astype(F32)
    mid = rest.astype(BF)
    low = (rest - mid.astype(F32)).astype(BF)
    lane = lax.broadcasted_iota(jnp.int32, (column.shape[0], PAIR), 1)
    zero = jnp.zeros((column.shape[0], PAIR), BF)
    return jnp.where(lane == 0, high, jnp.where(lane == 1, mid, jnp.where(lane == 2, low, zero)))


def attend_back_kernel(
    n_dp, n_t, cap,
    q_ref, k_ref, k_far, v_ref, v_far, o_ref, lse_ref, do_ref, mixed_ref, grads_ref,
    dq_ref, dk_ref, dv_ref, dk_far, dv_far, mixed_out, grads_full,
    dk_send, dv_send, sends, recvs, g_send, g_recv, g_own, swap,
):
    p = Place(n_dp, n_t, cap)
    step, steps = pl.program_id(0), pl.num_programs(0)
    rows = q_ref.shape[0]
    gather = Gather(
        p, grads_ref.at[0], grads_full, range(n_t), (g_send, g_recv, g_own),
        spread=lambda d: grads_ref.at[n_t - d], by_rows=False,
    )
    swap_sems = [swap.at[i] for i in range(3)]

    def starts():
        greet(p.gather_peers() + p.other_core_peers())
        gather.start()
        move(p, mixed_ref, mixed_out, swap_sems, "start")

    events = [starts]
    for d in range(n_t):
        events.append(lambda d=d: gather.diag(d))
        if d + 1 < n_t:
            events.append(lambda d=d: gather.relay(d + 1))
        events.append(lambda d=d: gather.share(d))
    for i in range(8):
        batch = events[:1] if i == 0 else events[1 + (len(events) - 1) * (i - 1) // 7 : 1 + (len(events) - 1) * i // 7]

        @pl.when(step == i)
        def _():
            for event in batch:
                event()

    keys = with_far(k_ref, k_far)
    length = keys.shape[0]
    ones = ones_lanes(length, 3)
    keys_more = jnp.concatenate([keys, ones], axis=1)
    values_more = jnp.concatenate([with_far(v_ref, v_far), ones], axis=1)
    queries, grad = q_ref[...], do_ref[...]
    zero = jnp.zeros_like(queries)
    product = grad.astype(F32) * o_ref[...].astype(F32)
    d_queries, d_keys, d_values = [], 0.0, 0.0
    for head, mask in enumerate(head_masks(queries.shape)):
        query = jnp.where(mask, queries, zero)
        grad_head = jnp.where(mask, grad, zero)
        lse = lse_ref[:, head * HEAD_DIM : head * HEAD_DIM + 1]
        delta = jnp.sum(jnp.where(mask, product, 0.0), axis=1, keepdims=True)
        probs = jnp.exp2(dot(jnp.concatenate([query, split_lanes(lse)], axis=1), keys_more, 1, 1))
        slope = dot(jnp.concatenate([grad_head, split_lanes(delta)], axis=1), values_more, 1, 1)
        score_grad = (probs * slope).astype(BF)
        d_queries.append(dot(score_grad, keys, 1, 0))
        d_values = d_values + dot(grad_head, probs.astype(BF), 0, 0)
        d_keys = d_keys + dot(query, score_grad, 0, 0)
    first, _ = head_masks((rows, PAIR))
    dq_ref[...] = (jnp.where(first, d_queries[0], d_queries[1]) * HEAD_DIM**-0.5).astype(BF)
    d_keys = (d_keys * LN2).T.astype(BF)
    d_values = d_values.T.astype(BF)
    dk_ref[...] = d_keys[:rows]
    dv_ref[...] = d_values[:rows]

    def far_copy(i, m, h):
        at = pl.ds(pl.multiple_of(h * PAIR, PAIR), PAIR)
        source, target = ((dk_send, dk_far), (dv_send, dv_far))[i]
        return remote(
            source.at[m - 1, :, at], target.at[m - 1, :, at],
            sends.at[i, m - 1, h], recvs.at[i, m - 1, h], p.mate(p.group - m),
        )

    at = pl.ds(pl.multiple_of(step * PAIR, PAIR), PAIR)
    for m in range(1, p.group):
        dk_send[m - 1, :, at] = d_keys[m * rows : (m + 1) * rows]
        dv_send[m - 1, :, at] = d_values[m * rows : (m + 1) * rows]
        far_copy(0, m, step).start()
        far_copy(1, m, step).start()

    @pl.when(step == steps - 1)
    def _():
        for d in range(n_t):
            gather.done(d)
        gather.finish()
        move(p, mixed_ref, mixed_out, swap_sems, "wait")

        @pl.loop(0, steps)
        def _(h):
            for m in range(1, p.group):
                far_copy(0, m, h).wait()
                far_copy(1, m, h).wait()


def attention_backward(cap, q, k, k_far, v, v_far, o, lse, do, mixed, grads):
    n_dp, n_t = lax.axis_size("dp"), lax.axis_size("tensor")
    rows, width = q.shape
    others = k_far.shape[0]
    pair = pl.BlockSpec((rows, PAIR), lambda h: (0, h))
    far = pl.BlockSpec((others, rows, PAIR), lambda h: (0, 0, h))
    shape = jax.ShapeDtypeStruct
    count = (2, others, width // PAIR)
    return pl.pallas_call(
        functools.partial(attend_back_kernel, n_dp, n_t, cap),
        grid=(width // PAIR,),
        in_specs=[pair, pair, far, pair, far, pair, pair, pair, ANY, ANY],
        out_specs=[pair] * 3 + [ANY] * 4,
        out_shape=[shape((rows, width), BF)] * 3
        + [shape((others, rows, width), BF)] * 2
        + [shape((rows, width), BF), shape((n_t, n_dp // 2, 2, *grads.shape[1:]), BF)],
        scratch_shapes=[
            pltpu.VMEM((others, rows, width), BF), pltpu.VMEM((others, rows, width), BF),
            DMA(count), DMA(count), *Gather.scratch(n_dp, range(n_t)), DMA((3,)),
        ],
        compiler_params=params(collective_id=3, has_side_effects=True),
        name="attention_backward",
    )(q, k, k_far, v, v_far, o, lse, do, mixed, grads)


def gelu_parts(hidden):
    share = 0.5 * (1.0 + lax.erf(hidden * 0.7071067811865476))
    density = jnp.exp(-0.5 * hidden * hidden) * 0.3989422804014327
    return hidden * share, share + hidden * density


def middle_kernel(
    n_dp, n_t, cap, sub,
    x_ref, att_ref, cot_ref, gain_ref, rep_ref, thin_ref, wo_ref, we_near, ws_near, we_ref, ws_ref,
    mixed_ref, mgrad_ref, agrad_ref, grads_ref, we_full, ws_full,
    middle_ref, second_ref, dy_ref, acc2_ref, acc3_ref, einner_ref, einner_t_ref, sback_ref, sback_t_ref,
    sinner_ref, eback_ref, oinner_ref, we_buf, ws_buf, buf_sems, *sems,
):
    p = Place(n_dp, n_t, cap)
    step, steps = pl.program_id(0), pl.num_programs(0)
    cols = wo_ref.shape[-1]
    width = x_ref.shape[1]
    hid = we_ref.shape[-1]
    size = hid // sub
    near = n_t // 2
    late = list(range(near, n_t))
    exp_g = Gather(p, we_ref, we_full, late, sems[0:3])
    shr_g = Gather(p, ws_ref, ws_full, late, sems[3:6])
    both = (exp_g, shr_g)
    down_e, up_o, up_s = rep_ref[2 * RANK : 3 * RANK], rep_ref[RANK : 2 * RANK], rep_ref[3 * RANK : 4 * RANK]
    alive = rep_ref[4 * RANK : 4 * RANK + 1, 0:1].astype(F32)
    at_od, at_eu = 3 * width, 3 * width + cols
    at_sd, at_id = at_eu + hid, at_eu + 2 * hid

    def load(i):
        d, part = i // sub, i % sub
        at = pl.ds(part * size, size)
        pair = (we_near, ws_near) if d < near else (we_full, ws_full)
        index = d if d < near else d - near
        return [
            pltpu.make_async_copy(src.at[index, :, :, :, at], buf.at[i % 2], buf_sems.at[i % 2, j])
            for j, (src, buf) in enumerate(zip(pair, (we_buf, ws_buf)))
        ]

    @pl.when(step == 0)
    def _():
        greet(p.gather_peers())
        for g in both:
            g.start()
        for copy in load(0):
            copy.start()
        branch, inner = 0.0, 0.0
        for d in range(n_t):
            att = att_ref[:, p.column(d, cols)]
            branch = branch + dot(att, wo_ref[d].reshape(width, cols), 1, 1)
            inner = inner + dot(att, thin_ref[d, :, 3 * cols : 4 * cols], 1, 1)
        inner = inner.astype(BF)
        oinner_ref[...] = inner
        middle = x_ref[...].astype(F32) + (branch + dot(inner, up_o, 1, 0))
        middle_ref[...] = middle
        hat, _ = norm_parts(middle)
        second = (hat * gain_ref[...]).astype(BF)
        second_ref[...] = second
        dy = (cot_ref[...].astype(F32) * alive).astype(BF)
        dy_ref[...] = dy
        einner_ref[...] = dot(second, down_e, 1, 1).astype(BF)
        einner_t_ref[...] = dot(down_e, second, 1, 1).astype(BF)
        sback_ref[...] = dot(dy, up_s, 1, 1).astype(BF)
        sback_t_ref[...] = dot(up_s, dy, 1, 1).astype(BF)
        acc2_ref[...] = jnp.zeros_like(acc2_ref)
        acc3_ref[...] = jnp.zeros_like(acc3_ref)
        sinner_ref[...] = jnp.zeros_like(sinner_ref)
        eback_ref[...] = jnp.zeros_like(eback_ref)

    for i in range(n_t * sub):

        @pl.when(step == i)
        def _():
            for d in late:
                first = (d - 2) * sub if near == 2 else 0
                if i == max(1, first + sub - 1):
                    [g.relay(d) for g in both]
                if i == max(1, first + sub):
                    [g.diag(d) for g in both]
                if i == max(1, first + sub + 1):
                    [g.share(d) for g in both]
            for copy in load(i):
                copy.wait()
            if i + 1 < n_t * sub and (i + 1) // sub < near:
                for copy in load(i + 1):
                    copy.start()

    buf = step % 2
    d, part = step // sub, step % sub
    we, ws = we_buf[buf].reshape(width, size), ws_buf[buf].reshape(width, size)
    at = pl.multiple_of(part * size, size)
    e_up = thin_ref[d, :, pl.ds(4 * cols + at, size)]
    s_down = thin_ref[d, :, pl.ds(4 * cols + hid + at, size)]
    hidden = dot(second_ref[...], we, 1, 0) + dot(einner_ref[...], e_up, 1, 0)
    value, slope = gelu_parts(hidden)
    act = value.astype(BF)
    acc2_ref[...] += dot(act, ws, 1, 1)
    sinner_ref[...] += dot(act, s_down, 1, 1)
    act_grad = dot(dy_ref[...], ws, 1, 0) + dot(sback_ref[...], s_down, 1, 0)
    hid_grad = (act_grad * slope).astype(BF)
    acc3_ref[...] += dot(hid_grad, we, 1, 1)
    eback_ref[...] += dot(hid_grad, e_up, 1, 1)
    grads_ref[d, :, pl.ds(at_eu + at, size)] = dot(einner_t_ref[...], hid_grad, 1, 0).astype(BF)
    grads_ref[d, :, pl.ds(at_sd + at, size)] = dot(sback_t_ref[...], act, 1, 0).astype(BF)

    for i in range(n_t * sub - 1):
        if (i + 1) // sub >= near:

            @pl.when(step == i)
            def _():
                if (i + 1) % sub == 0:
                    for g in both:
                        g.done((i + 1) // sub)
                for copy in load(i + 1):
                    copy.start()

    @pl.when(step == steps - 1)
    def _():
        s_inner, e_back = sinner_ref[...].astype(BF), eback_ref[...].astype(BF)
        middle = middle_ref[...]
        mixed_ref[...] = (alive * (middle + (acc2_ref[...] + dot(s_inner, up_s, 1, 0)))).astype(BF)
        shrink_up = dot(s_inner, dy_ref[...], 0, 0).astype(BF)
        expand_down = dot(e_back, second_ref[...], 0, 0).astype(BF)
        second_grad = acc3_ref[...] + dot(e_back, down_e, 1, 0)
        hat, scale = norm_parts(middle)
        mgrad = cot_ref[...].astype(F32) * alive + norm_back(hat, scale, gain_ref[...], second_grad)
        mgrad_ref[...] = mgrad
        low = mgrad.astype(BF)
        o_back = dot(low, up_o, 1, 1).astype(BF)
        output_up = dot(oinner_ref[...], low, 0, 0).astype(BF)
        for d in range(n_t):
            at = p.column(d, cols)
            agrad_ref[:, at] = (
                dot(low, wo_ref[d].reshape(width, cols), 1, 0)
                + dot(o_back, thin_ref[d, :, 3 * cols : 4 * cols], 1, 0)
            ).astype(BF)
            grads_ref[d, :, :width] = expand_down
            grads_ref[d, :, width : 2 * width] = shrink_up
            grads_ref[d, :, 2 * width : 3 * width] = output_up
            grads_ref[d, :, at_od : at_od + cols] = dot(o_back, att_ref[:, at], 0, 0).astype(BF)
            grads_ref[d, :, at_id:] = rep_ref[4 * RANK :, : grads_ref.shape[2] - at_id]
        for g in both:
            g.finish()


ID_LANES = 128


def middle_both_ways(cap, x, att, cot, gain, rep, thin, wo_full, we_near, ws_near, we, ws):
    n_dp, n_t = lax.axis_size("dp"), lax.axis_size("tensor")
    rows, width = x.shape
    depth, hid = we.shape
    cols = wo_full.shape[-1]
    sub = max(1, hid // 512)
    size = hid // sub
    late = range(n_t // 2, n_t)
    grad_width = 3 * width + cols + 2 * hid + ID_LANES
    whole = lambda a: pl.BlockSpec(a.shape, lambda i: (0,) * len(a.shape))
    shape = jax.ShapeDtypeStruct
    full = shape((len(late), n_dp // 2, 2, depth, hid), BF)
    outs = [
        shape((rows, width), BF), shape((rows, width), F32), shape((rows, width), BF),
        shape((n_t, RANK, grad_width), BF),
    ]
    vmem = pltpu.VMEM
    return pl.pallas_call(
        functools.partial(middle_kernel, n_dp, n_t, cap, sub),
        grid=(n_t * sub,),
        in_specs=[whole(a) for a in (x, att, cot, gain, rep, thin, wo_full)] + [ANY] * 4,
        out_specs=[whole(a) for a in outs] + [ANY] * 2,
        out_shape=outs + [full, full],
        scratch_shapes=[
            vmem((rows, width), F32), vmem((rows, width), BF), vmem((rows, width), BF),
            vmem((rows, width), F32), vmem((rows, width), F32),
            vmem((rows, RANK), BF), vmem((RANK, rows), BF), vmem((rows, RANK), BF), vmem((RANK, rows), BF),
            vmem((rows, RANK), F32), vmem((rows, RANK), F32), vmem((rows, RANK), BF),
            vmem((2, n_dp // 2, 2, depth, size), BF), vmem((2, n_dp // 2, 2, depth, size), BF), DMA((2, 2)),
            *Gather.scratch(n_dp, late), *Gather.scratch(n_dp, late),
        ],
        compiler_params=params(collective_id=2, has_side_effects=True),
        name="middle_both_ways",
    )(x, att, cot, gain, rep, thin, wo_full, we_near, ws_near, we, ws)


def last_kernel(
    n_dp, n_t, cap, tiles,
    gain_ref, rep_ref, thin_ref, inner_t_ref, dq_ref, dk_ref, dv_ref, dk_far, dv_far, w_ref, mgrad_ref, tok_ref, normed_ref,
    tgrad_out, grads_full,
    weights, grad, far, mgrad, tok, normed, back_low, tgrad, grads, load_sems, g_send, g_recv, g_own, swaps,
):
    p = Place(n_dp, n_t, cap)
    cols = w_ref.shape[-1]
    depth = w_ref.shape[-2] // 3
    width = tok_ref.shape[1]
    loads = [
        pltpu.make_async_copy(src, dst, load_sems.at[i])
        for i, (src, dst) in enumerate(
            (
                (dq_ref, grad.at[0]), (dk_ref, grad.at[1]), (dk_far, far.at[0]), (dv_ref, grad.at[2]),
                (dv_far, far.at[1]), (normed_ref, normed), (w_ref, weights), (tok_ref, tok), (mgrad_ref, mgrad),
            )
        )
    ]
    for copy in loads:
        copy.start()
    greet(p.gather_peers() + p.other_core_peers())
    for copy in loads[:5]:
        copy.wait()
    for i in range(2):
        total = grad[1 + i].astype(F32)
        for m in range(far.shape[1]):
            total = total + far[i, m].astype(F32)
        grad[1 + i] = total.astype(BF)
    back = 0.0
    for d in range(n_t):
        at = p.column(d, cols)
        for which in range(3):
            part = grad[which, :, at]
            back = back + dot(part, thin_ref[d, :, which * cols : (which + 1) * cols], 1, 1)
            grads[d, :, which * cols : (which + 1) * cols] = dot(inner_t_ref[...], part, 1, 0).astype(BF)
    back = back.astype(BF)
    back_low[...] = back
    loads[5].wait()
    down_grad = dot(back, normed[...], 0, 0).astype(BF)
    for d in range(n_t):
        grads[d, :, 3 * cols :] = down_grad
    gather = Gather(
        p, grads.at[0], grads_full, range(n_t), (g_send, g_recv, g_own),
        spread=lambda d: grads.at[n_t - d], by_rows=False,
    )
    gather.start()
    for copy in loads[6:]:
        copy.wait()
    events = []
    for d in range(n_t):
        events.append(lambda d=d: gather.diag(d))
        if d + 1 < n_t:
            events.append(lambda d=d: gather.relay(d + 1))
        events.append(lambda d=d: gather.share(d))
    for n, (start, count) in enumerate(tiles):
        rows = pl.ds(start, count)
        total = dot(back_low[rows], rep_ref[:RANK], 1, 0)
        for d in range(n_t):
            at = p.column(d, cols)
            for which in range(3):
                piece = weights[d, :, :, which * depth : (which + 1) * depth].reshape(width, cols)
                total = total + dot(grad[which, rows, at], piece, 1, 1)
        hat, scale = norm_parts(tok[rows].astype(F32))
        tgrad[rows] = (mgrad[rows] + norm_back(hat, scale, gain_ref[...], total)).astype(BF)
        move(p, tgrad, tgrad_out, [swaps.at[n, i] for i in range(3)], "start", rows)
        for event in events[len(events) * n // len(tiles) : len(events) * (n + 1) // len(tiles)]:
            event()
    for d in range(n_t):
        gather.done(d)
    gather.finish()
    for n, (start, count) in enumerate(tiles):
        move(p, tgrad, tgrad_out, [swaps.at[n, i] for i in range(3)], "wait", pl.ds(start, count))


def last_part(cap, gain, rep, thin, inner_t, dq, dk, dv, dk_far, dv_far, w_full, mgrad, tok, normed):
    n_dp, n_t = lax.axis_size("dp"), lax.axis_size("tensor")
    rows, width = tok.shape
    cols = w_full.shape[-1]
    others = dk_far.shape[0]
    count = 3 if rows % 16 == 0 else 1
    step = rows // count // 16 * 16 if count > 1 else rows
    tiles = [(0, rows - step * (count - 1))]
    tiles += [(tiles[0][1] + step * i, step) for i in range(count - 1)]
    grad_width = 3 * cols + width
    shape, vmem = jax.ShapeDtypeStruct, pltpu.VMEM
    return pl.pallas_call(
        functools.partial(last_kernel, n_dp, n_t, cap, tiles),
        in_specs=[IN_VMEM] * 4 + [ANY] * 9,
        out_specs=[ANY] * 2,
        out_shape=[shape((rows, width), BF), shape((n_t, n_dp // 2, 2, RANK, grad_width), BF)],
        scratch_shapes=[
            vmem(w_full.shape, BF), vmem((3, rows, width), BF), vmem((2, others, rows, width), BF),
            vmem((rows, width), F32), vmem((rows, width), BF), vmem((rows, width), BF), vmem((rows, RANK), BF),
            vmem((rows, width), BF), vmem((n_t, RANK, grad_width), BF), DMA((9,)),
            *Gather.scratch(n_dp, range(n_t)), DMA((len(tiles), 3)),
        ],
        compiler_params=params(collective_id=4, has_side_effects=True),
        name="last_part",
    )(gain, rep, thin, inner_t, dq, dk, dv, dk_far, dv_far, w_full, mgrad, tok, normed)


def sum_kernel(
    width, cols, hid, mid_ref, end_ref, entry_down, entry_up, output_down, output_up, expand_down, expand_up,
    shrink_down, shrink_up,
):
    outs = (entry_down, entry_up, output_down, output_up, expand_down, expand_up, shrink_down, shrink_up)
    for out in outs:
        out[...] = jnp.zeros_like(out)
    sources = mid_ref.shape[0]

    @pl.loop(0, sources)
    def _(i):
        tail = mid_ref[i, :, 3 * width + cols + 2 * hid :].astype(F32)
        a = jnp.max(tail[RANK // 2 :]).astype(jnp.int32)
        take = lambda ref, at, size: ref[i, :, at : at + size].astype(F32)
        expand_down[a] += take(mid_ref, 0, width)
        shrink_up[a] += take(mid_ref, width, width)
        output_up[a] += take(mid_ref, 2 * width, width)
        output_down[a] += take(mid_ref, 3 * width, cols)
        expand_up[a] += take(mid_ref, 3 * width + cols, hid)
        shrink_down[a] += take(mid_ref, 3 * width + cols + hid, hid)
        for which in range(3):
            entry_up[a, which] += take(end_ref, which * cols, cols)
        entry_down[a] += take(end_ref, 3 * cols, width)


def sum_gradients(adapters, cols, hid, width, mid, end):
    shape = jax.ShapeDtypeStruct
    wide = shape((adapters, RANK, width), F32)
    flat = lambda a: a.reshape(-1, *a.shape[-2:])
    return pl.pallas_call(
        functools.partial(sum_kernel, width, cols, hid),
        in_specs=[IN_VMEM] * 2,
        out_specs=[IN_VMEM] * 8,
        out_shape=[
            wide, shape((adapters, 3, RANK, cols), F32), shape((adapters, RANK, cols), F32), wide,
            wide, shape((adapters, RANK, hid), F32), shape((adapters, RANK, hid), F32), wide,
        ],
        compiler_params=params(),
        name="sum_gradients",
    )(flat(mid), flat(end))


def local(
    tokens, cotangent, norm_first, norm_second, entry_weight, output_weight, expand_weight, shrink_weight,
    entry_down, entry_up, output_down, output_up, expand_down, expand_up, shrink_down, shrink_up,
    adapter_choice, clip_count,
):
    cap = adapter_choice.shape[0]
    rows, width = tokens.shape
    adapters = entry_down.shape[0]
    cols, hid = output_weight.shape[1], expand_weight.shape[1]
    gain_first, gain_second = norm_first.reshape(1, width), norm_second.reshape(1, width)
    flip = lambda a: a.transpose(0, 2, 1)
    w_entry = entry_weight.transpose(1, 0, 2).reshape(-1, cols)
    q, k, v, normed, inner_t, thin, rep, tok, k_far, v_far, w_full = first_part(
        cap, adapter_choice, clip_count, tokens, w_entry, gain_first,
        (flip(entry_down), output_up, flip(expand_down), shrink_up),
        (entry_up.transpose(0, 2, 1, 3), flip(output_down), expand_up, flip(shrink_down)),
    )
    att, lse, wo_full, we_near, ws_near, cot = attention_forward(
        cap, q, k, k_far, v, v_far, output_weight, expand_weight, shrink_weight, cotangent
    )
    mixed, mgrad, agrad, grads, _, _ = middle_both_ways(
        cap, tok, att, cot, gain_second, rep, thin, wo_full, we_near, ws_near, expand_weight, shrink_weight
    )
    dq, dk, dv, dk_far, dv_far, mixed, mid_grads = attention_backward(
        cap, q, k, k_far, v, v_far, att, lse, agrad, mixed, grads
    )
    token_grad, end_grads = last_part(
        cap, gain_first, rep, thin, inner_t, dq, dk, dv, dk_far, dv_far, w_full, mgrad, tok, normed
    )
    ed, eu, od, ou, xd, xu, sd, su = sum_gradients(adapters, cols, hid, width, mid_grads, end_grads)
    return (
        mixed, token_grad, flip(ed), eu.transpose(0, 2, 1, 3), flip(od), ou, flip(xd), xu, flip(sd), su,
    )


def solution(mesh):
    in_specs = (
        P(BOTH, None), P(BOTH, None), P(), P(),
        P("dp", None, "tensor"), P("dp", "tensor"), P("dp", "tensor"), P("dp", "tensor"),
        P(), P(None, None, None, "tensor"), P(None, "tensor", None), P(),
        P(), P(None, None, "tensor"), P(None, "tensor", None), P(), P("dp"), P("dp"),
    )
    out_specs = (
        P(BOTH, None), P(BOTH, None), P(), P(None, None, None, "tensor"), P(None, "tensor", None), P(),
        P(), P(None, None, "tensor"), P(None, "tensor", None), P(),
    )
    return jax.shard_map(local, mesh=mesh, in_specs=in_specs, out_specs=out_specs, check_vma=False)
```

```python
import functools

import jax
import jax.numpy as jnp
from jax import lax
from jax.experimental import pallas as pl
from jax.experimental.pallas import tpu as pltpu
from jax.sharding import PartitionSpec as P

HEAD_DIM = 64
PAIR = 2 * HEAD_DIM
RANK = 16
LOG2E = 1.4426950408889634
LN2 = 0.6931471805599453
F32, BF = jnp.float32, jnp.bfloat16
VMEM_LIMIT = 60 * 2**20


def dot(a, b, ca, cb):
    return lax.dot_general(a, b, (((ca,), (cb,)), ((), ())), preferred_element_type=F32)


def params(**more):
    return pltpu.CompilerParams(vmem_limit_bytes=VMEM_LIMIT, **more)


def merge_rows(block):
    return block.reshape(block.shape[0] * block.shape[1], block.shape[2])


def norm_parts(values):
    centre = jnp.mean(values, axis=-1, keepdims=True)
    shifted = values - centre
    scale = lax.rsqrt(jnp.mean(shifted * shifted, axis=-1, keepdims=True) + 1e-05)
    return shifted * scale, scale


def norm_back(hat, scale, gain, grad):
    inner = grad * gain
    mean_one = jnp.mean(inner, axis=-1, keepdims=True)
    mean_two = jnp.mean(inner * hat, axis=-1, keepdims=True)
    return scale * (inner - mean_one - hat * mean_two)


MESH = pl.DeviceIdType.MESH
BOTH = ("dp", "tensor")
ANY = pl.BlockSpec(memory_space=pl.ANY)
IN_VMEM = pl.BlockSpec(memory_space=pltpu.VMEM)
IN_SMEM = pl.BlockSpec(memory_space=pltpu.SMEM)
DMA = pltpu.SemaphoreType.DMA


class Place:
    def __init__(self, n_dp, n_t, cap):
        self.n_dp, self.n_t, self.cap = n_dp, n_t, cap
        self.dp, self.t = lax.axis_index("dp"), lax.axis_index("tensor")
        self.core, self.q = self.dp % 2, self.dp // 2
        self.n_q, self.n_hi = n_dp // 2, n_dp // 4
        self.lo, self.hi = self.q % 2, self.q // 2
        self.group = n_t // cap
        self.half = self.group // 2
        self.slot, block = self.t // self.group, self.t % self.group
        self.high, self.low = block // self.half, block % self.half
        self.stays = self.core == self.high
        self.sibling = (self.dp + 1 - 2 * self.core, self.t)
        self.partner = (self.dp - self.core + self.high, self.t - block + self.core * self.half + self.low)

    def along(self, d):
        return (self.t + d) % self.n_t

    def column(self, d, cols):
        return pl.ds(pl.multiple_of(((self.t + self.n_t - d) % self.n_t) * cols, cols), cols)

    def lo_q(self):
        return self.q + 1 - 2 * self.lo

    def hi_q(self, m, lo=None):
        return ((self.hi + m) % self.n_hi) * 2 + (self.lo if lo is None else lo)

    def device(self, q, core=None, t=None):
        return (q * 2 + (self.core if core is None else core), self.t if t is None else t)

    def mate(self, shift):
        block = (self.core * self.half + self.low + shift) % self.group
        return (self.dp - self.core + block // self.half, self.t - self.low + block % self.half)

    def gather_peers(self):
        return (
            [(self.dp, self.along(d)) for d in range(1, self.n_t)]
            + [self.sibling, self.device(self.lo_q())]
            + [self.device(self.hi_q(m)) for m in range(1, self.n_hi)]
        )

    def other_core_peers(self):
        return [(self.sibling[0], self.along(d)) for d in range(1, self.n_t)]


def greet(peers):
    barrier = pltpu.get_barrier_semaphore()
    for peer in peers:
        pl.semaphore_signal(barrier, inc=1, device_id=peer, device_id_type=MESH)
    pl.semaphore_wait(barrier, len(peers))


def remote(src, dst, send, recv, device):
    return pltpu.make_async_remote_copy(
        src_ref=src, dst_ref=dst, send_sem=send, recv_sem=recv, device_id=device, device_id_type=MESH
    )


class Gather:
    @staticmethod
    def keys(n_hi, ds, here):
        found = []
        for d in ds:
            found += [] if d in here else [("z", d)]
            found += [("x", d), ("s", d)]
            for m in range(1, n_hi):
                found += [("y", m, d), ("dy", m, d), ("dx", m, d)]
        return found

    @staticmethod
    def scratch(n_dp, ds, here=(0,)):
        count = len(Gather.keys(n_dp // 4, ds, here))
        return [DMA((count,)), DMA((count,)), DMA((len(here),))]

    def __init__(self, place, sources, full, ds, sems, spread=None, by_rows=True):
        self.place, self.sources, self.full, self.ds = place, sources, full, list(ds)
        self.send, self.recv, self.own = sems
        self.index = {k: i for i, k in enumerate(Gather.keys(place.n_hi, self.ds, sources))}
        self.spread, self.by_rows = spread, by_rows
        self.ms = range(1, place.n_hi)

    def block(self, d, q, half=None):
        ref = self.full.at[self.ds.index(d), q, self.place.core]
        if half is None:
            return ref
        rows, cols = self.full.shape[-2:]
        if self.by_rows:
            return ref.at[pl.ds(half * (rows // 2), rows // 2)]
        first = cols // 2 // 128 * 128
        return ref.at[:, pl.ds(half * first, cols - first if half else first)]

    def copy(self, key):
        p, kind, d = self.place, key[0], key[-1]
        i = self.index[key]
        if kind == "z":
            src = self.sources[0] if self.spread is None else self.spread(d)
            dst, device = self.block(d, p.q), (p.dp, p.along(d))
        elif kind == "s":
            src = dst = self.full.at[self.ds.index(d), :, p.core]
            device = p.sibling
        elif kind in "xy":
            src = self.sources[d] if d in self.sources else self.block(d, p.q)
            dst = self.block(d, p.q)
            device = p.device(p.lo_q() if kind == "x" else p.hi_q(key[1]))
        elif kind == "dy":
            src = dst = self.block(d, p.lo_q(), 0)
            device = p.device(p.hi_q(key[1]))
        else:
            src = dst = self.block(d, p.hi_q(p.n_hi - key[1]), 1)
            device = p.device(p.lo_q())
        return remote(src, dst, self.send.at[i], self.recv.at[i], device)

    def own_copy(self, d):
        i = list(self.sources).index(d)
        return pltpu.make_async_copy(self.sources[d], self.block(d, self.place.q), self.own.at[i])

    def along(self, d):
        self.copy(("z", d)).start()

    def relay(self, d):
        if d in self.sources:
            self.own_copy(d).start()
        else:
            self.copy(("z", d)).wait_recv()
        self.copy(("x", d)).start()
        for m in self.ms:
            self.copy(("y", m, d)).start()

    def diag(self, d):
        self.copy(("x", d)).wait_recv()
        for m in self.ms:
            self.copy(("dy", m, d)).start()
        for m in self.ms:
            self.copy(("y", m, d)).wait_recv()
            self.copy(("dx", m, d)).start()

    def share(self, d):
        if d in self.sources:
            self.own_copy(d).wait()
        for m in self.ms:
            self.copy(("dy", m, d)).wait_recv()
            self.copy(("dx", m, d)).wait_recv()
        self.copy(("s", d)).start()

    def done(self, d):
        self.copy(("s", d)).wait_recv()

    def finish(self):
        for key in self.index:
            self.copy(key).wait_send()


def run_events(step, batches):
    for i, batch in enumerate(batches):
        if batch:

            @pl.when(step == i)
            def _():
                for event in batch:
                    event()


def cut(names, word):
    parts = [[]]
    for name in names:
        if name.startswith(word):
            parts.append([])
        else:
            parts[-1].append(name)
    return parts


def orders(n_t, pairs, sub, group):
    if (n_t, pairs, sub, group) == (4, 2, 2, 2):
        return FRONT, MIDDLE
    near = n_t // 2
    late = list(reversed(range(near, n_t)))
    front = ["greet", "tok", "e.relay.0", "x.relay.0", "h.relay.0", "o.relay.0"]
    for d in range(1, n_t):
        front += [f"e.along.{d}", f"o.along.{d}"] + ([f"x.along.{d}", f"h.along.{d}"] if d < near else [])
    front += ["lx", "lh", "cot"]
    every = lambda g, d: ([f"{g}.relay.{d}"] if d else []) + [f"{g}.diag.{d}", f"{g}.share.{d}"]
    for d in range(n_t):
        front += every("e", d)
    front += ["wtok", "go", "ln"]
    for d in range(n_t):
        front += [f"ready.{d}", f"proj.{d}"]
    for d in range(n_t):
        front += every("o", d) + (every("x", d) + every("h", d) if d < near else [])
    for d in range(n_t):
        front += [f"arrive.{d}"] + [f"attn.{d * pairs + i}" for i in range(pairs)]
    middle = []
    for g in "xh":
        middle += [f"{g}.relay.{late[0]}"] + [f"{g}.along.{d}" for d in late[1:]]
    middle += ["pre"]
    for i in range(n_t * sub):
        middle += [f"ffn.{i}"]
        if i == 0:
            for d in late:
                for g in "xh":
                    middle += ([f"{g}.relay.{d}"] if d != late[0] else []) + [f"{g}.diag.{d}", f"{g}.share.{d}"]
        if (i + 1) % sub == 0 and near <= (i + 1) // sub < n_t:
            middle += [f"cr.{late[(i + 1) // sub - near]}"]
    return front, middle


FRONT = (
    "greet", "e.along.1", "h.relay.0", "e.relay.0", "x.relay.0", "tok", "e.diag.0", "e.along.2",
    "h.diag.0", "e.share.0", "e.relay.1", "wtok", "e.diag.1", "x.diag.0", "e.along.3", "o.along.3",
    "ln", "e.share.1", "o.relay.0", "o.along.2", "e.relay.2", "ready.0", "go", "x.along.1",
    "proj.0", "h.along.1", "ready.1", "e.relay.3", "arrive.0", "o.diag.0", "attn.0", "o.along.1",
    "x.share.0", "e.diag.2", "e.diag.3", "o.relay.2", "proj.1", "x.relay.1", "attn.1", "e.share.2",
    "h.relay.1", "cot", "arrive.1", "attn.2", "h.share.0", "ready.2", "proj.2", "o.relay.1",
    "e.share.3", "attn.3", "h.diag.1", "o.diag.2", "ready.3", "o.relay.3", "lx", "o.diag.1",
    "proj.3", "arrive.2", "attn.4", "arrive.3", "o.share.0", "h.share.1", "o.diag.3", "o.share.2",
    "x.diag.1", "attn.5", "o.share.1", "lh", "o.share.3", "attn.6", "x.share.1", "attn.7",
)
MIDDLE = (
    "x.along.2", "x.relay.3", "pre", "h.relay.3", "ffn.0", "x.diag.3", "x.relay.2", "h.along.2",
    "ffn.1", "h.diag.3", "ffn.2", "x.diag.2", "x.share.3", "h.share.3", "h.relay.2", "ffn.3",
    "cr.3", "x.share.2", "h.diag.2", "ffn.4", "h.share.2", "ffn.5", "cr.2", "ffn.6",
    "ffn.7",
)


def move(place, source, target, sems, kind, rows=None):
    if rows is not None:
        source, target = source.at[rows], target.at[rows]

    @pl.when(place.stays)
    def _():
        here = pltpu.make_async_copy(source, target, sems[2])
        here.start() if kind == "start" else here.wait()

    @pl.when(jnp.logical_not(place.stays))
    def _():
        there = remote(source, target, sems[0], sems[1], place.partner)
        there.start() if kind == "start" else there.wait()


def head_masks(shape):
    lane = lax.broadcasted_iota(jnp.int32, shape, 1)
    return lane < HEAD_DIM, lane >= HEAD_DIM


def ones_lanes(rows, count):
    lane = lax.broadcasted_iota(jnp.int32, (rows, PAIR), 1)
    return jnp.where(lane < count, 1.0, 0.0).astype(BF)


def attend(queries, keys, values, o_ref, lse_ref):
    rows, length = queries.shape[0], keys.shape[0]
    values = jnp.concatenate([values, ones_lanes(length, 1)], axis=1)
    zero = jnp.zeros_like(queries)
    outs, sums = [], []
    both = [dot(jnp.where(mask, queries, zero), keys, 1, 1) for mask in head_masks(queries.shape)]
    for scores in both:
        top = jnp.max(scores, axis=1, keepdims=True)
        probs = jnp.exp2(scores - top).astype(BF)
        mixed = dot(probs, values, 1, 0)
        total = mixed[:, PAIR : PAIR + 1]
        outs.append(mixed[:, :PAIR] / total)
        sums.append(top + jnp.log2(total))
    first, _ = head_masks((rows, PAIR))
    o_ref[...] = jnp.where(first, outs[0], outs[1]).astype(BF)
    lse_ref[...] = jnp.where(first, sums[0], sums[1])


def front_kernel(
    n_dp, n_t, cap,
    choice_ref, count_ref, gain_ref, ed_tab, ou_tab, xd_tab, su_tab, eu_tab, od_tab, xu_tab, sd_tab,
    tokens_ref, cot_ref, w_ref, wo_ref, we_ref, ws_ref,
    o_ref, lse_ref, inner_t_ref, thin_out, rep_out,
    q_out, k_out, v_out, k_far_out, v_far_out, normed_out, tok_out, cot_out, w_full, wo_full, we_full, ws_full,
    we_land, ws_land,
    q, k, v, k_far, v_far, tok, cot, normed, thin, rep, thin_send, stage, inner,
    tok_sems, cot_sems, thin_sends, thin_recvs, rep_sems, stage_sems, kv_sends, kv_recvs, keep_sems, kept_sems,
    land_sems, go_sem, *sems,
):
    p = Place(n_dp, n_t, cap)
    step, steps = pl.program_id(0), pl.num_programs(0)
    cols, hid = od_tab.shape[-1], xu_tab.shape[-1]
    pairs = cols // PAIR
    depth = w_ref.shape[0] // 3
    early = list(range(n_t // 2))
    entry = Gather(p, {0: w_ref}, w_full, range(n_t), sems[0:3])
    out_g = Gather(p, {0: wo_ref}, wo_full, range(n_t), sems[3:6])
    exp_g = Gather(p, {0: we_ref}, we_full, early, sems[6:9])
    shr_g = Gather(p, {0: ws_ref}, ws_full, early, sems[9:12])
    both = (exp_g, shr_g)
    tok_three = [tok_sems.at[i] for i in range(3)]
    cot_three = [cot_sems.at[i] for i in range(3)]

    def thin_targets():
        for s in range(cap):
            for low in range(p.half):
                to = s * p.group + p.core * p.half + low
                for core in range(2):
                    i = (s * p.half + low) * 2 + core
                    elsewhere = jnp.logical_or(core != p.core, to != p.t)
                    yield s, to, core, i, elsewhere

    def send_thin(near):
        for s, to, core, i, elsewhere in thin_targets():
            d = (to + n_t - p.t) % n_t

            @pl.when(jnp.logical_and(elsewhere, (to == p.t) == near))
            def _():
                remote(
                    thin_send.at[s], thin.at[d], thin_sends.at[i], thin_recvs.at[d], (p.dp - p.core + core, to)
                ).start()

    def send_adapters():
        for s in range(cap):
            a = choice_ref[s]
            for i in range(3):
                thin_send[s, :, i * cols : (i + 1) * cols] = eu_tab[a, i]
            thin_send[s, :, 3 * cols : 4 * cols] = od_tab[a]
            thin_send[s, :, 4 * cols : 4 * cols + hid] = xu_tab[a]
            thin_send[s, :, 4 * cols + hid :] = sd_tab[a]
        send_thin(True)

        @pl.when(p.stays)
        def _():
            a = choice_ref[p.slot]
            for i, table in enumerate((ed_tab, ou_tab, xd_tab, su_tab)):
                rep[i * RANK : (i + 1) * RANK] = table[a]
            row = lax.broadcasted_iota(jnp.int32, (RANK, rep.shape[1]), 0)
            alive = jnp.where(p.slot < count_ref[0], 1.0, 0.0)
            rep[4 * RANK :] = jnp.where(row < RANK // 2, alive, a.astype(F32)).astype(BF)
            remote(rep, rep, rep_sems.at[0], rep_sems.at[1], p.sibling).start()
            thin[0] = thin_send[p.slot]

    def take_near():
        @pl.when(jnp.logical_not(p.stays))
        def _():
            remote(rep, rep, rep_sems.at[0], rep_sems.at[1], p.sibling).wait_recv()
            remote(thin_send.at[0], thin.at[0], thin_sends.at[0], thin_recvs.at[0], p.sibling).wait_recv()

        rep_out[...] = rep[...]
        thin_out[0] = thin[0]

    def take_thin(d):
        remote(thin_send.at[0], thin.at[d], thin_sends.at[0], thin_recvs.at[d], p.sibling).wait_recv()
        thin_out[d] = thin[d]

    def load(d):
        return pltpu.make_async_copy(w_full.at[d], stage.at[d % 2], stage_sems.at[d % 2])

    def kept():
        return [pltpu.make_async_copy(tok, tok_out, keep_sems.at[0]), pltpu.make_async_copy(normed, normed_out, keep_sems.at[1])]

    def first_norm():
        hat, _ = norm_parts(tok[...].astype(F32))
        value = (hat * gain_ref[...]).astype(BF)
        normed[...] = value
        down = rep[:RANK]
        inner[...] = dot(value, down, 1, 1).astype(BF)
        inner_t_ref[...] = dot(down, value, 1, 1).astype(BF)
        for copy in kept():
            copy.start()

    def far_copy(d, which, m):
        source, target = ((k, k_far), (v, v_far))[which]
        device = p.mate(m)
        there = (d + device[1] + n_t - p.t) % n_t
        return remote(
            source.at[pl.ds(d * pairs, pairs)], target.at[m - 1, pl.ds(there * pairs, pairs)],
            kv_sends.at[d, which, m - 1], kv_recvs.at[there, which, m - 1], device,
        )

    def far_arrival(d, which, m):
        source, target = ((k, k_far), (v, v_far))[which]
        return remote(
            source.at[pl.ds(d * pairs, pairs)], target.at[m - 1, pl.ds(d * pairs, pairs)],
            kv_sends.at[d, which, m - 1], kv_recvs.at[d, which, m - 1], p.mate(m),
        )

    def project(d):
        if d:
            take_thin(d)
        load(d).wait()
        for which, out in ((1, k), (2, v), (0, q)):
            weights = stage[d % 2, :, :, which * depth : (which + 1) * depth].reshape(n_dp * depth, cols)
            part = dot(normed[...], weights, 1, 0)
            part = part + dot(inner[...], thin[d, :, which * cols : (which + 1) * cols], 1, 0)
            if which == 0:
                part = part * (HEAD_DIM**-0.5 * LOG2E)
            part = part.astype(BF)
            for i in range(pairs):
                out[d * pairs + i] = part[:, i * PAIR : (i + 1) * PAIR]
            if which:
                for m in range(1, p.group):
                    far_copy(d, which - 1, m).start()

    def copies_out(d):
        at = pl.ds(d * pairs, pairs)
        found = [(a.at[at], b.at[at]) for a, b in ((q, q_out), (k, k_out), (v, v_out))]
        for a, b in ((k_far, k_far_out), (v_far, v_far_out)):
            found += [(a.at[m, at], b.at[m, at]) for m in range(p.group - 1)]
        return [pltpu.make_async_copy(a, b, kept_sems.at[d, i]) for i, (a, b) in enumerate(found)]

    def arrive(d):
        for m in range(1, p.group):
            far_arrival(d, 0, m).wait_recv()
            far_arrival(d, 1, m).wait_recv()
        for copy in copies_out(d):
            copy.start()

    def land(i):
        source, target = ((we_ref, we_land), (ws_ref, ws_land))[i]
        return remote(source, target, land_sems.at[0, i], land_sems.at[1, i], (p.dp, p.along(n_t - 1)))

    def ready(d):
        entry.done(d)
        load(d).start()

    def go():
        @pl.when(jnp.logical_not(p.stays))
        def _():
            pl.semaphore_signal(go_sem, inc=1, device_id=p.sibling, device_id_type=MESH)

        @pl.when(p.stays)
        def _():
            pl.semaphore_wait(go_sem, 1)

    def arrived():
        move(p, tokens_ref, tok, tok_three, "wait")
        send_thin(False)

    def norm():
        take_near()
        first_norm()

    def opened():
        greet(p.gather_peers() + p.other_core_peers())

    gathers = {"e": entry, "x": exp_g, "h": shr_g, "o": out_g}
    plain = {
        "greet": opened, "go": go, "wtok": arrived, "ln": norm,
        "tok": lambda: move(p, tokens_ref, tok, tok_three, "start"),
        "cot": lambda: move(p, cot_ref, cot, cot_three, "start"),
        "lx": lambda: land(0).start(), "lh": lambda: land(1).start(),
        "adapters": send_adapters,
    }
    counted = {"ready": ready, "proj": project, "arrive": arrive}

    def event(name):
        word = name.split(".")
        if len(word) == 1:
            return plain[name]
        if len(word) == 2:
            return lambda: counted[word[0]](int(word[1]))
        return lambda: getattr(gathers[word[0]], word[1])(int(word[2]))

    names = list(orders(n_t, pairs, max(1, hid // 512), p.group)[0])
    names.insert(names.index("e.diag.0"), "adapters")
    batches = [[event(name) for name in part] for part in cut(names, "attn")]
    closing = batches.pop()
    run_events(step, batches)
    keys = jnp.concatenate([k[step]] + [k_far[m, step] for m in range(p.group - 1)], axis=0)
    values = jnp.concatenate([v[step]] + [v_far[m, step] for m in range(p.group - 1)], axis=0)
    attend(q[step], keys, values, o_ref, lse_ref)

    @pl.when(step == steps - 1)
    def _():
        for call in closing:
            call()
        for g in (exp_g, shr_g, out_g):
            for d in g.ds:
                g.done(d)
        for g in (entry, exp_g, shr_g, out_g):
            g.finish()
        for i in range(2):
            land(i).wait()
        move(p, cot_ref, cot, cot_three, "wait")
        keep_cot = pltpu.make_async_copy(cot, cot_out, keep_sems.at[2])
        keep_cot.start()

        @pl.when(p.stays)
        def _():
            remote(rep, rep, rep_sems.at[0], rep_sems.at[1], p.sibling).wait_send()

        for s, to, core, i, elsewhere in thin_targets():

            @pl.when(elsewhere)
            def _():
                remote(thin_send.at[s], thin.at[0], thin_sends.at[i], thin_recvs.at[0], p.sibling).wait_send()

        for copy in [keep_cot, *kept()]:
            copy.wait()
        for d in range(n_t):
            for m in range(1, p.group):
                far_copy(d, 0, m).wait_send()
                far_copy(d, 1, m).wait_send()
            for copy in copies_out(d):
                copy.wait()


def front_part(cap, choice, count, gain, rep_tables, thin_tables, tokens, cot, w, wo, we, ws):
    n_dp, n_t = lax.axis_size("dp"), lax.axis_size("tensor")
    rows, width = tokens.shape
    cols = wo.shape[-1]
    others = n_t // cap - 1
    count_pairs = width // PAIR
    early = n_t // 2
    thin_width = 4 * cols + 2 * we.shape[-1]
    shape, vmem = jax.ShapeDtypeStruct, pltpu.VMEM
    whole = lambda *s: pl.BlockSpec(s, lambda h: (0,) * len(s))
    pair = pl.BlockSpec((None, rows, PAIR), lambda h: (h, 0, 0))
    full = lambda n, a: shape((n, n_dp // 2, 2, *a.shape), BF)
    heads, far = (count_pairs, rows, PAIR), (others, count_pairs, rows, PAIR)
    small = [(RANK, rows), (n_t, RANK, thin_width), (5 * RANK, width)]
    return pl.pallas_call(
        functools.partial(front_kernel, n_dp, n_t, cap),
        grid=(count_pairs,),
        in_specs=[IN_SMEM, IN_SMEM] + [whole(*a.shape) for a in (gain, *rep_tables, *thin_tables)]
        + [ANY] * 2 + [whole(*a.shape) for a in (w, wo, we, ws)],
        out_specs=[pair, pair] + [whole(*s) for s in small] + [ANY] * 14,
        out_shape=[shape(heads, BF), shape(heads, F32)] + [shape(s, BF) for s in small]
        + [shape(heads, BF)] * 3 + [shape(far, BF)] * 2 + [shape((rows, width), BF)] * 3
        + [full(n_t, w), full(n_t, wo), full(early, we), full(early, ws), shape(we.shape, BF), shape(ws.shape, BF)],
        scratch_shapes=[
            vmem(heads, BF), vmem(heads, BF), vmem(heads, BF), vmem(far, BF), vmem(far, BF),
            vmem((rows, width), BF), vmem((rows, width), BF), vmem((rows, width), BF), vmem(small[1], BF), vmem(small[2], BF),
            vmem((cap, RANK, thin_width), BF),
            vmem((2, n_dp // 2, 2, *w.shape), BF), vmem((rows, RANK), BF),
            DMA((3,)), DMA((3,)), DMA((n_t,)), DMA((n_t,)), DMA((2,)), DMA((2,)),
            DMA((n_t, 2, others)), DMA((n_t, 2, others)), DMA((3,)), DMA((n_t, 3 + 2 * others)), DMA((2, 2)),
            pltpu.SemaphoreType.REGULAR,
            *Gather.scratch(n_dp, range(n_t)), *Gather.scratch(n_dp, range(n_t)),
            *Gather.scratch(n_dp, range(early)), *Gather.scratch(n_dp, range(early)),
        ],
        compiler_params=params(collective_id=0, has_side_effects=True),
        name="front_part",
    )(choice, count, gain, *rep_tables, *thin_tables, tokens, cot, w, wo, we, ws)


def split_lanes(column):
    column = -column
    high = column.astype(BF)
    rest = column - high.astype(F32)
    mid = rest.astype(BF)
    low = (rest - mid.astype(F32)).astype(BF)
    lane = lax.broadcasted_iota(jnp.int32, (column.shape[0], PAIR), 1)
    zero = jnp.zeros((column.shape[0], PAIR), BF)
    return jnp.where(lane == 0, high, jnp.where(lane == 1, mid, jnp.where(lane == 2, low, zero)))


def back_kernel(
    n_dp, n_t, cap, tiles,
    q_ref, k_ref, k_far, v_ref, v_far, o_ref, lse_ref, do_ref, gain_ref, rep_ref, thin_ref, inner_t_ref, grads_ref,
    mixed_ref, w_ref, mgrad_ref, tok_ref, normed_ref,
    mixed_out, mid_full, tgrad_out, end_full,
    grad, send, far, mixed, weights, mgrad, tok, normed, back_low, tgrad, end, sends, recvs, swap, swaps, load_sems,
    *sems,
):
    p = Place(n_dp, n_t, cap)
    step, steps = pl.program_id(0), pl.num_programs(0)
    rows = q_ref.shape[0]
    pairs = grad.shape[1] // n_t
    cols = w_ref.shape[-1]
    depth = w_ref.shape[-2] // 3
    width = tok_ref.shape[1]
    mid_g = Gather(
        p, {0: grads_ref.at[0]}, mid_full, range(n_t), sems[0:3],
        spread=lambda d: grads_ref.at[n_t - d], by_rows=False,
    )
    end_g = Gather(
        p, {0: end.at[0]}, end_full, range(n_t), sems[3:6], spread=lambda d: end.at[n_t - d], by_rows=False
    )
    swap_sems = [swap.at[i] for i in range(3)]
    loads = [
        pltpu.make_async_copy(src, dst, load_sems.at[i])
        for i, (src, dst) in enumerate(((w_ref, weights), (normed_ref, normed), (tok_ref, tok), (mgrad_ref, mgrad)))
    ]
    relay, diag, share = ((lambda d, f=f: lambda: f(d)) for f in (mid_g.relay, mid_g.diag, mid_g.share))
    start_swap = lambda: move(p, mixed_ref, mixed, swap_sems, "start")
    start_loads = lambda: [copy.start() for copy in loads]

    def opening():
        greet(p.gather_peers() + p.other_core_peers())
        mid_g.relay(0)
        for d in range(1, n_t):
            mid_g.along(d)

    if n_t == 4:
        table = {
            0: [opening], 1: [diag(0), relay(1)], 2: [share(0), diag(1), relay(2), start_swap],
            3: [share(1), diag(2), relay(3)], 4: [share(2), diag(3), start_loads], 5: [share(3)],
        }
    else:
        table = {0: [opening, start_swap, start_loads, diag(0), share(0)]}
        for d in range(1, n_t):
            table[0] += [relay(d), diag(d), share(d)]
    run_events(step, [table.get(i, []) for i in range(max(table) + 1)])

    with_far = lambda near, far: jnp.concatenate([near[...]] + [far[m] for m in range(p.group - 1)], axis=0)
    keys = with_far(k_ref, k_far)
    length = keys.shape[0]
    ones = ones_lanes(length, 3)
    keys_more = jnp.concatenate([keys, ones], axis=1)
    values_more = jnp.concatenate([with_far(v_ref, v_far), ones], axis=1)
    queries, grad_out = q_ref[...], do_ref[...]
    zero = jnp.zeros_like(queries)
    product = grad_out.astype(F32) * o_ref[...].astype(F32)
    d_queries, d_keys, d_values = [], 0.0, 0.0
    for head, mask in enumerate(head_masks(queries.shape)):
        query = jnp.where(mask, queries, zero)
        grad_head = jnp.where(mask, grad_out, zero)
        lse = lse_ref[:, head * HEAD_DIM : head * HEAD_DIM + 1]
        delta = jnp.sum(jnp.where(mask, product, 0.0), axis=1, keepdims=True)
        probs = jnp.exp2(dot(jnp.concatenate([query, split_lanes(lse)], axis=1), keys_more, 1, 1))
        slope = dot(jnp.concatenate([grad_head, split_lanes(delta)], axis=1), values_more, 1, 1)
        score_grad = (probs * slope).astype(BF)
        d_queries.append(dot(score_grad, keys, 1, 0))
        d_values = d_values + dot(grad_head, probs.astype(BF), 0, 0)
        d_keys = d_keys + dot(query, score_grad, 0, 0)
    first, _ = head_masks((rows, PAIR))
    grad[0, step] = (jnp.where(first, d_queries[0], d_queries[1]) * HEAD_DIM**-0.5).astype(BF)
    d_keys = (d_keys * LN2).T.astype(BF)
    d_values = d_values.T.astype(BF)
    grad[1, step] = d_keys[:rows]
    grad[2, step] = d_values[:rows]

    def far_copy(i, m, h):
        device = p.mate(p.group - m)
        there = (h // pairs + device[1] + n_t - p.t) % n_t * pairs + h % pairs
        return remote(
            send.at[i, m - 1, h], far.at[i, m - 1, there], sends.at[i, m - 1, h], recvs.at[i, m - 1, there], device
        )

    for m in range(1, p.group):
        send[0, m - 1, step] = d_keys[m * rows : (m + 1) * rows]
        send[1, m - 1, step] = d_values[m * rows : (m + 1) * rows]
        far_copy(0, m, step).start()
        far_copy(1, m, step).start()

    @pl.when(step == steps - 1)
    def _():
        move(p, mixed_ref, mixed, swap_sems, "wait")
        keep = pltpu.make_async_copy(mixed, mixed_out, swap.at[3])
        keep.start()
        for i in range(2):
            for m in range(1, p.group):
                for h in range(n_t * pairs):
                    remote(
                        send.at[i, m - 1, h], far.at[i, m - 1, h], sends.at[i, m - 1, h], recvs.at[i, m - 1, h], p.sibling
                    ).wait_recv()
            for h in range(n_t * pairs):
                total = grad[1 + i, h].astype(F32)
                for m in range(p.group - 1):
                    total = total + far[i, m, h].astype(F32)
                grad[1 + i, h] = total.astype(BF)
        columns = lambda which, d, rows: jnp.concatenate(
            [grad[which, d * pairs + i, rows] for i in range(pairs)], axis=1
        )
        back = 0.0
        for d in range(n_t):
            for which in range(3):
                up = thin_ref[d, :, which * cols : (which + 1) * cols]
                back = back + dot(columns(which, d, slice(None)), up, 1, 1)
        back_low[...] = back.astype(BF)
        for copy in loads:
            copy.wait()

        def tile(n):
            start, count = tiles[n]
            rows = pl.ds(start, count)
            total = dot(back_low[rows], rep_ref[:RANK], 1, 0)
            for d in range(n_t):
                for which in range(3):
                    piece = weights[d, :, :, which * depth : (which + 1) * depth].reshape(width, cols)
                    total = total + dot(columns(which, d, rows), piece, 1, 1)
            hat, scale = norm_parts(tok[rows].astype(F32))
            tgrad[rows] = (mgrad[rows] + norm_back(hat, scale, gain_ref[...], total)).astype(BF)
            move(p, tgrad, tgrad_out, [swaps.at[n, i] for i in range(3)], "start", rows)

        tile(0)
        down_grad = dot(back_low[...], normed[...], 0, 0).astype(BF)
        for d in range(n_t):
            for which in range(3):
                end[d, :, which * cols : (which + 1) * cols] = dot(
                    inner_t_ref[...], columns(which, d, slice(None)), 1, 0
                ).astype(BF)
            end[d, :, 3 * cols :] = down_grad
        end_g.relay(0)
        for d in range(1, n_t):
            end_g.along(d)
        for n in range(1, len(tiles)):
            tile(n)
            if n == 1:
                end_g.diag(0)
        if len(tiles) == 1:
            end_g.diag(0)
        for d in range(1, n_t):
            end_g.relay(d)
            end_g.share(d - 1)
            end_g.diag(d)
        end_g.share(n_t - 1)
        for d in range(n_t):
            mid_g.done(d)
            end_g.done(d)
        mid_g.finish()
        end_g.finish()
        for n, (start, count) in enumerate(tiles):
            move(p, tgrad, tgrad_out, [swaps.at[n, i] for i in range(3)], "wait", pl.ds(start, count))

        @pl.loop(0, steps)
        def _(h):
            for m in range(1, p.group):
                for i in range(2):
                    far_copy(i, m, h).wait_send()

        keep.wait()


def back_part(cap, q, k, k_far, v, v_far, o, lse, do, gain, rep, thin, inner_t, grads, mixed, w_full, mgrad, tok, normed):
    n_dp, n_t = lax.axis_size("dp"), lax.axis_size("tensor")
    heads, rows, _ = q.shape
    width, cols = tok.shape[1], w_full.shape[-1]
    others = k_far.shape[0]
    pair = pl.BlockSpec((None, rows, PAIR), lambda h: (h, 0, 0))
    far = pl.BlockSpec((others, None, rows, PAIR), lambda h: (0, h, 0, 0))
    whole = lambda a: pl.BlockSpec(a.shape, lambda h: (0,) * len(a.shape))
    shape, vmem = jax.ShapeDtypeStruct, pltpu.VMEM
    count = (2, others, heads)
    number = 3 if rows % 16 == 0 else 1
    size = rows // number // 16 * 16 if number > 1 else rows
    tiles = [(0, rows - size * (number - 1))]
    tiles += [(tiles[0][1] + size * i, size) for i in range(number - 1)]
    end_width = 3 * cols + width
    full = lambda n: shape((n_t, n_dp // 2, 2, RANK, n), BF)
    return pl.pallas_call(
        functools.partial(back_kernel, n_dp, n_t, cap, tiles),
        grid=(heads,),
        in_specs=[pair, pair, far, pair, far, pair, pair, pair]
        + [whole(a) for a in (gain, rep, thin, inner_t, grads)] + [ANY] * 5,
        out_specs=[ANY] * 4,
        out_shape=[shape(mixed.shape, BF), full(grads.shape[-1]), shape(tok.shape, BF), full(end_width)],
        scratch_shapes=[
            vmem((3, heads, rows, PAIR), BF), vmem((2, *k_far.shape), BF), vmem((2, *k_far.shape), BF),
            vmem(mixed.shape, BF), vmem(w_full.shape, BF), vmem(mgrad.shape, F32), vmem(tok.shape, BF),
            vmem(tok.shape, BF), vmem((rows, RANK), BF), vmem(tok.shape, BF), vmem((n_t, RANK, end_width), BF),
            DMA(count), DMA(count), DMA((4,)), DMA((len(tiles), 3)), DMA((4,)),
            *Gather.scratch(n_dp, range(n_t)), *Gather.scratch(n_dp, range(n_t)),
        ],
        compiler_params=params(collective_id=1, has_side_effects=True),
        name="back_part",
    )(q, k, k_far, v, v_far, o, lse, do, gain, rep, thin, inner_t, grads, mixed, w_full, mgrad, tok, normed)


def gelu_parts(hidden):
    share = 0.5 * (1.0 + lax.erf(hidden * 0.7071067811865476))
    density = jnp.exp(-0.5 * hidden * hidden) * 0.3989422804014327
    return hidden * share, share + hidden * density


def middle_kernel(
    n_dp, n_t, cap, sub,
    x_ref, att_ref, cot_ref, gain_ref, rep_ref, thin_ref, wo_ref, we_near, ws_near, we_land, ws_land, we_ref, ws_ref,
    mixed_ref, mgrad_ref, agrad_ref, grads_ref, we_full, ws_full,
    middle_ref, second_ref, dy_ref, acc2_ref, acc3_ref, einner_ref, einner_t_ref, sback_ref, sback_t_ref,
    sinner_ref, eback_ref, oinner_ref, we_buf, ws_buf, buf_sems, *sems,
):
    p = Place(n_dp, n_t, cap)
    step, steps = pl.program_id(0), pl.num_programs(0)
    cols = wo_ref.shape[-1]
    width = x_ref.shape[1]
    hid = we_ref.shape[-1]
    size = hid // sub
    near = n_t // 2
    late = list(reversed(range(near, n_t)))
    exp_g = Gather(p, {n_t - 1: we_land}, we_full, late, sems[0:3], spread=lambda d: we_ref)
    shr_g = Gather(p, {n_t - 1: ws_land}, ws_full, late, sems[3:6], spread=lambda d: ws_ref)
    pairs = cols // PAIR
    both = (exp_g, shr_g)
    down_e, up_o, up_s = rep_ref[2 * RANK : 3 * RANK], rep_ref[RANK : 2 * RANK], rep_ref[3 * RANK : 4 * RANK]
    alive = rep_ref[4 * RANK : 4 * RANK + 1, 0:1].astype(F32)
    at_od, at_eu = 3 * width, 3 * width + cols
    at_sd, at_id = at_eu + hid, at_eu + 2 * hid

    def load(i):
        index, part = i // sub, i % sub
        at = pl.ds(part * size, size)
        pair = (we_near, ws_near) if index < near else (we_full, ws_full)
        index = index if index < near else index - near
        return [
            pltpu.make_async_copy(src.at[index, :, :, :, at], buf.at[i % 3], buf_sems.at[i % 3, j])
            for j, (src, buf) in enumerate(zip(pair, (we_buf, ws_buf)))
        ]

    gathers = {"x": exp_g, "h": shr_g}

    def bring(d):
        exp_g.done(d)
        shr_g.done(d)
        for i in range(sub):
            for copy in load((near + late.index(d)) * sub + i):
                copy.start()

    def event(name):
        word = name.split(".")
        if len(word) == 2:
            return lambda: bring(int(word[1]))
        return lambda: getattr(gathers[word[0]], word[1])(int(word[2]))

    names = orders(n_t, pairs, sub, p.group)[1]
    begun = names.index("pre")
    start = [event(name) for name in names[:begun]]
    opening, *after = [[event(name) for name in part] for part in cut(names[begun + 1 :], "ffn")]
    columns = lambda d: jnp.concatenate([att_ref[d * pairs + i] for i in range(pairs)], axis=1)

    @pl.when(step == 0)
    def _():
        greet(p.gather_peers())
        for call in start:
            call()
        for i in range(2):
            for copy in load(i):
                copy.start()
        branch, inner = 0.0, 0.0
        for d in range(n_t):
            att = columns(d)
            branch = branch + dot(att, wo_ref[d].reshape(width, cols), 1, 1)
            inner = inner + dot(att, thin_ref[d, :, 3 * cols : 4 * cols], 1, 1)
        inner = inner.astype(BF)
        oinner_ref[...] = inner
        middle = x_ref[...].astype(F32) + (branch + dot(inner, up_o, 1, 0))
        middle_ref[...] = middle
        hat, _ = norm_parts(middle)
        second = (hat * gain_ref[...]).astype(BF)
        second_ref[...] = second
        dy = (cot_ref[...].astype(F32) * alive).astype(BF)
        dy_ref[...] = dy
        einner_ref[...] = dot(second, down_e, 1, 1).astype(BF)
        einner_t_ref[...] = dot(down_e, second, 1, 1).astype(BF)
        sback_ref[...] = dot(dy, up_s, 1, 1).astype(BF)
        sback_t_ref[...] = dot(up_s, dy, 1, 1).astype(BF)
        acc2_ref[...] = jnp.zeros_like(acc2_ref)
        acc3_ref[...] = jnp.zeros_like(acc3_ref)
        sinner_ref[...] = jnp.zeros_like(sinner_ref)
        eback_ref[...] = jnp.zeros_like(eback_ref)

    run_events(step, [opening])
    for i in range(n_t * sub):

        @pl.when(step == i)
        def _():
            for copy in load(i):
                copy.wait()
            if i + 2 < near * sub:
                for copy in load(i + 2):
                    copy.start()

    buf = step % 3
    d, part = step // sub, step % sub
    d = jnp.where(d < near, d, n_t - 1 + near - d)
    we, ws = we_buf[buf].reshape(width, size), ws_buf[buf].reshape(width, size)
    at = pl.multiple_of(part * size, size)
    e_up = thin_ref[d, :, pl.ds(4 * cols + at, size)]
    s_down = thin_ref[d, :, pl.ds(4 * cols + hid + at, size)]
    hidden = dot(second_ref[...], we, 1, 0) + dot(einner_ref[...], e_up, 1, 0)
    value, slope = gelu_parts(hidden)
    act = value.astype(BF)
    acc2_ref[...] += dot(act, ws, 1, 1)
    sinner_ref[...] += dot(act, s_down, 1, 1)
    act_grad = dot(dy_ref[...], ws, 1, 0) + dot(sback_ref[...], s_down, 1, 0)
    hid_grad = (act_grad * slope).astype(BF)
    acc3_ref[...] += dot(hid_grad, we, 1, 1)
    eback_ref[...] += dot(hid_grad, e_up, 1, 1)
    grads_ref[d, :, pl.ds(at_eu + at, size)] = dot(einner_t_ref[...], hid_grad, 1, 0).astype(BF)
    grads_ref[d, :, pl.ds(at_sd + at, size)] = dot(sback_t_ref[...], act, 1, 0).astype(BF)

    run_events(step, after)
    @pl.when(step == steps - 1)
    def _():
        s_inner, e_back = sinner_ref[...].astype(BF), eback_ref[...].astype(BF)
        middle = middle_ref[...]
        mixed_ref[...] = (alive * (middle + (acc2_ref[...] + dot(s_inner, up_s, 1, 0)))).astype(BF)
        shrink_up = dot(s_inner, dy_ref[...], 0, 0).astype(BF)
        expand_down = dot(e_back, second_ref[...], 0, 0).astype(BF)
        second_grad = acc3_ref[...] + dot(e_back, down_e, 1, 0)
        hat, scale = norm_parts(middle)
        mgrad = cot_ref[...].astype(F32) * alive + norm_back(hat, scale, gain_ref[...], second_grad)
        mgrad_ref[...] = mgrad
        low = mgrad.astype(BF)
        o_back = dot(low, up_o, 1, 1).astype(BF)
        output_up = dot(oinner_ref[...], low, 0, 0).astype(BF)
        for d in range(n_t):
            agrad = dot(low, wo_ref[d].reshape(width, cols), 1, 0)
            agrad = (agrad + dot(o_back, thin_ref[d, :, 3 * cols : 4 * cols], 1, 0)).astype(BF)
            for i in range(pairs):
                agrad_ref[d * pairs + i] = agrad[:, i * PAIR : (i + 1) * PAIR]
            grads_ref[d, :, :width] = expand_down
            grads_ref[d, :, width : 2 * width] = shrink_up
            grads_ref[d, :, 2 * width : 3 * width] = output_up
            grads_ref[d, :, at_od : at_od + cols] = dot(o_back, columns(d), 0, 0).astype(BF)
            grads_ref[d, :, at_id:] = rep_ref[4 * RANK :, : grads_ref.shape[2] - at_id]
        for g in both:
            g.finish()


ID_LANES = 128


def middle_both_ways(cap, x, att, cot, gain, rep, thin, wo_full, we_near, ws_near, we_land, ws_land, we, ws):
    n_dp, n_t = lax.axis_size("dp"), lax.axis_size("tensor")
    rows, width = x.shape
    depth, hid = we.shape
    cols = wo_full.shape[-1]
    sub = max(1, hid // 512)
    size = hid // sub
    late = list(reversed(range(n_t // 2, n_t)))
    grad_width = 3 * width + cols + 2 * hid + ID_LANES
    whole = lambda a: pl.BlockSpec(a.shape, lambda i: (0,) * len(a.shape))
    shape = jax.ShapeDtypeStruct
    full = shape((len(late), n_dp // 2, 2, depth, hid), BF)
    outs = [
        shape((rows, width), BF), shape((rows, width), F32), shape(att.shape, BF),
        shape((n_t, RANK, grad_width), BF),
    ]
    vmem = pltpu.VMEM
    return pl.pallas_call(
        functools.partial(middle_kernel, n_dp, n_t, cap, sub),
        grid=(n_t * sub,),
        in_specs=[whole(a) for a in (x, att, cot, gain, rep, thin, wo_full)]
        + [ANY] * 2 + [whole(we_land), whole(ws_land)] + [ANY] * 2,
        out_specs=[whole(a) for a in outs] + [ANY] * 2,
        out_shape=outs + [full, full],
        scratch_shapes=[
            vmem((rows, width), F32), vmem((rows, width), BF), vmem((rows, width), BF),
            vmem((rows, width), F32), vmem((rows, width), F32),
            vmem((rows, RANK), BF), vmem((RANK, rows), BF), vmem((rows, RANK), BF), vmem((RANK, rows), BF),
            vmem((rows, RANK), F32), vmem((rows, RANK), F32), vmem((rows, RANK), BF),
            vmem((3, n_dp // 2, 2, depth, size), BF), vmem((3, n_dp // 2, 2, depth, size), BF), DMA((3, 2)),
            *Gather.scratch(n_dp, late, late[:1]), *Gather.scratch(n_dp, late, late[:1]),
        ],
        compiler_params=params(collective_id=2, has_side_effects=True),
        name="middle_both_ways",
    )(x, att, cot, gain, rep, thin, wo_full, we_near, ws_near, we_land, ws_land, we, ws)


def sum_kernel(
    width, cols, hid, mid_ref, end_ref, entry_down, entry_up, output_down, output_up, expand_down, expand_up,
    shrink_down, shrink_up,
):
    outs = (entry_down, entry_up, output_down, output_up, expand_down, expand_up, shrink_down, shrink_up)

    @pl.when(pl.program_id(0) == 0)
    def _():
        for out in outs:
            out[...] = jnp.zeros_like(out)

    sources = range(mid_ref.shape[0])
    at_id = 3 * width + cols + 2 * hid
    chosen = [jnp.max(mid_ref[i, RANK // 2 :, at_id : at_id + 128].astype(F32)).astype(jnp.int32) for i in sources]
    for i in sources:
        a = chosen[i]
        take = lambda ref, at, size: ref[i, :, at : at + size].astype(F32)
        expand_down[a] += take(mid_ref, 0, width)
        shrink_up[a] += take(mid_ref, width, width)
        output_up[a] += take(mid_ref, 2 * width, width)
        output_down[a] += take(mid_ref, 3 * width, cols)
        expand_up[a] += take(mid_ref, 3 * width + cols, hid)
        shrink_down[a] += take(mid_ref, 3 * width + cols + hid, hid)
        for which in range(3):
            entry_up[a, which] += take(end_ref, which * cols, cols)
        entry_down[a] += take(end_ref, 3 * cols, width)


def sum_gradients(adapters, cols, hid, width, mid, end):
    shape = jax.ShapeDtypeStruct
    wide = shape((adapters, RANK, width), F32)
    flat = lambda a: a.reshape(a.shape[0], -1, *a.shape[-2:])
    mid, end = flat(mid), flat(end)
    outs = [
        wide, shape((adapters, 3, RANK, cols), F32), shape((adapters, RANK, cols), F32), wide,
        wide, shape((adapters, RANK, hid), F32), shape((adapters, RANK, hid), F32), wide,
    ]
    part = lambda a: pl.BlockSpec((None, *a.shape[1:]), lambda i: (i, 0, 0, 0))
    return pl.pallas_call(
        functools.partial(sum_kernel, width, cols, hid),
        grid=(mid.shape[0],),
        in_specs=[part(mid), part(end)],
        out_specs=[pl.BlockSpec(a.shape, lambda i, n=len(a.shape): (0,) * n) for a in outs],
        out_shape=outs,
        compiler_params=params(),
        name="sum_gradients",
    )(mid, end)


def local(
    tokens, cotangent, norm_first, norm_second, entry_weight, output_weight, expand_weight, shrink_weight,
    entry_down, entry_up, output_down, output_up, expand_down, expand_up, shrink_down, shrink_up,
    adapter_choice, clip_count,
):
    cap = adapter_choice.shape[0]
    rows, width = tokens.shape
    adapters = entry_down.shape[0]
    cols, hid = output_weight.shape[1], expand_weight.shape[1]
    gain_first, gain_second = norm_first.reshape(1, width), norm_second.reshape(1, width)
    flip = lambda a: a.transpose(0, 2, 1)
    w_entry = entry_weight.transpose(1, 0, 2).reshape(-1, cols)
    (
        att, lse, inner_t, thin, rep, q, k, v, k_far, v_far, normed, tok, cot, w_full, wo_full, we_near, ws_near,
        we_land, ws_land,
    ) = front_part(
        cap, adapter_choice, clip_count, gain_first,
        (flip(entry_down), output_up, flip(expand_down), shrink_up),
        (entry_up.transpose(0, 2, 1, 3), flip(output_down), expand_up, flip(shrink_down)),
        tokens, cotangent, w_entry, output_weight, expand_weight, shrink_weight,
    )
    mixed, mgrad, agrad, grads, _, _ = middle_both_ways(
        cap, tok, att, cot, gain_second, rep, thin, wo_full, we_near, ws_near, we_land, ws_land,
        expand_weight, shrink_weight,
    )
    mixed, mid_grads, token_grad, end_grads = back_part(
        cap, q, k, k_far, v, v_far, att, lse, agrad, gain_first, rep, thin, inner_t, grads, mixed, w_full, mgrad, tok,
        normed,
    )
    ed, eu, od, ou, xd, xu, sd, su = sum_gradients(adapters, cols, hid, width, mid_grads, end_grads)
    return (
        mixed, token_grad, flip(ed), eu.transpose(0, 2, 1, 3), flip(od), ou, flip(xd), xu, flip(sd), su,
    )


def solution(mesh):
    in_specs = (
        P(BOTH, None), P(BOTH, None), P(), P(),
        P("dp", None, "tensor"), P("dp", "tensor"), P("dp", "tensor"), P("dp", "tensor"),
        P(), P(None, None, None, "tensor"), P(None, "tensor", None), P(),
        P(), P(None, None, "tensor"), P(None, "tensor", None), P(), P("dp"), P("dp"),
    )
    out_specs = (
        P(BOTH, None), P(BOTH, None), P(), P(None, None, None, "tensor"), P(None, "tensor", None), P(),
        P(), P(None, None, "tensor"), P(None, "tensor", None), P(),
    )
    return jax.shard_map(local, mesh=mesh, in_specs=in_specs, out_specs=out_specs, check_vma=False)
```

```python
import functools

import jax
import jax.numpy as jnp
from jax import lax
from jax.experimental import pallas as pl
from jax.experimental.pallas import tpu as pltpu
from jax.sharding import PartitionSpec as P

HEAD_DIM = 64
PAIR = 2 * HEAD_DIM
RANK = 16
LOG2E = 1.4426950408889634
LN2 = 0.6931471805599453
F32, BF = jnp.float32, jnp.bfloat16
VMEM_LIMIT = 60 * 2**20


def dot(a, b, ca, cb):
    return lax.dot_general(a, b, (((ca,), (cb,)), ((), ())), preferred_element_type=F32)


def params(**more):
    return pltpu.CompilerParams(vmem_limit_bytes=VMEM_LIMIT, **more)


def merge_rows(block):
    return block.reshape(block.shape[0] * block.shape[1], block.shape[2])


def norm_parts(values):
    centre = jnp.mean(values, axis=-1, keepdims=True)
    shifted = values - centre
    scale = lax.rsqrt(jnp.mean(shifted * shifted, axis=-1, keepdims=True) + 1e-05)
    return shifted * scale, scale


def norm_back(hat, scale, gain, grad):
    inner = grad * gain
    mean_one = jnp.mean(inner, axis=-1, keepdims=True)
    mean_two = jnp.mean(inner * hat, axis=-1, keepdims=True)
    return scale * (inner - mean_one - hat * mean_two)


MESH = pl.DeviceIdType.MESH
BOTH = ("dp", "tensor")
ANY = pl.BlockSpec(memory_space=pl.ANY)
IN_VMEM = pl.BlockSpec(memory_space=pltpu.VMEM)
IN_SMEM = pl.BlockSpec(memory_space=pltpu.SMEM)
DMA = pltpu.SemaphoreType.DMA


class Place:
    def __init__(self, n_dp, n_t, cap):
        self.n_dp, self.n_t, self.cap = n_dp, n_t, cap
        self.dp, self.t = lax.axis_index("dp"), lax.axis_index("tensor")
        self.core, self.q = self.dp % 2, self.dp // 2
        self.n_q, self.n_hi = n_dp // 2, n_dp // 4
        self.lo, self.hi = self.q % 2, self.q // 2
        self.group = n_t // cap
        self.half = self.group // 2
        self.slot, block = self.t // self.group, self.t % self.group
        self.high, self.low = block // self.half, block % self.half
        self.stays = self.core == self.high
        self.sibling = (self.dp + 1 - 2 * self.core, self.t)
        self.partner = (self.dp - self.core + self.high, self.t - block + self.core * self.half + self.low)

    def along(self, d):
        return (self.t + d) % self.n_t

    def column(self, d, cols):
        return pl.ds(pl.multiple_of(((self.t + self.n_t - d) % self.n_t) * cols, cols), cols)

    def lo_q(self):
        return self.q + 1 - 2 * self.lo

    def hi_q(self, m, lo=None):
        return ((self.hi + m) % self.n_hi) * 2 + (self.lo if lo is None else lo)

    def device(self, q, core=None, t=None):
        return (q * 2 + (self.core if core is None else core), self.t if t is None else t)

    def mate(self, shift):
        block = (self.core * self.half + self.low + shift) % self.group
        return (self.dp - self.core + block // self.half, self.t - self.low + block % self.half)

    def gather_peers(self):
        return (
            [(self.dp, self.along(d)) for d in range(1, self.n_t)]
            + [self.sibling, self.device(self.lo_q())]
            + [self.device(self.hi_q(m)) for m in range(1, self.n_hi)]
        )

    def other_core_peers(self):
        return [(self.sibling[0], self.along(d)) for d in range(1, self.n_t)]


def greet(peers):
    barrier = pltpu.get_barrier_semaphore()
    for peer in peers:
        pl.semaphore_signal(barrier, inc=1, device_id=peer, device_id_type=MESH)
    pl.semaphore_wait(barrier, len(peers))


def remote(src, dst, send, recv, device):
    return pltpu.make_async_remote_copy(
        src_ref=src, dst_ref=dst, send_sem=send, recv_sem=recv, device_id=device, device_id_type=MESH
    )


class Gather:
    @staticmethod
    def keys(n_hi, ds, here):
        found = []
        for d in ds:
            found += [] if d in here else [("z", d)]
            found += [("x", d), ("s", d)]
            for m in range(1, n_hi):
                found += [("y", m, d), ("dy", m, d), ("dx", m, d)]
        return found

    @staticmethod
    def scratch(n_dp, ds, here=(0,)):
        count = len(Gather.keys(n_dp // 4, ds, here))
        return [DMA((count,)), DMA((count,)), DMA((len(here),))]

    def __init__(self, place, sources, full, ds, sems, spread=None, by_rows=True):
        self.place, self.sources, self.full, self.ds = place, sources, full, list(ds)
        self.send, self.recv, self.own = sems
        self.index = {k: i for i, k in enumerate(Gather.keys(place.n_hi, self.ds, sources))}
        self.spread, self.by_rows = spread, by_rows
        self.ms = range(1, place.n_hi)

    def block(self, d, q, half=None):
        ref = self.full.at[self.ds.index(d), q, self.place.core]
        if half is None:
            return ref
        rows, cols = self.full.shape[-2:]
        if self.by_rows:
            return ref.at[pl.ds(half * (rows // 2), rows // 2)]
        first = cols // 2 // 128 * 128
        return ref.at[:, pl.ds(half * first, cols - first if half else first)]

    def copy(self, key):
        p, kind, d = self.place, key[0], key[-1]
        i = self.index[key]
        if kind == "z":
            src = self.sources[0] if self.spread is None else self.spread(d)
            dst, device = self.block(d, p.q), (p.dp, p.along(d))
        elif kind == "s":
            src = dst = self.full.at[self.ds.index(d), :, p.core]
            device = p.sibling
        elif kind in "xy":
            src = self.sources[d] if d in self.sources else self.block(d, p.q)
            dst = self.block(d, p.q)
            device = p.device(p.lo_q() if kind == "x" else p.hi_q(key[1]))
        elif kind == "dy":
            src = dst = self.block(d, p.lo_q(), 0)
            device = p.device(p.hi_q(key[1]))
        else:
            src = dst = self.block(d, p.hi_q(p.n_hi - key[1]), 1)
            device = p.device(p.lo_q())
        return remote(src, dst, self.send.at[i], self.recv.at[i], device)

    def own_copy(self, d):
        i = list(self.sources).index(d)
        return pltpu.make_async_copy(self.sources[d], self.block(d, self.place.q), self.own.at[i])

    def along(self, d):
        self.copy(("z", d)).start()

    def relay(self, d):
        if d in self.sources:
            self.own_copy(d).start()
        else:
            self.copy(("z", d)).wait_recv()
        self.copy(("x", d)).start()
        for m in self.ms:
            self.copy(("y", m, d)).start()

    def diag(self, d):
        self.copy(("x", d)).wait_recv()
        for m in self.ms:
            self.copy(("dy", m, d)).start()
        for m in self.ms:
            self.copy(("y", m, d)).wait_recv()
            self.copy(("dx", m, d)).start()

    def share(self, d):
        if d in self.sources:
            self.own_copy(d).wait()
        for m in self.ms:
            self.copy(("dy", m, d)).wait_recv()
            self.copy(("dx", m, d)).wait_recv()
        self.copy(("s", d)).start()

    def done(self, d):
        self.copy(("s", d)).wait_recv()

    def finish(self):
        for key in self.index:
            self.copy(key).wait_send()


def run_events(step, batches):
    for i, batch in enumerate(batches):
        if batch:

            @pl.when(step == i)
            def _():
                for event in batch:
                    event()


def cut(names, letter):
    parts = [[]]
    for name in names:
        if name[0] == letter:
            parts.append([])
        else:
            parts[-1].append(name)
    return parts


def orders(n_t, pairs, sub, group):
    if (n_t, pairs, sub, group) == (4, 2, 2, 2):
        return FRONT, MIDDLE
    near = n_t // 2
    late = list(reversed(range(near, n_t)))
    name = lambda letters, d: letters + str(d)
    front = ["G", "T", "er0", "xr0", "hr0", "or0", "A"]
    for d in range(1, n_t):
        front += [name(g, d) for g in (("ea", "oa", "xa", "ha") if d < near else ("ea", "oa"))]
    front += ["X", "H", "C"]
    every = lambda g, d: [name(g + a, d) for a in ("rds" if d else "ds")]
    for d in range(n_t):
        front += every("e", d)
    front += ["W", "g", "N"]
    for d in range(n_t):
        front += [name("R", d), name("P", d)]
    for d in range(n_t):
        front += every("o", d) + (every("x", d) + every("h", d) if d < near else [])
    for d in range(n_t):
        front += [name("V", d)] + [name("K", d * pairs + i) for i in range(pairs)]
    middle = []
    for g in "xh":
        middle += [name(g + "r", late[0])] + [name(g + "a", d) for d in late[1:]]
    middle += ["I"]
    for i in range(n_t * sub):
        middle += [name("F", i)]
        if i == 0:
            for d in late:
                for g in "xh":
                    middle += every(g, d)[1 if d == late[0] else 0 :]
        if (i + 1) % sub == 0 and near <= (i + 1) // sub < n_t:
            middle += [name("B", late[(i + 1) // sub - near])]
    return front, middle


FRONT = (
    "G", "ea1", "hr0", "er0", "xr0", "T", "A", "ed0", "ea2", "hd0", "es0", "er1", "W", "ed1", "xd0", "ea3",
    "oa3", "N", "es1", "or0", "oa2", "er2", "R0", "g", "xa1", "P0", "ha1", "R1", "er3", "V0", "od0", "K0",
    "oa1", "xs0", "ed2", "ed3", "or2", "P1", "xr1", "K1", "es2", "hr1", "C", "V1", "K2", "hs0", "R2", "P2",
    "or1", "es3", "K3", "hd1", "od2", "R3", "or3", "X", "od1", "P3", "V2", "K4", "V3", "os0", "hs1", "od3",
    "os2", "xd1", "K5", "os1", "H", "os3", "K6", "xs1", "K7",
)
MIDDLE = (
    "xa2", "xr3", "I", "hr3", "F0", "xd3", "xr2", "ha2", "F1", "hd3", "F2", "xd2", "xs3", "hs3", "hr2", "F3",
    "B3", "xs2", "hd2", "F4", "hs2", "F5", "B2", "F6", "F7",
)
STEPS = {"a": Gather.along, "r": Gather.relay, "d": Gather.diag, "s": Gather.share}


def move(place, source, target, sems, begin, rows=None):
    if rows is not None:
        source, target = source.at[rows], target.at[rows]

    @pl.when(place.stays)
    def _():
        here = pltpu.make_async_copy(source, target, sems[2])
        here.start() if begin else here.wait()

    @pl.when(jnp.logical_not(place.stays))
    def _():
        there = remote(source, target, sems[0], sems[1], place.partner)
        there.start() if begin else there.wait()


def head_masks(shape):
    lane = lax.broadcasted_iota(jnp.int32, shape, 1)
    return lane < HEAD_DIM, lane >= HEAD_DIM


def ones_lanes(rows, count):
    lane = lax.broadcasted_iota(jnp.int32, (rows, PAIR), 1)
    return jnp.where(lane < count, 1.0, 0.0).astype(BF)


def attend(queries, keys, values, o_ref, lse_ref):
    rows, length = queries.shape[0], keys.shape[0]
    values = jnp.concatenate([values, ones_lanes(length, 1)], axis=1)
    zero = jnp.zeros_like(queries)
    outs, sums = [], []
    both = [dot(jnp.where(mask, queries, zero), keys, 1, 1) for mask in head_masks(queries.shape)]
    for scores in both:
        top = jnp.max(scores, axis=1, keepdims=True)
        probs = jnp.exp2(scores - top).astype(BF)
        mixed = dot(probs, values, 1, 0)
        total = mixed[:, PAIR : PAIR + 1]
        outs.append(mixed[:, :PAIR] / total)
        sums.append(top + jnp.log2(total))
    first, _ = head_masks((rows, PAIR))
    o_ref[...] = jnp.where(first, outs[0], outs[1]).astype(BF)
    lse_ref[...] = jnp.where(first, sums[0], sums[1])


def front_kernel(
    n_dp, n_t, cap,
    choice_ref, count_ref, gain_ref, ed_tab, ou_tab, xd_tab, su_tab, eu_tab, od_tab, xu_tab, sd_tab,
    tokens_ref, cot_ref, w_ref, wo_ref, we_ref, ws_ref,
    o_ref, lse_ref, inner_t_ref, thin_out, rep_out,
    q_out, k_out, v_out, k_far_out, v_far_out, normed_out, tok_out, cot_out, w_full, wo_full, we_full, ws_full,
    we_land, ws_land,
    q, k, v, k_far, v_far, tok, cot, normed, thin, rep, thin_send, stage, inner,
    tok_sems, cot_sems, thin_sends, thin_recvs, rep_sems, stage_sems, kv_sends, kv_recvs, keep_sems, kept_sems,
    land_sems, go_sem, *sems,
):
    p = Place(n_dp, n_t, cap)
    step, steps = pl.program_id(0), pl.num_programs(0)
    cols, hid = od_tab.shape[-1], xu_tab.shape[-1]
    pairs = cols // PAIR
    depth = w_ref.shape[0] // 3
    early = list(range(n_t // 2))
    entry = Gather(p, {0: w_ref}, w_full, range(n_t), sems[0:3])
    out_g = Gather(p, {0: wo_ref}, wo_full, range(n_t), sems[3:6])
    exp_g = Gather(p, {0: we_ref}, we_full, early, sems[6:9])
    shr_g = Gather(p, {0: ws_ref}, ws_full, early, sems[9:12])
    both = (exp_g, shr_g)
    tok_three = [tok_sems.at[i] for i in range(3)]
    cot_three = [cot_sems.at[i] for i in range(3)]

    def thin_targets():
        for s in range(cap):
            for low in range(p.half):
                to = s * p.group + p.core * p.half + low
                for core in range(2):
                    i = (s * p.half + low) * 2 + core
                    elsewhere = jnp.logical_or(core != p.core, to != p.t)
                    yield s, to, core, i, elsewhere

    def send_thin(near):
        for s, to, core, i, elsewhere in thin_targets():
            d = (to + n_t - p.t) % n_t

            @pl.when(jnp.logical_and(elsewhere, (to == p.t) == near))
            def _():
                remote(
                    thin_send.at[s], thin.at[d], thin_sends.at[i], thin_recvs.at[d], (p.dp - p.core + core, to)
                ).start()

    def send_adapters():
        for s in range(cap):
            a = choice_ref[s]
            for i in range(3):
                thin_send[s, :, i * cols : (i + 1) * cols] = eu_tab[a, i]
            thin_send[s, :, 3 * cols : 4 * cols] = od_tab[a]
            thin_send[s, :, 4 * cols : 4 * cols + hid] = xu_tab[a]
            thin_send[s, :, 4 * cols + hid :] = sd_tab[a]
        send_thin(True)

        @pl.when(p.stays)
        def _():
            a = choice_ref[p.slot]
            for i, table in enumerate((ed_tab, ou_tab, xd_tab, su_tab)):
                rep[i * RANK : (i + 1) * RANK] = table[a]
            row = lax.broadcasted_iota(jnp.int32, (RANK, rep.shape[1]), 0)
            alive = jnp.where(p.slot < count_ref[0], 1.0, 0.0)
            rep[4 * RANK :] = jnp.where(row < RANK // 2, alive, a.astype(F32)).astype(BF)
            remote(rep, rep, rep_sems.at[0], rep_sems.at[1], p.sibling).start()
            thin[0] = thin_send[p.slot]

    def take_near():
        @pl.when(jnp.logical_not(p.stays))
        def _():
            remote(rep, rep, rep_sems.at[0], rep_sems.at[1], p.sibling).wait_recv()
            remote(thin_send.at[0], thin.at[0], thin_sends.at[0], thin_recvs.at[0], p.sibling).wait_recv()

        rep_out[...] = rep[...]
        thin_out[0] = thin[0]

    def take_thin(d):
        remote(thin_send.at[0], thin.at[d], thin_sends.at[0], thin_recvs.at[d], p.sibling).wait_recv()
        thin_out[d] = thin[d]

    def load(d):
        return pltpu.make_async_copy(w_full.at[d], stage.at[d % 2], stage_sems.at[d % 2])

    def kept():
        return [pltpu.make_async_copy(tok, tok_out, keep_sems.at[0]), pltpu.make_async_copy(normed, normed_out, keep_sems.at[1])]

    def first_norm():
        hat, _ = norm_parts(tok[...].astype(F32))
        value = (hat * gain_ref[...]).astype(BF)
        normed[...] = value
        down = rep[:RANK]
        inner[...] = dot(value, down, 1, 1).astype(BF)
        inner_t_ref[...] = dot(down, value, 1, 1).astype(BF)
        for copy in kept():
            copy.start()

    def far_copy(d, which, m):
        source, target = ((k, k_far), (v, v_far))[which]
        device = p.mate(m)
        there = (d + device[1] + n_t - p.t) % n_t
        return remote(
            source.at[pl.ds(d * pairs, pairs)], target.at[m - 1, pl.ds(there * pairs, pairs)],
            kv_sends.at[d, which, m - 1], kv_recvs.at[there, which, m - 1], device,
        )

    def far_arrival(d, which, m):
        source, target = ((k, k_far), (v, v_far))[which]
        return remote(
            source.at[pl.ds(d * pairs, pairs)], target.at[m - 1, pl.ds(d * pairs, pairs)],
            kv_sends.at[d, which, m - 1], kv_recvs.at[d, which, m - 1], p.mate(m),
        )

    def project(d):
        if d:
            take_thin(d)
        load(d).wait()
        for which, out in ((1, k), (2, v), (0, q)):
            weights = stage[d % 2, :, :, which * depth : (which + 1) * depth].reshape(n_dp * depth, cols)
            part = dot(normed[...], weights, 1, 0)
            part = part + dot(inner[...], thin[d, :, which * cols : (which + 1) * cols], 1, 0)
            if which == 0:
                part = part * (HEAD_DIM**-0.5 * LOG2E)
            part = part.astype(BF)
            for i in range(pairs):
                out[d * pairs + i] = part[:, i * PAIR : (i + 1) * PAIR]
            if which:
                for m in range(1, p.group):
                    far_copy(d, which - 1, m).start()

    def copies_out(d):
        at = pl.ds(d * pairs, pairs)
        found = [(a.at[at], b.at[at]) for a, b in ((q, q_out), (k, k_out), (v, v_out))]
        for a, b in ((k_far, k_far_out), (v_far, v_far_out)):
            found += [(a.at[m, at], b.at[m, at]) for m in range(p.group - 1)]
        return [pltpu.make_async_copy(a, b, kept_sems.at[d, i]) for i, (a, b) in enumerate(found)]

    def arrive(d):
        for m in range(1, p.group):
            far_arrival(d, 0, m).wait_recv()
            far_arrival(d, 1, m).wait_recv()
        for copy in copies_out(d):
            copy.start()

    def land(i):
        source, target = ((we_ref, we_land), (ws_ref, ws_land))[i]
        return remote(source, target, land_sems.at[0, i], land_sems.at[1, i], (p.dp, p.along(n_t - 1)))

    def ready(d):
        entry.done(d)
        load(d).start()

    def go():
        @pl.when(jnp.logical_not(p.stays))
        def _():
            pl.semaphore_signal(go_sem, inc=1, device_id=p.sibling, device_id_type=MESH)

        @pl.when(p.stays)
        def _():
            pl.semaphore_wait(go_sem, 1)

    def arrived():
        move(p, tokens_ref, tok, tok_three, False)
        send_thin(False)

    def norm():
        take_near()
        first_norm()

    def opened():
        greet(p.gather_peers() + p.other_core_peers())

    gathers = {"e": entry, "x": exp_g, "h": shr_g, "o": out_g}
    plain = {
        "G": opened, "g": go, "W": arrived, "N": norm, "A": send_adapters,
        "T": lambda: move(p, tokens_ref, tok, tok_three, True), "C": lambda: move(p, cot_ref, cot, cot_three, True),
        "X": lambda: land(0).start(), "H": lambda: land(1).start(),
    }
    counted = {"R": ready, "P": project, "V": arrive}

    def event(name):
        if len(name) == 1:
            return plain[name]
        if len(name) == 2:
            return lambda: counted[name[0]](int(name[1]))
        return lambda: STEPS[name[1]](gathers[name[0]], int(name[2]))

    names = orders(n_t, pairs, max(1, hid // 512), p.group)[0]
    batches = [[event(name) for name in part] for part in cut(names, "K")]
    closing = batches.pop()
    run_events(step, batches)
    keys = jnp.concatenate([k[step]] + [k_far[m, step] for m in range(p.group - 1)], axis=0)
    values = jnp.concatenate([v[step]] + [v_far[m, step] for m in range(p.group - 1)], axis=0)
    attend(q[step], keys, values, o_ref, lse_ref)

    @pl.when(step == steps - 1)
    def _():
        for call in closing:
            call()
        for g in (exp_g, shr_g, out_g):
            for d in g.ds:
                g.done(d)
        for g in (entry, exp_g, shr_g, out_g):
            g.finish()
        for i in range(2):
            land(i).wait()
        move(p, cot_ref, cot, cot_three, False)
        keep_cot = pltpu.make_async_copy(cot, cot_out, keep_sems.at[2])
        keep_cot.start()

        @pl.when(p.stays)
        def _():
            remote(rep, rep, rep_sems.at[0], rep_sems.at[1], p.sibling).wait_send()

        for s, to, core, i, elsewhere in thin_targets():

            @pl.when(elsewhere)
            def _():
                remote(thin_send.at[s], thin.at[0], thin_sends.at[i], thin_recvs.at[0], p.sibling).wait_send()

        for copy in [keep_cot, *kept()]:
            copy.wait()
        for d in range(n_t):
            for m in range(1, p.group):
                far_copy(d, 0, m).wait_send()
                far_copy(d, 1, m).wait_send()
            for copy in copies_out(d):
                copy.wait()


def front_part(cap, choice, count, gain, rep_tables, thin_tables, tokens, cot, w, wo, we, ws):
    n_dp, n_t = lax.axis_size("dp"), lax.axis_size("tensor")
    rows, width = tokens.shape
    cols = wo.shape[-1]
    others = n_t // cap - 1
    count_pairs = width // PAIR
    early = n_t // 2
    thin_width = 4 * cols + 2 * we.shape[-1]
    shape, vmem = jax.ShapeDtypeStruct, pltpu.VMEM
    whole = lambda *s: pl.BlockSpec(s, lambda h: (0,) * len(s))
    pair = pl.BlockSpec((None, rows, PAIR), lambda h: (h, 0, 0))
    full = lambda n, a: shape((n, n_dp // 2, 2, *a.shape), BF)
    heads, far = (count_pairs, rows, PAIR), (others, count_pairs, rows, PAIR)
    small = [(RANK, rows), (n_t, RANK, thin_width), (5 * RANK, width)]
    return pl.pallas_call(
        functools.partial(front_kernel, n_dp, n_t, cap),
        grid=(count_pairs,),
        in_specs=[IN_SMEM, IN_SMEM] + [whole(*a.shape) for a in (gain, *rep_tables, *thin_tables)]
        + [ANY] * 2 + [whole(*a.shape) for a in (w, wo, we, ws)],
        out_specs=[pair, pair] + [whole(*s) for s in small] + [ANY] * 14,
        out_shape=[shape(heads, BF), shape(heads, F32)] + [shape(s, BF) for s in small]
        + [shape(heads, BF)] * 3 + [shape(far, BF)] * 2 + [shape((rows, width), BF)] * 3
        + [full(n_t, w), full(n_t, wo), full(early, we), full(early, ws), shape(we.shape, BF), shape(ws.shape, BF)],
        scratch_shapes=[
            vmem(heads, BF), vmem(heads, BF), vmem(heads, BF), vmem(far, BF), vmem(far, BF),
            vmem((rows, width), BF), vmem((rows, width), BF), vmem((rows, width), BF), vmem(small[1], BF), vmem(small[2], BF),
            vmem((cap, RANK, thin_width), BF),
            vmem((2, n_dp // 2, 2, *w.shape), BF), vmem((rows, RANK), BF),
            DMA((3,)), DMA((3,)), DMA((n_t,)), DMA((n_t,)), DMA((2,)), DMA((2,)),
            DMA((n_t, 2, others)), DMA((n_t, 2, others)), DMA((3,)), DMA((n_t, 3 + 2 * others)), DMA((2, 2)),
            pltpu.SemaphoreType.REGULAR,
            *Gather.scratch(n_dp, range(n_t)), *Gather.scratch(n_dp, range(n_t)),
            *Gather.scratch(n_dp, range(early)), *Gather.scratch(n_dp, range(early)),
        ],
        compiler_params=params(collective_id=0, has_side_effects=True),
        name="front_part",
    )(choice, count, gain, *rep_tables, *thin_tables, tokens, cot, w, wo, we, ws)


def split_lanes(column):
    column = -column
    high = column.astype(BF)
    rest = column - high.astype(F32)
    mid = rest.astype(BF)
    low = (rest - mid.astype(F32)).astype(BF)
    lane = lax.broadcasted_iota(jnp.int32, (column.shape[0], PAIR), 1)
    zero = jnp.zeros((column.shape[0], PAIR), BF)
    return jnp.where(lane == 0, high, jnp.where(lane == 1, mid, jnp.where(lane == 2, low, zero)))


def back_kernel(
    n_dp, n_t, cap, tiles,
    q_ref, k_ref, k_far, v_ref, v_far, o_ref, lse_ref, do_ref, gain_ref, rep_ref, thin_ref, inner_t_ref, grads_ref,
    mixed_ref, w_ref, mgrad_ref, tok_ref, normed_ref,
    mixed_out, mid_full, tgrad_out, end_full,
    grad, send, far, mixed, weights, mgrad, tok, normed, back_low, tgrad, end, sends, recvs, swap, swaps, load_sems,
    *sems,
):
    p = Place(n_dp, n_t, cap)
    step, steps = pl.program_id(0), pl.num_programs(0)
    rows = q_ref.shape[0]
    pairs = grad.shape[1] // n_t
    cols = w_ref.shape[-1]
    depth = w_ref.shape[-2] // 3
    width = tok_ref.shape[1]
    mid_g = Gather(
        p, {0: grads_ref.at[0]}, mid_full, range(n_t), sems[0:3],
        spread=lambda d: grads_ref.at[n_t - d], by_rows=False,
    )
    end_g = Gather(
        p, {0: end.at[0]}, end_full, range(n_t), sems[3:6], spread=lambda d: end.at[n_t - d], by_rows=False
    )
    swap_sems = [swap.at[i] for i in range(3)]
    loads = [
        pltpu.make_async_copy(src, dst, load_sems.at[i])
        for i, (src, dst) in enumerate(((w_ref, weights), (normed_ref, normed), (tok_ref, tok), (mgrad_ref, mgrad)))
    ]
    relay, diag, share = ((lambda d, f=f: lambda: f(d)) for f in (mid_g.relay, mid_g.diag, mid_g.share))
    start_swap = lambda: move(p, mixed_ref, mixed, swap_sems, True)
    start_loads = lambda: [copy.start() for copy in loads]

    def opening():
        greet(p.gather_peers() + p.other_core_peers())
        mid_g.relay(0)
        for d in range(1, n_t):
            mid_g.along(d)

    if n_t == 4:
        table = {
            0: [opening], 1: [diag(0), relay(1)], 2: [share(0), diag(1), relay(2), start_swap],
            3: [share(1), diag(2), relay(3)], 4: [share(2), diag(3), start_loads], 5: [share(3)],
        }
    else:
        table = {0: [opening, start_swap, start_loads, diag(0), share(0)]}
        for d in range(1, n_t):
            table[0] += [relay(d), diag(d), share(d)]
    run_events(step, [table.get(i, []) for i in range(max(table) + 1)])

    with_far = lambda near, far: jnp.concatenate([near[...]] + [far[m] for m in range(p.group - 1)], axis=0)
    keys = with_far(k_ref, k_far)
    length = keys.shape[0]
    ones = ones_lanes(length, 3)
    keys_more = jnp.concatenate([keys, ones], axis=1)
    values_more = jnp.concatenate([with_far(v_ref, v_far), ones], axis=1)
    queries, grad_out = q_ref[...], do_ref[...]
    zero = jnp.zeros_like(queries)
    product = grad_out.astype(F32) * o_ref[...].astype(F32)
    d_queries, both = [], [[], [], [], []]
    for head, mask in enumerate(head_masks(queries.shape)):
        query = jnp.where(mask, queries, zero)
        grad_head = jnp.where(mask, grad_out, zero)
        lse = lse_ref[:, head * HEAD_DIM : head * HEAD_DIM + 1]
        delta = jnp.sum(jnp.where(mask, product, 0.0), axis=1, keepdims=True)
        probs = jnp.exp2(dot(jnp.concatenate([query, split_lanes(lse)], axis=1), keys_more, 1, 1))
        slope = dot(jnp.concatenate([grad_head, split_lanes(delta)], axis=1), values_more, 1, 1)
        score_grad = (probs * slope).astype(BF)
        d_queries.append(dot(score_grad, keys, 1, 0))
        for kept, one in zip(both, (grad_head, probs.astype(BF), query, score_grad)):
            kept.append(one)
    grad_heads, probs, query, score_grad = [jnp.concatenate(kept, axis=0) for kept in both]
    d_values = dot(grad_heads, probs, 0, 0)
    d_keys = dot(query, score_grad, 0, 0)
    first, _ = head_masks((rows, PAIR))
    grad[0, step] = (jnp.where(first, d_queries[0], d_queries[1]) * HEAD_DIM**-0.5).astype(BF)
    d_keys = (d_keys * LN2).T.astype(BF)
    d_values = d_values.T.astype(BF)
    grad[1, step] = d_keys[:rows]
    grad[2, step] = d_values[:rows]

    def far_copy(i, m, h):
        device = p.mate(p.group - m)
        there = (h // pairs + device[1] + n_t - p.t) % n_t * pairs + h % pairs
        return remote(
            send.at[i, m - 1, h], far.at[i, m - 1, there], sends.at[i, m - 1, h], recvs.at[i, m - 1, there], device
        )

    for m in range(1, p.group):
        send[0, m - 1, step] = d_keys[m * rows : (m + 1) * rows]
        send[1, m - 1, step] = d_values[m * rows : (m + 1) * rows]
        far_copy(0, m, step).start()
        far_copy(1, m, step).start()

    @pl.when(step == steps - 1)
    def _():
        move(p, mixed_ref, mixed, swap_sems, False)
        keep = pltpu.make_async_copy(mixed, mixed_out, swap.at[3])
        keep.start()
        for i in range(2):
            for m in range(1, p.group):
                for h in range(n_t * pairs):
                    remote(
                        send.at[i, m - 1, h], far.at[i, m - 1, h], sends.at[i, m - 1, h], recvs.at[i, m - 1, h], p.sibling
                    ).wait_recv()
            for h in range(n_t * pairs):
                total = grad[1 + i, h].astype(F32)
                for m in range(p.group - 1):
                    total = total + far[i, m, h].astype(F32)
                grad[1 + i, h] = total.astype(BF)
        columns = lambda which, d, rows: jnp.concatenate(
            [grad[which, d * pairs + i, rows] for i in range(pairs)], axis=1
        )
        back = 0.0
        for d in range(n_t):
            for which in range(3):
                up = thin_ref[d, :, which * cols : (which + 1) * cols]
                back = back + dot(columns(which, d, slice(None)), up, 1, 1)
        back_low[...] = back.astype(BF)
        loads[1].wait()
        down_grad = dot(back_low[...], normed[...], 0, 0).astype(BF)
        for d in range(n_t):
            for which in range(3):
                end[d, :, which * cols : (which + 1) * cols] = dot(
                    inner_t_ref[...], columns(which, d, slice(None)), 1, 0
                ).astype(BF)
            end[d, :, 3 * cols :] = down_grad
        end_g.relay(0)
        for d in range(1, n_t):
            end_g.along(d)
        for copy in (loads[0], *loads[2:]):
            copy.wait()

        def tile(n):
            start, count = tiles[n]
            rows = pl.ds(start, count)
            total = dot(back_low[rows], rep_ref[:RANK], 1, 0)
            for d in range(n_t):
                for which in range(3):
                    piece = weights[d, :, :, which * depth : (which + 1) * depth].reshape(width, cols)
                    total = total + dot(columns(which, d, rows), piece, 1, 1)
            hat, scale = norm_parts(tok[rows].astype(F32))
            tgrad[rows] = (mgrad[rows] + norm_back(hat, scale, gain_ref[...], total)).astype(BF)
            move(p, tgrad, tgrad_out, [swaps.at[n, i] for i in range(3)], True, rows)

        for n in range(len(tiles)):
            tile(n)
            if n == 0:
                end_g.diag(0)
                end_g.relay(1)
            if n == min(1, len(tiles) - 1):
                for d in range(2, n_t):
                    end_g.relay(d)
                end_g.share(0)
                end_g.diag(1)
        for d in range(2, n_t):
            end_g.diag(d)
            end_g.share(d - 1)
        end_g.share(n_t - 1)
        for d in range(n_t):
            mid_g.done(d)
            end_g.done(d)
        mid_g.finish()
        end_g.finish()
        for n, (start, count) in enumerate(tiles):
            move(p, tgrad, tgrad_out, [swaps.at[n, i] for i in range(3)], False, pl.ds(start, count))

        @pl.loop(0, steps)
        def _(h):
            for m in range(1, p.group):
                for i in range(2):
                    far_copy(i, m, h).wait_send()

        keep.wait()


def back_part(cap, q, k, k_far, v, v_far, o, lse, do, gain, rep, thin, inner_t, grads, mixed, w_full, mgrad, tok, normed):
    n_dp, n_t = lax.axis_size("dp"), lax.axis_size("tensor")
    heads, rows, _ = q.shape
    width, cols = tok.shape[1], w_full.shape[-1]
    others = k_far.shape[0]
    pair = pl.BlockSpec((None, rows, PAIR), lambda h: (h, 0, 0))
    far = pl.BlockSpec((others, None, rows, PAIR), lambda h: (0, h, 0, 0))
    whole = lambda a: pl.BlockSpec(a.shape, lambda h: (0,) * len(a.shape))
    shape, vmem = jax.ShapeDtypeStruct, pltpu.VMEM
    count = (2, others, heads)
    number = 3 if rows % 16 == 0 else 1
    size = rows // number // 16 * 16 if number > 1 else rows
    tiles = [(0, rows - size * (number - 1))]
    tiles += [(tiles[0][1] + size * i, size) for i in range(number - 1)]
    end_width = 3 * cols + width
    full = lambda n: shape((n_t, n_dp // 2, 2, RANK, n), BF)
    return pl.pallas_call(
        functools.partial(back_kernel, n_dp, n_t, cap, tiles),
        grid=(heads,),
        in_specs=[pair, pair, far, pair, far, pair, pair, pair]
        + [whole(a) for a in (gain, rep, thin, inner_t, grads)] + [ANY] * 5,
        out_specs=[ANY] * 4,
        out_shape=[shape(mixed.shape, BF), full(grads.shape[-1]), shape(tok.shape, BF), full(end_width)],
        scratch_shapes=[
            vmem((3, heads, rows, PAIR), BF), vmem((2, *k_far.shape), BF), vmem((2, *k_far.shape), BF),
            vmem(mixed.shape, BF), vmem(w_full.shape, BF), vmem(mgrad.shape, F32), vmem(tok.shape, BF),
            vmem(tok.shape, BF), vmem((rows, RANK), BF), vmem(tok.shape, BF), vmem((n_t, RANK, end_width), BF),
            DMA(count), DMA(count), DMA((4,)), DMA((len(tiles), 3)), DMA((4,)),
            *Gather.scratch(n_dp, range(n_t)), *Gather.scratch(n_dp, range(n_t)),
        ],
        compiler_params=params(collective_id=1, has_side_effects=True),
        name="back_part",
    )(q, k, k_far, v, v_far, o, lse, do, gain, rep, thin, inner_t, grads, mixed, w_full, mgrad, tok, normed)


def gelu_parts(hidden):
    share = 0.5 * (1.0 + lax.erf(hidden * 0.7071067811865476))
    density = jnp.exp(-0.5 * hidden * hidden) * 0.3989422804014327
    return hidden * share, share + hidden * density


def middle_kernel(
    n_dp, n_t, cap, sub,
    x_ref, att_ref, cot_ref, gain_ref, rep_ref, thin_ref, wo_ref, we_near, ws_near, we_land, ws_land, we_ref, ws_ref,
    mixed_ref, mgrad_ref, agrad_ref, grads_ref, we_full, ws_full,
    middle_ref, second_ref, dy_ref, acc2_ref, acc3_ref, einner_ref, einner_t_ref, sback_ref, sback_t_ref,
    sinner_ref, eback_ref, oinner_ref, we_buf, ws_buf, buf_sems, *sems,
):
    p = Place(n_dp, n_t, cap)
    step, steps = pl.program_id(0), pl.num_programs(0)
    cols = wo_ref.shape[-1]
    width = x_ref.shape[1]
    hid = we_ref.shape[-1]
    size = hid // sub
    near = n_t // 2
    late = list(reversed(range(near, n_t)))
    exp_g = Gather(p, {n_t - 1: we_land}, we_full, late, sems[0:3], spread=lambda d: we_ref)
    shr_g = Gather(p, {n_t - 1: ws_land}, ws_full, late, sems[3:6], spread=lambda d: ws_ref)
    pairs = cols // PAIR
    both = (exp_g, shr_g)
    down_e, up_o, up_s = rep_ref[2 * RANK : 3 * RANK], rep_ref[RANK : 2 * RANK], rep_ref[3 * RANK : 4 * RANK]
    alive = rep_ref[4 * RANK : 4 * RANK + 1, 0:1].astype(F32)
    at_od, at_eu = 3 * width, 3 * width + cols
    at_sd, at_id = at_eu + hid, at_eu + 2 * hid

    def load(i):
        index, part = i // sub, i % sub
        at = pl.ds(part * size, size)
        pair = (we_near, ws_near) if index < near else (we_full, ws_full)
        index = index if index < near else index - near
        return [
            pltpu.make_async_copy(src.at[index, :, :, :, at], buf.at[i % 3], buf_sems.at[i % 3, j])
            for j, (src, buf) in enumerate(zip(pair, (we_buf, ws_buf)))
        ]

    gathers = {"x": exp_g, "h": shr_g}

    def bring(d):
        exp_g.done(d)
        shr_g.done(d)
        for i in range(sub):
            for copy in load((near + late.index(d)) * sub + i):
                copy.start()

    def event(name):
        if len(name) == 2:
            return lambda: bring(int(name[1]))
        return lambda: STEPS[name[1]](gathers[name[0]], int(name[2]))

    names = orders(n_t, pairs, sub, p.group)[1]
    begun = names.index("I")
    start = [event(name) for name in names[:begun]]
    opening, *after = [[event(name) for name in part] for part in cut(names[begun + 1 :], "F")]
    columns = lambda d: jnp.concatenate([att_ref[d * pairs + i] for i in range(pairs)], axis=1)

    @pl.when(step == 0)
    def _():
        greet(p.gather_peers())
        for call in start:
            call()
        for i in range(2):
            for copy in load(i):
                copy.start()
        branch, inner = 0.0, 0.0
        for d in range(n_t):
            att = columns(d)
            branch = branch + dot(att, wo_ref[d].reshape(width, cols), 1, 1)
            inner = inner + dot(att, thin_ref[d, :, 3 * cols : 4 * cols], 1, 1)
        inner = inner.astype(BF)
        oinner_ref[...] = inner
        middle = x_ref[...].astype(F32) + (branch + dot(inner, up_o, 1, 0))
        middle_ref[...] = middle
        hat, _ = norm_parts(middle)
        second = (hat * gain_ref[...]).astype(BF)
        second_ref[...] = second
        dy = (cot_ref[...].astype(F32) * alive).astype(BF)
        dy_ref[...] = dy
        einner_ref[...] = dot(second, down_e, 1, 1).astype(BF)
        einner_t_ref[...] = dot(down_e, second, 1, 1).astype(BF)
        sback_ref[...] = dot(dy, up_s, 1, 1).astype(BF)
        sback_t_ref[...] = dot(up_s, dy, 1, 1).astype(BF)
        acc2_ref[...] = jnp.zeros_like(acc2_ref)
        acc3_ref[...] = jnp.zeros_like(acc3_ref)
        sinner_ref[...] = jnp.zeros_like(sinner_ref)
        eback_ref[...] = jnp.zeros_like(eback_ref)

    run_events(step, [opening])
    for i in range(n_t * sub):

        @pl.when(step == i)
        def _():
            for copy in load(i):
                copy.wait()
            if i + 2 < near * sub:
                for copy in load(i + 2):
                    copy.start()

    buf = step % 3
    d, part = step // sub, step % sub
    d = jnp.where(d < near, d, n_t - 1 + near - d)
    we, ws = we_buf[buf].reshape(width, size), ws_buf[buf].reshape(width, size)
    at = pl.multiple_of(part * size, size)
    e_up = thin_ref[d, :, pl.ds(4 * cols + at, size)]
    s_down = thin_ref[d, :, pl.ds(4 * cols + hid + at, size)]
    hidden = dot(second_ref[...], we, 1, 0) + dot(einner_ref[...], e_up, 1, 0)
    value, slope = gelu_parts(hidden)
    act = value.astype(BF)
    acc2_ref[...] += dot(act, ws, 1, 1)
    sinner_ref[...] += dot(act, s_down, 1, 1)
    act_grad = dot(dy_ref[...], ws, 1, 0) + dot(sback_ref[...], s_down, 1, 0)
    hid_grad = (act_grad * slope).astype(BF)
    acc3_ref[...] += dot(hid_grad, we, 1, 1)
    eback_ref[...] += dot(hid_grad, e_up, 1, 1)
    grads_ref[d, :, pl.ds(at_eu + at, size)] = dot(einner_t_ref[...], hid_grad, 1, 0).astype(BF)
    grads_ref[d, :, pl.ds(at_sd + at, size)] = dot(sback_t_ref[...], act, 1, 0).astype(BF)

    run_events(step, after)
    @pl.when(step == steps - 1)
    def _():
        s_inner, e_back = sinner_ref[...].astype(BF), eback_ref[...].astype(BF)
        middle = middle_ref[...]
        mixed_ref[...] = (alive * (middle + (acc2_ref[...] + dot(s_inner, up_s, 1, 0)))).astype(BF)
        shrink_up = dot(s_inner, dy_ref[...], 0, 0).astype(BF)
        expand_down = dot(e_back, second_ref[...], 0, 0).astype(BF)
        second_grad = acc3_ref[...] + dot(e_back, down_e, 1, 0)
        hat, scale = norm_parts(middle)
        mgrad = cot_ref[...].astype(F32) * alive + norm_back(hat, scale, gain_ref[...], second_grad)
        mgrad_ref[...] = mgrad
        low = mgrad.astype(BF)
        o_back = dot(low, up_o, 1, 1).astype(BF)
        output_up = dot(oinner_ref[...], low, 0, 0).astype(BF)
        for d in range(n_t):
            agrad = dot(low, wo_ref[d].reshape(width, cols), 1, 0)
            agrad = (agrad + dot(o_back, thin_ref[d, :, 3 * cols : 4 * cols], 1, 0)).astype(BF)
            for i in range(pairs):
                agrad_ref[d * pairs + i] = agrad[:, i * PAIR : (i + 1) * PAIR]
            grads_ref[d, :, :width] = expand_down
            grads_ref[d, :, width : 2 * width] = shrink_up
            grads_ref[d, :, 2 * width : 3 * width] = output_up
            grads_ref[d, :, at_od : at_od + cols] = dot(o_back, columns(d), 0, 0).astype(BF)
            grads_ref[d, :, at_id:] = rep_ref[4 * RANK :, : grads_ref.shape[2] - at_id]
        for g in both:
            g.finish()


ID_LANES = 128


def middle_both_ways(cap, x, att, cot, gain, rep, thin, wo_full, we_near, ws_near, we_land, ws_land, we, ws):
    n_dp, n_t = lax.axis_size("dp"), lax.axis_size("tensor")
    rows, width = x.shape
    depth, hid = we.shape
    cols = wo_full.shape[-1]
    sub = max(1, hid // 512)
    size = hid // sub
    late = list(reversed(range(n_t // 2, n_t)))
    grad_width = 3 * width + cols + 2 * hid + ID_LANES
    whole = lambda a: pl.BlockSpec(a.shape, lambda i: (0,) * len(a.shape))
    shape = jax.ShapeDtypeStruct
    full = shape((len(late), n_dp // 2, 2, depth, hid), BF)
    outs = [
        shape((rows, width), BF), shape((rows, width), F32), shape(att.shape, BF),
        shape((n_t, RANK, grad_width), BF),
    ]
    vmem = pltpu.VMEM
    return pl.pallas_call(
        functools.partial(middle_kernel, n_dp, n_t, cap, sub),
        grid=(n_t * sub,),
        in_specs=[whole(a) for a in (x, att, cot, gain, rep, thin, wo_full)]
        + [ANY] * 2 + [whole(we_land), whole(ws_land)] + [ANY] * 2,
        out_specs=[whole(a) for a in outs] + [ANY] * 2,
        out_shape=outs + [full, full],
        scratch_shapes=[
            vmem((rows, width), F32), vmem((rows, width), BF), vmem((rows, width), BF),
            vmem((rows, width), F32), vmem((rows, width), F32),
            vmem((rows, RANK), BF), vmem((RANK, rows), BF), vmem((rows, RANK), BF), vmem((RANK, rows), BF),
            vmem((rows, RANK), F32), vmem((rows, RANK), F32), vmem((rows, RANK), BF),
            vmem((3, n_dp // 2, 2, depth, size), BF), vmem((3, n_dp // 2, 2, depth, size), BF), DMA((3, 2)),
            *Gather.scratch(n_dp, late, late[:1]), *Gather.scratch(n_dp, late, late[:1]),
        ],
        compiler_params=params(collective_id=2, has_side_effects=True),
        name="middle_both_ways",
    )(x, att, cot, gain, rep, thin, wo_full, we_near, ws_near, we_land, ws_land, we, ws)


def sum_kernel(
    width, cols, hid, mid_ref, end_ref, entry_down, entry_up, output_down, output_up, expand_down, expand_up,
    shrink_down, shrink_up,
):
    outs = (entry_down, entry_up, output_down, output_up, expand_down, expand_up, shrink_down, shrink_up)

    @pl.when(pl.program_id(0) == 0)
    def _():
        for out in outs:
            out[...] = jnp.zeros_like(out)

    sources = range(mid_ref.shape[0])
    at_id = 3 * width + cols + 2 * hid
    chosen = [jnp.max(mid_ref[i, RANK // 2 :, at_id : at_id + 128].astype(F32)).astype(jnp.int32) for i in sources]
    for i in sources:
        a = chosen[i]
        take = lambda ref, at, size: ref[i, :, at : at + size].astype(F32)
        expand_down[a] += take(mid_ref, 0, width)
        shrink_up[a] += take(mid_ref, width, width)
        output_up[a] += take(mid_ref, 2 * width, width)
        output_down[a] += take(mid_ref, 3 * width, cols)
        expand_up[a] += take(mid_ref, 3 * width + cols, hid)
        shrink_down[a] += take(mid_ref, 3 * width + cols + hid, hid)
        for which in range(3):
            entry_up[a, which] += take(end_ref, which * cols, cols)
        entry_down[a] += take(end_ref, 3 * cols, width)


def sum_gradients(adapters, cols, hid, width, mid, end):
    shape = jax.ShapeDtypeStruct
    wide = shape((adapters, RANK, width), F32)
    flat = lambda a: a.reshape(a.shape[0], -1, *a.shape[-2:])
    mid, end = flat(mid), flat(end)
    outs = [
        wide, shape((adapters, 3, RANK, cols), F32), shape((adapters, RANK, cols), F32), wide,
        wide, shape((adapters, RANK, hid), F32), shape((adapters, RANK, hid), F32), wide,
    ]
    part = lambda a: pl.BlockSpec((None, *a.shape[1:]), lambda i: (i, 0, 0, 0))
    return pl.pallas_call(
        functools.partial(sum_kernel, width, cols, hid),
        grid=(mid.shape[0],),
        in_specs=[part(mid), part(end)],
        out_specs=[pl.BlockSpec(a.shape, lambda i, n=len(a.shape): (0,) * n) for a in outs],
        out_shape=outs,
        compiler_params=params(),
        name="sum_gradients",
    )(mid, end)


def local(
    tokens, cotangent, norm_first, norm_second, entry_weight, output_weight, expand_weight, shrink_weight,
    entry_down, entry_up, output_down, output_up, expand_down, expand_up, shrink_down, shrink_up,
    adapter_choice, clip_count,
):
    cap = adapter_choice.shape[0]
    rows, width = tokens.shape
    adapters = entry_down.shape[0]
    cols, hid = output_weight.shape[1], expand_weight.shape[1]
    gain_first, gain_second = norm_first.reshape(1, width), norm_second.reshape(1, width)
    flip = lambda a: a.transpose(0, 2, 1)
    w_entry = entry_weight.transpose(1, 0, 2).reshape(-1, cols)
    (
        att, lse, inner_t, thin, rep, q, k, v, k_far, v_far, normed, tok, cot, w_full, wo_full, we_near, ws_near,
        we_land, ws_land,
    ) = front_part(
        cap, adapter_choice, clip_count, gain_first,
        (flip(entry_down), output_up, flip(expand_down), shrink_up),
        (entry_up.transpose(0, 2, 1, 3), flip(output_down), expand_up, flip(shrink_down)),
        tokens, cotangent, w_entry, output_weight, expand_weight, shrink_weight,
    )
    mixed, mgrad, agrad, grads, _, _ = middle_both_ways(
        cap, tok, att, cot, gain_second, rep, thin, wo_full, we_near, ws_near, we_land, ws_land,
        expand_weight, shrink_weight,
    )
    mixed, mid_grads, token_grad, end_grads = back_part(
        cap, q, k, k_far, v, v_far, att, lse, agrad, gain_first, rep, thin, inner_t, grads, mixed, w_full, mgrad, tok,
        normed,
    )
    ed, eu, od, ou, xd, xu, sd, su = sum_gradients(adapters, cols, hid, width, mid_grads, end_grads)
    return (
        mixed, token_grad, flip(ed), eu.transpose(0, 2, 1, 3), flip(od), ou, flip(xd), xu, flip(sd), su,
    )


def solution(mesh):
    in_specs = (
        P(BOTH, None), P(BOTH, None), P(), P(),
        P("dp", None, "tensor"), P("dp", "tensor"), P("dp", "tensor"), P("dp", "tensor"),
        P(), P(None, None, None, "tensor"), P(None, "tensor", None), P(),
        P(), P(None, None, "tensor"), P(None, "tensor", None), P(), P("dp"), P("dp"),
    )
    out_specs = (
        P(BOTH, None), P(BOTH, None), P(), P(None, None, None, "tensor"), P(None, "tensor", None), P(),
        P(), P(None, None, "tensor"), P(None, "tensor", None), P(),
    )
    return jax.shard_map(local, mesh=mesh, in_specs=in_specs, out_specs=out_specs, check_vma=False)
```

```python
import functools

import jax
import jax.numpy as jnp
from jax import lax
from jax.experimental import pallas as pl
from jax.experimental.pallas import tpu as pltpu
from jax.sharding import PartitionSpec as P

HEAD_DIM = 64
PAIR = 2 * HEAD_DIM
RANK = 16
LOG2E = 1.4426950408889634
LN2 = 0.6931471805599453
F32, BF = jnp.float32, jnp.bfloat16
VMEM_LIMIT = 60 * 2**20


def dot(a, b, ca, cb):
    return lax.dot_general(a, b, (((ca,), (cb,)), ((), ())), preferred_element_type=F32)


def params(**more):
    return pltpu.CompilerParams(vmem_limit_bytes=VMEM_LIMIT, **more)


def merge_rows(block):
    return block.reshape(block.shape[0] * block.shape[1], block.shape[2])


def norm_parts(values):
    centre = jnp.mean(values, axis=-1, keepdims=True)
    shifted = values - centre
    scale = lax.rsqrt(jnp.mean(shifted * shifted, axis=-1, keepdims=True) + 1e-05)
    return shifted * scale, scale


def norm_back(hat, scale, gain, grad):
    inner = grad * gain
    mean_one = jnp.mean(inner, axis=-1, keepdims=True)
    mean_two = jnp.mean(inner * hat, axis=-1, keepdims=True)
    return scale * (inner - mean_one - hat * mean_two)


MESH = pl.DeviceIdType.MESH
BOTH = ("dp", "tensor")
ANY = pl.BlockSpec(memory_space=pl.ANY)
IN_VMEM = pl.BlockSpec(memory_space=pltpu.VMEM)
IN_SMEM = pl.BlockSpec(memory_space=pltpu.SMEM)
DMA = pltpu.SemaphoreType.DMA


class Place:
    def __init__(self, n_dp, n_t, cap):
        self.n_dp, self.n_t, self.cap = n_dp, n_t, cap
        self.dp, self.t = lax.axis_index("dp"), lax.axis_index("tensor")
        self.core, self.q = self.dp % 2, self.dp // 2
        self.n_q, self.n_hi = n_dp // 2, n_dp // 4
        self.lo, self.hi = self.q % 2, self.q // 2
        self.group = n_t // cap
        self.half = self.group // 2
        self.slot, block = self.t // self.group, self.t % self.group
        self.high, self.low = block // self.half, block % self.half
        self.stays = self.core == self.high
        self.sibling = (self.dp + 1 - 2 * self.core, self.t)
        self.partner = (self.dp - self.core + self.high, self.t - block + self.core * self.half + self.low)

    def along(self, d):
        return (self.t + d) % self.n_t

    def column(self, d, cols):
        return pl.ds(pl.multiple_of(((self.t + self.n_t - d) % self.n_t) * cols, cols), cols)

    def lo_q(self):
        return self.q + 1 - 2 * self.lo

    def hi_q(self, m, lo=None):
        return ((self.hi + m) % self.n_hi) * 2 + (self.lo if lo is None else lo)

    def device(self, q, core=None, t=None):
        return (q * 2 + (self.core if core is None else core), self.t if t is None else t)

    def mate(self, shift):
        block = (self.core * self.half + self.low + shift) % self.group
        return (self.dp - self.core + block // self.half, self.t - self.low + block % self.half)

    def gather_peers(self):
        return (
            [(self.dp, self.along(d)) for d in range(1, self.n_t)]
            + [self.sibling, self.device(self.lo_q())]
            + [self.device(self.hi_q(m)) for m in range(1, self.n_hi)]
        )

    def other_core_peers(self):
        return [(self.sibling[0], self.along(d)) for d in range(1, self.n_t)]


def greet(peers):
    barrier = pltpu.get_barrier_semaphore()
    for peer in peers:
        pl.semaphore_signal(barrier, inc=1, device_id=peer, device_id_type=MESH)
    pl.semaphore_wait(barrier, len(peers))


def remote(src, dst, send, recv, device):
    return pltpu.make_async_remote_copy(
        src_ref=src, dst_ref=dst, send_sem=send, recv_sem=recv, device_id=device, device_id_type=MESH
    )


class Gather:
    @staticmethod
    def keys(n_hi, ds, here):
        found = []
        for d in ds:
            found += [] if d in here else [("z", d)]
            found += [("x", d), ("s", d)]
            for m in range(1, n_hi):
                found += [("y", m, d), ("dy", m, d), ("dx", m, d)]
        return found

    @staticmethod
    def scratch(n_dp, ds, here=(0,)):
        count = len(Gather.keys(n_dp // 4, ds, here))
        return [DMA((count,)), DMA((count,)), DMA((len(here),))]

    def __init__(self, place, sources, full, ds, sems, spread=None, by_rows=True):
        self.place, self.sources, self.full, self.ds = place, sources, full, list(ds)
        self.send, self.recv, self.own = sems
        self.index = {k: i for i, k in enumerate(Gather.keys(place.n_hi, self.ds, sources))}
        self.spread, self.by_rows = spread, by_rows
        self.ms = range(1, place.n_hi)

    def block(self, d, q, half=None):
        ref = self.full.at[self.ds.index(d), q, self.place.core]
        if half is None:
            return ref
        rows, cols = self.full.shape[-2:]
        if self.by_rows:
            return ref.at[pl.ds(half * (rows // 2), rows // 2)]
        first = cols // 2 // 128 * 128
        return ref.at[:, pl.ds(half * first, cols - first if half else first)]

    def copy(self, key):
        p, kind, d = self.place, key[0], key[-1]
        i = self.index[key]
        if kind == "z":
            src = self.sources[0] if self.spread is None else self.spread(d)
            dst, device = self.block(d, p.q), (p.dp, p.along(d))
        elif kind == "s":
            src = dst = self.full.at[self.ds.index(d), :, p.core]
            device = p.sibling
        elif kind in "xy":
            src = self.sources[d] if d in self.sources else self.block(d, p.q)
            dst = self.block(d, p.q)
            device = p.device(p.lo_q() if kind == "x" else p.hi_q(key[1]))
        elif kind == "dy":
            src = dst = self.block(d, p.lo_q(), 0)
            device = p.device(p.hi_q(key[1]))
        else:
            src = dst = self.block(d, p.hi_q(p.n_hi - key[1]), 1)
            device = p.device(p.lo_q())
        return remote(src, dst, self.send.at[i], self.recv.at[i], device)

    def own_copy(self, d):
        i = list(self.sources).index(d)
        return pltpu.make_async_copy(self.sources[d], self.block(d, self.place.q), self.own.at[i])

    def along(self, d):
        self.copy(("z", d)).start()

    def relay(self, d):
        if d in self.sources:
            self.own_copy(d).start()
        else:
            self.copy(("z", d)).wait_recv()
        self.copy(("x", d)).start()
        for m in self.ms:
            self.copy(("y", m, d)).start()

    def diag(self, d):
        self.copy(("x", d)).wait_recv()
        for m in self.ms:
            self.copy(("dy", m, d)).start()
        for m in self.ms:
            self.copy(("y", m, d)).wait_recv()
            self.copy(("dx", m, d)).start()

    def share(self, d):
        if d in self.sources:
            self.own_copy(d).wait()
        for m in self.ms:
            self.copy(("dy", m, d)).wait_recv()
            self.copy(("dx", m, d)).wait_recv()
        self.copy(("s", d)).start()

    def done(self, d):
        self.copy(("s", d)).wait_recv()

    def finish(self):
        for key in self.index:
            self.copy(key).wait_send()


def run_events(step, batches):
    for i, batch in enumerate(batches):
        if batch:

            @pl.when(step == i)
            def _():
                for event in batch:
                    event()


def cut(names, letter):
    parts = [[]]
    for name in names:
        if name[0] == letter:
            parts.append([])
        else:
            parts[-1].append(name)
    return parts


def orders(n_t, pairs, sub, group):
    if (n_t, pairs, sub, group) == (4, 2, 2, 2):
        return FRONT, MIDDLE
    near = n_t // 2
    late = list(reversed(range(near, n_t)))
    name = lambda letters, d: letters + str(d)
    front = ["G", "T", "er0", "xr0", "hr0", "or0", "A"]
    for d in range(1, n_t):
        front += [name(g, d) for g in (("ea", "oa", "xa", "ha") if d < near else ("ea", "oa"))]
    front += ["X", "H", "C"]
    every = lambda g, d: [name(g + a, d) for a in ("rds" if d else "ds")]
    for d in range(n_t):
        front += every("e", d)
    front += ["W", "g", "N"]
    for d in range(n_t):
        front += [name("R", d), name("P", d)]
    for d in range(n_t):
        front += every("o", d) + (every("x", d) + every("h", d) if d < near else [])
    for d in range(n_t):
        front += [name("V", d)] + [name("K", d * pairs + i) for i in range(pairs)]
    middle = []
    for g in "xh":
        middle += [name(g + "r", late[0])] + [name(g + "a", d) for d in late[1:]]
    middle += ["I"]
    for i in range(n_t * sub):
        middle += [name("F", i)]
        if i == 0:
            for d in late:
                for g in "xh":
                    middle += every(g, d)[1 if d == late[0] else 0 :]
        if (i + 1) % sub == 0 and near <= (i + 1) // sub < n_t:
            middle += [name("B", late[(i + 1) // sub - near])]
    return front, middle


FRONT = (
    "G", "ea1", "hr0", "er0", "xr0", "T", "A", "ed0", "ea2", "hd0", "es0", "er1", "W", "ed1", "xd0", "ea3",
    "oa3", "N", "es1", "or0", "oa2", "er2", "R0", "g", "xa1", "P0", "ha1", "R1", "er3", "V0", "od0", "K0",
    "oa1", "xs0", "ed2", "ed3", "or2", "P1", "xr1", "K1", "es2", "hr1", "C", "V1", "K2", "hs0", "R2", "P2",
    "or1", "es3", "K3", "hd1", "od2", "R3", "or3", "X", "od1", "P3", "V2", "K4", "V3", "os0", "hs1", "od3",
    "os2", "xd1", "K5", "os1", "H", "os3", "K6", "xs1", "K7",
)
MIDDLE = (
    "xa2", "xr3", "I", "hr3", "F0", "xd3", "xr2", "ha2", "F1", "hd3", "F2", "xd2", "xs3", "hs3", "hr2", "F3",
    "B3", "xs2", "hd2", "F4", "hs2", "F5", "B2", "F6", "F7",
)
STEPS = {"a": Gather.along, "r": Gather.relay, "d": Gather.diag, "s": Gather.share}


def move(place, source, target, sems, begin, rows=None):
    if rows is not None:
        source, target = source.at[rows], target.at[rows]

    @pl.when(place.stays)
    def _():
        here = pltpu.make_async_copy(source, target, sems[2])
        here.start() if begin else here.wait()

    @pl.when(jnp.logical_not(place.stays))
    def _():
        there = remote(source, target, sems[0], sems[1], place.partner)
        there.start() if begin else there.wait()


def head_masks(shape):
    lane = lax.broadcasted_iota(jnp.int32, shape, 1)
    return lane < HEAD_DIM, lane >= HEAD_DIM


def ones_lanes(rows, count):
    lane = lax.broadcasted_iota(jnp.int32, (rows, PAIR), 1)
    return jnp.where(lane < count, 1.0, 0.0).astype(BF)


def attend(queries, keys, values, o_ref, lse_ref):
    rows, length = queries.shape[0], keys.shape[0]
    values = jnp.concatenate([values, ones_lanes(length, 1)], axis=1)
    zero = jnp.zeros_like(queries)
    outs, sums = [], []
    both = [dot(jnp.where(mask, queries, zero), keys, 1, 1) for mask in head_masks(queries.shape)]
    for scores in both:
        top = jnp.max(scores, axis=1, keepdims=True)
        probs = jnp.exp2(scores - top).astype(BF)
        mixed = dot(probs, values, 1, 0)
        total = mixed[:, PAIR : PAIR + 1]
        outs.append(mixed[:, :PAIR] / total)
        sums.append(top + jnp.log2(total))
    first, _ = head_masks((rows, PAIR))
    o_ref[...] = jnp.where(first, outs[0], outs[1]).astype(BF)
    lse_ref[...] = jnp.where(first, sums[0], sums[1])


def front_kernel(
    n_dp, n_t, cap,
    choice_ref, count_ref, gain_ref, ed_tab, ou_tab, xd_tab, su_tab, eu_tab, od_tab, xu_tab, sd_tab,
    tokens_ref, cot_ref, w_ref, wo_ref, we_ref, ws_ref,
    o_ref, lse_ref, inner_t_ref, thin_out, rep_out,
    q_out, k_out, v_out, k_far_out, v_far_out, normed_out, tok_out, cot_out, w_full, wo_full, we_full, ws_full,
    we_land, ws_land,
    q, k, v, k_far, v_far, tok, cot, normed, thin, rep, thin_send, stage, inner,
    tok_sems, cot_sems, thin_sends, thin_recvs, rep_sems, stage_sems, kv_sends, kv_recvs, keep_sems, kept_sems,
    land_sems, go_sem, *sems,
):
    p = Place(n_dp, n_t, cap)
    step, steps = pl.program_id(0), pl.num_programs(0)
    cols, hid = od_tab.shape[-1], xu_tab.shape[-1]
    pairs = cols // PAIR
    depth = w_ref.shape[0] // 3
    early = list(range(n_t // 2))
    entry = Gather(p, {0: w_ref}, w_full, range(n_t), sems[0:3])
    out_g = Gather(p, {0: wo_ref}, wo_full, range(n_t), sems[3:6])
    exp_g = Gather(p, {0: we_ref}, we_full, early, sems[6:9])
    shr_g = Gather(p, {0: ws_ref}, ws_full, early, sems[9:12])
    both = (exp_g, shr_g)
    tok_three = [tok_sems.at[i] for i in range(3)]
    cot_three = [cot_sems.at[i] for i in range(3)]

    def thin_targets():
        for s in range(cap):
            for low in range(p.half):
                to = s * p.group + p.core * p.half + low
                for core in range(2):
                    i = (s * p.half + low) * 2 + core
                    elsewhere = jnp.logical_or(core != p.core, to != p.t)
                    yield s, to, core, i, elsewhere

    def send_thin(near):
        for s, to, core, i, elsewhere in thin_targets():
            d = (to + n_t - p.t) % n_t

            @pl.when(jnp.logical_and(elsewhere, (to == p.t) == near))
            def _():
                remote(
                    thin_send.at[s], thin.at[d], thin_sends.at[i], thin_recvs.at[d], (p.dp - p.core + core, to)
                ).start()

    def send_adapters():
        for s in range(cap):
            a = choice_ref[s]
            for i in range(3):
                thin_send[s, :, i * cols : (i + 1) * cols] = eu_tab[a, i]
            thin_send[s, :, 3 * cols : 4 * cols] = od_tab[a]
            thin_send[s, :, 4 * cols : 4 * cols + hid] = xu_tab[a]
            thin_send[s, :, 4 * cols + hid :] = sd_tab[a]
        send_thin(True)

        @pl.when(p.stays)
        def _():
            a = choice_ref[p.slot]
            for i, table in enumerate((ed_tab, ou_tab, xd_tab, su_tab)):
                rep[i * RANK : (i + 1) * RANK] = table[a]
            row = lax.broadcasted_iota(jnp.int32, (RANK, rep.shape[1]), 0)
            alive = jnp.where(p.slot < count_ref[0], 1.0, 0.0)
            rep[4 * RANK :] = jnp.where(row < RANK // 2, alive, a.astype(F32)).astype(BF)
            remote(rep, rep, rep_sems.at[0], rep_sems.at[1], p.sibling).start()
            thin[0] = thin_send[p.slot]

    def take_near():
        @pl.when(jnp.logical_not(p.stays))
        def _():
            remote(rep, rep, rep_sems.at[0], rep_sems.at[1], p.sibling).wait_recv()
            remote(thin_send.at[0], thin.at[0], thin_sends.at[0], thin_recvs.at[0], p.sibling).wait_recv()

        rep_out[...] = rep[...]
        thin_out[0] = thin[0]

    def take_thin(d):
        remote(thin_send.at[0], thin.at[d], thin_sends.at[0], thin_recvs.at[d], p.sibling).wait_recv()
        thin_out[d] = thin[d]

    def load(d):
        return pltpu.make_async_copy(w_full.at[d], stage.at[d % 2], stage_sems.at[d % 2])

    def kept():
        return [pltpu.make_async_copy(tok, tok_out, keep_sems.at[0]), pltpu.make_async_copy(normed, normed_out, keep_sems.at[1])]

    def first_norm():
        hat, _ = norm_parts(tok[...].astype(F32))
        value = (hat * gain_ref[...]).astype(BF)
        normed[...] = value
        down = rep[:RANK]
        inner[...] = dot(value, down, 1, 1).astype(BF)
        inner_t_ref[...] = dot(down, value, 1, 1).astype(BF)
        for copy in kept():
            copy.start()

    def far_copy(d, which, m):
        source, target = ((k, k_far), (v, v_far))[which]
        device = p.mate(m)
        there = (d + device[1] + n_t - p.t) % n_t
        return remote(
            source.at[pl.ds(d * pairs, pairs)], target.at[m - 1, pl.ds(there * pairs, pairs)],
            kv_sends.at[d, which, m - 1], kv_recvs.at[there, which, m - 1], device,
        )

    def far_arrival(d, which, m):
        source, target = ((k, k_far), (v, v_far))[which]
        return remote(
            source.at[pl.ds(d * pairs, pairs)], target.at[m - 1, pl.ds(d * pairs, pairs)],
            kv_sends.at[d, which, m - 1], kv_recvs.at[d, which, m - 1], p.mate(m),
        )

    def project(d):
        load(d).wait()
        for which, out in ((1, k), (2, v), (0, q)):
            weights = stage[d % 2, :, :, which * depth : (which + 1) * depth].reshape(n_dp * depth, cols)
            part = dot(normed[...], weights, 1, 0)
            part = part + dot(inner[...], thin[d, :, which * cols : (which + 1) * cols], 1, 0)
            if which == 0:
                part = part * (HEAD_DIM**-0.5 * LOG2E)
            part = part.astype(BF)
            for i in range(pairs):
                out[d * pairs + i] = part[:, i * PAIR : (i + 1) * PAIR]
            if which:
                for m in range(1, p.group):
                    far_copy(d, which - 1, m).start()

    def copies_out(d):
        at = pl.ds(d * pairs, pairs)
        found = [(a.at[at], b.at[at]) for a, b in ((q, q_out), (k, k_out), (v, v_out))]
        for a, b in ((k_far, k_far_out), (v_far, v_far_out)):
            found += [(a.at[m, at], b.at[m, at]) for m in range(p.group - 1)]
        return [pltpu.make_async_copy(a, b, kept_sems.at[d, i]) for i, (a, b) in enumerate(found)]

    def arrive(d):
        for m in range(1, p.group):
            far_arrival(d, 0, m).wait_recv()
            far_arrival(d, 1, m).wait_recv()
        for copy in copies_out(d):
            copy.start()

    def land(i):
        source, target = ((we_ref, we_land), (ws_ref, ws_land))[i]
        return remote(source, target, land_sems.at[0, i], land_sems.at[1, i], (p.dp, p.along(n_t - 1)))

    def ready(d):
        if d:
            take_thin(d)
        entry.done(d)
        load(d).start()

    def go():
        @pl.when(jnp.logical_not(p.stays))
        def _():
            pl.semaphore_signal(go_sem, inc=1, device_id=p.sibling, device_id_type=MESH)

        @pl.when(p.stays)
        def _():
            pl.semaphore_wait(go_sem, 1)

    def arrived():
        move(p, tokens_ref, tok, tok_three, False)
        send_thin(False)

    def norm():
        take_near()
        first_norm()

    def opened():
        greet(p.gather_peers() + p.other_core_peers())

    gathers = {"e": entry, "x": exp_g, "h": shr_g, "o": out_g}
    plain = {
        "G": opened, "g": go, "W": arrived, "N": norm, "A": send_adapters,
        "T": lambda: move(p, tokens_ref, tok, tok_three, True), "C": lambda: move(p, cot_ref, cot, cot_three, True),
        "X": lambda: land(0).start(), "H": lambda: land(1).start(),
    }
    counted = {"R": ready, "P": project, "V": arrive}

    def event(name):
        if len(name) == 1:
            return plain[name]
        if len(name) == 2:
            return lambda: counted[name[0]](int(name[1]))
        return lambda: STEPS[name[1]](gathers[name[0]], int(name[2]))

    names = orders(n_t, pairs, max(1, hid // 512), p.group)[0]
    parts = cut(names, "K")
    closing = [event(name) for name in parts.pop()]
    first = ["P0" in part or sum(name[0] == "P" for name in part) > 1 for part in parts]
    single = {}
    before, after = [], []
    for i, part in enumerate(parts):
        places = [] if first[i] else [j for j, name in enumerate(part) if name[0] == "P"]
        at = places[0] if places else len(part)
        if places:
            single[i] = int(part[at][1])
        before.append([event(name) for name in part[:at]])
        after.append([event(name) for name in part[at + 1 :]])
    run_events(step, before)
    if single:
        chunk = sum(jnp.where(step == i, d, 0) for i, d in single.items())

        @pl.when(chunk > 0)
        def _():
            project(chunk)

    run_events(step, after)
    keys = jnp.concatenate([k[step]] + [k_far[m, step] for m in range(p.group - 1)], axis=0)
    values = jnp.concatenate([v[step]] + [v_far[m, step] for m in range(p.group - 1)], axis=0)
    attend(q[step], keys, values, o_ref, lse_ref)

    @pl.when(step == steps - 1)
    def _():
        for call in closing:
            call()
        for g in (exp_g, shr_g, out_g):
            for d in g.ds:
                g.done(d)
        for g in (entry, exp_g, shr_g, out_g):
            g.finish()
        for i in range(2):
            land(i).wait()
        move(p, cot_ref, cot, cot_three, False)
        keep_cot = pltpu.make_async_copy(cot, cot_out, keep_sems.at[2])
        keep_cot.start()

        @pl.when(p.stays)
        def _():
            remote(rep, rep, rep_sems.at[0], rep_sems.at[1], p.sibling).wait_send()

        for s, to, core, i, elsewhere in thin_targets():

            @pl.when(elsewhere)
            def _():
                remote(thin_send.at[s], thin.at[0], thin_sends.at[i], thin_recvs.at[0], p.sibling).wait_send()

        for copy in [keep_cot, *kept()]:
            copy.wait()
        for d in range(n_t):
            for m in range(1, p.group):
                far_copy(d, 0, m).wait_send()
                far_copy(d, 1, m).wait_send()
            for copy in copies_out(d):
                copy.wait()


def front_part(cap, choice, count, gain, rep_tables, thin_tables, tokens, cot, w, wo, we, ws):
    n_dp, n_t = lax.axis_size("dp"), lax.axis_size("tensor")
    rows, width = tokens.shape
    cols = wo.shape[-1]
    others = n_t // cap - 1
    count_pairs = width // PAIR
    early = n_t // 2
    thin_width = 4 * cols + 2 * we.shape[-1]
    shape, vmem = jax.ShapeDtypeStruct, pltpu.VMEM
    whole = lambda *s: pl.BlockSpec(s, lambda h: (0,) * len(s))
    pair = pl.BlockSpec((None, rows, PAIR), lambda h: (h, 0, 0))
    full = lambda n, a: shape((n, n_dp // 2, 2, *a.shape), BF)
    heads, far = (count_pairs, rows, PAIR), (others, count_pairs, rows, PAIR)
    small = [(RANK, rows), (n_t, RANK, thin_width), (5 * RANK, width)]
    return pl.pallas_call(
        functools.partial(front_kernel, n_dp, n_t, cap),
        grid=(count_pairs,),
        in_specs=[IN_SMEM, IN_SMEM] + [whole(*a.shape) for a in (gain, *rep_tables, *thin_tables)]
        + [ANY] * 2 + [whole(*a.shape) for a in (w, wo, we, ws)],
        out_specs=[pair, pair] + [whole(*s) for s in small] + [ANY] * 14,
        out_shape=[shape(heads, BF), shape(heads, F32)] + [shape(s, BF) for s in small]
        + [shape(heads, BF)] * 3 + [shape(far, BF)] * 2 + [shape((rows, width), BF)] * 3
        + [full(n_t, w), full(n_t, wo), full(early, we), full(early, ws), shape(we.shape, BF), shape(ws.shape, BF)],
        scratch_shapes=[
            vmem(heads, BF), vmem(heads, BF), vmem(heads, BF), vmem(far, BF), vmem(far, BF),
            vmem((rows, width), BF), vmem((rows, width), BF), vmem((rows, width), BF), vmem(small[1], BF), vmem(small[2], BF),
            vmem((cap, RANK, thin_width), BF),
            vmem((2, n_dp // 2, 2, *w.shape), BF), vmem((rows, RANK), BF),
            DMA((3,)), DMA((3,)), DMA((n_t,)), DMA((n_t,)), DMA((2,)), DMA((2,)),
            DMA((n_t, 2, others)), DMA((n_t, 2, others)), DMA((3,)), DMA((n_t, 3 + 2 * others)), DMA((2, 2)),
            pltpu.SemaphoreType.REGULAR,
            *Gather.scratch(n_dp, range(n_t)), *Gather.scratch(n_dp, range(n_t)),
            *Gather.scratch(n_dp, range(early)), *Gather.scratch(n_dp, range(early)),
        ],
        compiler_params=params(collective_id=0, has_side_effects=True),
        name="front_part",
    )(choice, count, gain, *rep_tables, *thin_tables, tokens, cot, w, wo, we, ws)


def split_lanes(column):
    column = -column
    high = column.astype(BF)
    rest = column - high.astype(F32)
    mid = rest.astype(BF)
    low = (rest - mid.astype(F32)).astype(BF)
    lane = lax.broadcasted_iota(jnp.int32, (column.shape[0], PAIR), 1)
    zero = jnp.zeros((column.shape[0], PAIR), BF)
    return jnp.where(lane == 0, high, jnp.where(lane == 1, mid, jnp.where(lane == 2, low, zero)))


def back_kernel(
    n_dp, n_t, cap, tiles,
    q_ref, k_ref, k_far, v_ref, v_far, o_ref, lse_ref, do_ref, gain_ref, rep_ref, thin_ref, inner_t_ref, grads_ref,
    mixed_ref, w_ref, mgrad_ref, tok_ref, normed_ref,
    mixed_out, mid_full, tgrad_out, end_full,
    grad, send, far, mixed, weights, mgrad, tok, normed, back_sum, row_sum, back_low, tgrad, end, sends, recvs, swap, swaps, load_sems,
    *sems,
):
    p = Place(n_dp, n_t, cap)
    step, steps = pl.program_id(0), pl.num_programs(0)
    rows = q_ref.shape[0]
    pairs = grad.shape[1] // n_t
    cols = w_ref.shape[-1]
    depth = w_ref.shape[-2] // 3
    width = tok_ref.shape[1]
    mid_g = Gather(
        p, {0: grads_ref.at[0]}, mid_full, range(n_t), sems[0:3],
        spread=lambda d: grads_ref.at[n_t - d], by_rows=False,
    )
    end_g = Gather(
        p, {0: end.at[0]}, end_full, range(n_t), sems[3:6], spread=lambda d: end.at[n_t - d], by_rows=False
    )
    swap_sems = [swap.at[i] for i in range(3)]
    loads = [
        pltpu.make_async_copy(src, dst, load_sems.at[i])
        for i, (src, dst) in enumerate(((w_ref, weights), (normed_ref, normed), (tok_ref, tok), (mgrad_ref, mgrad)))
    ]
    relay, diag, share = ((lambda d, f=f: lambda: f(d)) for f in (mid_g.relay, mid_g.diag, mid_g.share))
    start_swap = lambda: move(p, mixed_ref, mixed, swap_sems, True)
    start_loads = lambda: [copy.start() for copy in loads]

    def opening():
        greet(p.gather_peers() + p.other_core_peers())
        mid_g.relay(0)
        for d in range(1, n_t):
            mid_g.along(d)

    if n_t == 4:
        table = {
            0: [opening], 1: [diag(0), relay(1)], 2: [share(0), diag(1), relay(2), start_swap],
            3: [share(1), diag(2), relay(3)], 4: [share(2), diag(3), start_loads], 5: [share(3)],
        }
    else:
        table = {0: [opening, start_swap, start_loads, diag(0), share(0)]}
        for d in range(1, n_t):
            table[0] += [relay(d), diag(d), share(d)]
    run_events(step, [table.get(i, []) for i in range(max(table) + 1)])

    with_far = lambda near, far: jnp.concatenate([near[...]] + [far[m] for m in range(p.group - 1)], axis=0)
    keys = with_far(k_ref, k_far)
    length = keys.shape[0]
    ones = ones_lanes(length, 3)
    keys_more = jnp.concatenate([keys, ones], axis=1)
    values_more = jnp.concatenate([with_far(v_ref, v_far), ones], axis=1)
    queries, grad_out = q_ref[...], do_ref[...]
    zero = jnp.zeros_like(queries)
    product = grad_out.astype(F32) * o_ref[...].astype(F32)
    d_queries, both = [], [[], [], [], []]
    for head, mask in enumerate(head_masks(queries.shape)):
        query = jnp.where(mask, queries, zero)
        grad_head = jnp.where(mask, grad_out, zero)
        lse = lse_ref[:, head * HEAD_DIM : head * HEAD_DIM + 1]
        delta = jnp.sum(jnp.where(mask, product, 0.0), axis=1, keepdims=True)
        probs = jnp.exp2(dot(jnp.concatenate([query, split_lanes(lse)], axis=1), keys_more, 1, 1))
        slope = dot(jnp.concatenate([grad_head, split_lanes(delta)], axis=1), values_more, 1, 1)
        score_grad = (probs * slope).astype(BF)
        d_queries.append(dot(score_grad, keys, 1, 0))
        for kept, one in zip(both, (grad_head, probs.astype(BF), query, score_grad)):
            kept.append(one)
    grad_heads, probs, query, score_grad = [jnp.concatenate(kept, axis=0) for kept in both]
    d_values = dot(grad_heads, probs, 0, 0)
    d_keys = dot(query, score_grad, 0, 0)
    first, _ = head_masks((rows, PAIR))
    grad[0, step] = (jnp.where(first, d_queries[0], d_queries[1]) * HEAD_DIM**-0.5).astype(BF)
    d_keys = (d_keys * LN2).T.astype(BF)
    d_values = d_values.T.astype(BF)
    grad[1, step] = d_keys[:rows]
    grad[2, step] = d_values[:rows]

    def far_copy(i, m, h):
        device = p.mate(p.group - m)
        there = (h // pairs + device[1] + n_t - p.t) % n_t * pairs + h % pairs
        return remote(
            send.at[i, m - 1, h], far.at[i, m - 1, there], sends.at[i, m - 1, h], recvs.at[i, m - 1, there], device
        )

    for m in range(1, p.group):
        send[0, m - 1, step] = d_keys[m * rows : (m + 1) * rows]
        send[1, m - 1, step] = d_values[m * rows : (m + 1) * rows]
        far_copy(0, m, step).start()
        far_copy(1, m, step).start()

    @pl.when(step == steps - 1)
    def _():
        move(p, mixed_ref, mixed, swap_sems, False)
        keep = pltpu.make_async_copy(mixed, mixed_out, swap.at[3])
        keep.start()
        for i in range(2):
            for m in range(1, p.group):
                for h in range(n_t * pairs):
                    remote(
                        send.at[i, m - 1, h], far.at[i, m - 1, h], sends.at[i, m - 1, h], recvs.at[i, m - 1, h], p.sibling
                    ).wait_recv()

            @pl.loop(0, steps)
            def _(h):
                total = grad[1 + i, h].astype(F32)
                for m in range(p.group - 1):
                    total = total + far[i, m, h].astype(F32)
                grad[1 + i, h] = total.astype(BF)

        columns = lambda which, d, rows: jnp.concatenate(
            [grad[which, d * pairs + i, rows] for i in range(pairs)], axis=1
        )
        chunks = n_t * 3
        back_sum[...] = jnp.zeros_like(back_sum)

        @pl.loop(0, chunks)
        def _(j):
            d, at = j // 3, pl.ds(pl.multiple_of(j % 3 * cols, cols), cols)
            part = columns(j % 3, d, slice(None))
            back_sum[...] += dot(part, thin_ref[d, :, at], 1, 1)
            end[d, :, at] = dot(inner_t_ref[...], part, 1, 0).astype(BF)

        back_low[...] = back_sum[...].astype(BF)
        loads[1].wait()
        down_grad = dot(back_low[...], normed[...], 0, 0).astype(BF)
        for d in range(n_t):
            end[d, :, 3 * cols :] = down_grad
        end_g.relay(0)
        for d in range(1, n_t):
            end_g.along(d)
        for copy in (loads[0], *loads[2:]):
            copy.wait()

        def tile(n):
            start, count = tiles[n]
            rows = pl.ds(start, count)
            acc = row_sum.at[pl.ds(0, count)]
            acc[...] = dot(back_low[rows], rep_ref[:RANK], 1, 0)

            @pl.loop(0, chunks)
            def _(j):
                at = pl.ds(pl.multiple_of(j % 3 * depth, depth), depth)
                piece = weights[j // 3, :, :, at].reshape(width, cols)
                acc[...] += dot(columns(j % 3, j // 3, rows), piece, 1, 1)

            total = acc[...]
            hat, scale = norm_parts(tok[rows].astype(F32))
            tgrad[rows] = (mgrad[rows] + norm_back(hat, scale, gain_ref[...], total)).astype(BF)
            move(p, tgrad, tgrad_out, [swaps.at[n, i] for i in range(3)], True, rows)

        for n in range(len(tiles)):
            tile(n)
            if n == 0:
                end_g.diag(0)
                end_g.relay(1)
            if n == min(1, len(tiles) - 1):
                for d in range(2, n_t):
                    end_g.relay(d)
                end_g.share(0)
                end_g.diag(1)
        for d in range(2, n_t):
            end_g.diag(d)
            end_g.share(d - 1)
        end_g.share(n_t - 1)
        for d in range(n_t):
            mid_g.done(d)
            end_g.done(d)
        mid_g.finish()
        end_g.finish()
        for n, (start, count) in enumerate(tiles):
            move(p, tgrad, tgrad_out, [swaps.at[n, i] for i in range(3)], False, pl.ds(start, count))

        @pl.loop(0, steps)
        def _(h):
            for m in range(1, p.group):
                for i in range(2):
                    far_copy(i, m, h).wait_send()

        keep.wait()


def back_part(cap, q, k, k_far, v, v_far, o, lse, do, gain, rep, thin, inner_t, grads, mixed, w_full, mgrad, tok, normed):
    n_dp, n_t = lax.axis_size("dp"), lax.axis_size("tensor")
    heads, rows, _ = q.shape
    width, cols = tok.shape[1], w_full.shape[-1]
    others = k_far.shape[0]
    pair = pl.BlockSpec((None, rows, PAIR), lambda h: (h, 0, 0))
    far = pl.BlockSpec((others, None, rows, PAIR), lambda h: (0, h, 0, 0))
    whole = lambda a: pl.BlockSpec(a.shape, lambda h: (0,) * len(a.shape))
    shape, vmem = jax.ShapeDtypeStruct, pltpu.VMEM
    count = (2, others, heads)
    number = 3 if rows % 16 == 0 else 1
    size = rows // number // 16 * 16 if number > 1 else rows
    tiles = [(0, rows - size * (number - 1))]
    tiles += [(tiles[0][1] + size * i, size) for i in range(number - 1)]
    end_width = 3 * cols + width
    full = lambda n: shape((n_t, n_dp // 2, 2, RANK, n), BF)
    return pl.pallas_call(
        functools.partial(back_kernel, n_dp, n_t, cap, tiles),
        grid=(heads,),
        in_specs=[pair, pair, far, pair, far, pair, pair, pair]
        + [whole(a) for a in (gain, rep, thin, inner_t, grads)] + [ANY] * 5,
        out_specs=[ANY] * 4,
        out_shape=[shape(mixed.shape, BF), full(grads.shape[-1]), shape(tok.shape, BF), full(end_width)],
        scratch_shapes=[
            vmem((3, heads, rows, PAIR), BF), vmem((2, *k_far.shape), BF), vmem((2, *k_far.shape), BF),
            vmem(mixed.shape, BF), vmem(w_full.shape, BF), vmem(mgrad.shape, F32), vmem(tok.shape, BF),
            vmem(tok.shape, BF), vmem((rows, RANK), F32), vmem((tiles[0][1], width), F32), vmem((rows, RANK), BF),
            vmem(tok.shape, BF), vmem((n_t, RANK, end_width), BF),
            DMA(count), DMA(count), DMA((4,)), DMA((len(tiles), 3)), DMA((4,)),
            *Gather.scratch(n_dp, range(n_t)), *Gather.scratch(n_dp, range(n_t)),
        ],
        compiler_params=params(collective_id=1, has_side_effects=True),
        name="back_part",
    )(q, k, k_far, v, v_far, o, lse, do, gain, rep, thin, inner_t, grads, mixed, w_full, mgrad, tok, normed)


def gelu_parts(hidden):
    share = 0.5 * (1.0 + lax.erf(hidden * 0.7071067811865476))
    density = jnp.exp(-0.5 * hidden * hidden) * 0.3989422804014327
    return hidden * share, share + hidden * density


def middle_kernel(
    n_dp, n_t, cap, sub,
    x_ref, att_ref, cot_ref, gain_ref, rep_ref, thin_ref, wo_ref, we_near, ws_near, we_land, ws_land, we_ref, ws_ref,
    mixed_ref, mgrad_ref, agrad_ref, grads_ref, we_full, ws_full,
    middle_ref, second_ref, dy_ref, acc2_ref, acc3_ref, einner_ref, einner_t_ref, sback_ref, sback_t_ref,
    sinner_ref, eback_ref, oinner_ref, we_buf, ws_buf, buf_sems, *sems,
):
    p = Place(n_dp, n_t, cap)
    step, steps = pl.program_id(0), pl.num_programs(0)
    cols = wo_ref.shape[-1]
    width = x_ref.shape[1]
    hid = we_ref.shape[-1]
    size = hid // sub
    near = n_t // 2
    late = list(reversed(range(near, n_t)))
    exp_g = Gather(p, {n_t - 1: we_land}, we_full, late, sems[0:3], spread=lambda d: we_ref)
    shr_g = Gather(p, {n_t - 1: ws_land}, ws_full, late, sems[3:6], spread=lambda d: ws_ref)
    pairs = cols // PAIR
    both = (exp_g, shr_g)
    down_e, up_o, up_s = rep_ref[2 * RANK : 3 * RANK], rep_ref[RANK : 2 * RANK], rep_ref[3 * RANK : 4 * RANK]
    alive = rep_ref[4 * RANK : 4 * RANK + 1, 0:1].astype(F32)
    at_od, at_eu = 3 * width, 3 * width + cols
    at_sd, at_id = at_eu + hid, at_eu + 2 * hid

    def load(i):
        index, part = i // sub, i % sub
        at = pl.ds(part * size, size)
        pair = (we_near, ws_near) if index < near else (we_full, ws_full)
        index = index if index < near else index - near
        return [
            pltpu.make_async_copy(src.at[index, :, :, :, at], buf.at[i % 3], buf_sems.at[i % 3, j])
            for j, (src, buf) in enumerate(zip(pair, (we_buf, ws_buf)))
        ]

    gathers = {"x": exp_g, "h": shr_g}

    def bring(d):
        exp_g.done(d)
        shr_g.done(d)
        for i in range(sub):
            for copy in load((near + late.index(d)) * sub + i):
                copy.start()

    def event(name):
        if len(name) == 2:
            return lambda: bring(int(name[1]))
        return lambda: STEPS[name[1]](gathers[name[0]], int(name[2]))

    names = orders(n_t, pairs, sub, p.group)[1]
    begun = names.index("I")
    start = [event(name) for name in names[:begun]]
    opening, *after = [[event(name) for name in part] for part in cut(names[begun + 1 :], "F")]
    columns = lambda d: jnp.concatenate([att_ref[d * pairs + i] for i in range(pairs)], axis=1)

    @pl.when(step == 0)
    def _():
        greet(p.gather_peers())
        for call in start:
            call()
        for i in range(2):
            for copy in load(i):
                copy.start()
        branch, inner = 0.0, 0.0
        for d in range(n_t):
            att = columns(d)
            branch = branch + dot(att, wo_ref[d].reshape(width, cols), 1, 1)
            inner = inner + dot(att, thin_ref[d, :, 3 * cols : 4 * cols], 1, 1)
        inner = inner.astype(BF)
        oinner_ref[...] = inner
        middle = x_ref[...].astype(F32) + (branch + dot(inner, up_o, 1, 0))
        middle_ref[...] = middle
        hat, _ = norm_parts(middle)
        second = (hat * gain_ref[...]).astype(BF)
        second_ref[...] = second
        dy = (cot_ref[...].astype(F32) * alive).astype(BF)
        dy_ref[...] = dy
        einner_ref[...] = dot(second, down_e, 1, 1).astype(BF)
        einner_t_ref[...] = dot(down_e, second, 1, 1).astype(BF)
        sback_ref[...] = dot(dy, up_s, 1, 1).astype(BF)
        sback_t_ref[...] = dot(up_s, dy, 1, 1).astype(BF)
        acc2_ref[...] = jnp.zeros_like(acc2_ref)
        acc3_ref[...] = jnp.zeros_like(acc3_ref)
        sinner_ref[...] = jnp.zeros_like(sinner_ref)
        eback_ref[...] = jnp.zeros_like(eback_ref)

    run_events(step, [opening])
    for i in range(n_t * sub):

        @pl.when(step == i)
        def _():
            for copy in load(i):
                copy.wait()
            if i + 2 < near * sub:
                for copy in load(i + 2):
                    copy.start()

    buf = step % 3
    d, part = step // sub, step % sub
    d = jnp.where(d < near, d, n_t - 1 + near - d)
    we, ws = we_buf[buf].reshape(width, size), ws_buf[buf].reshape(width, size)
    at = pl.multiple_of(part * size, size)
    e_up = thin_ref[d, :, pl.ds(4 * cols + at, size)]
    s_down = thin_ref[d, :, pl.ds(4 * cols + hid + at, size)]
    hidden = dot(second_ref[...], we, 1, 0) + dot(einner_ref[...], e_up, 1, 0)
    value, slope = gelu_parts(hidden)
    act = value.astype(BF)
    acc2_ref[...] += dot(act, ws, 1, 1)
    sinner_ref[...] += dot(act, s_down, 1, 1)
    act_grad = dot(dy_ref[...], ws, 1, 0) + dot(sback_ref[...], s_down, 1, 0)
    hid_grad = (act_grad * slope).astype(BF)
    acc3_ref[...] += dot(hid_grad, we, 1, 1)
    eback_ref[...] += dot(hid_grad, e_up, 1, 1)
    grads_ref[d, :, pl.ds(at_eu + at, size)] = dot(einner_t_ref[...], hid_grad, 1, 0).astype(BF)
    grads_ref[d, :, pl.ds(at_sd + at, size)] = dot(sback_t_ref[...], act, 1, 0).astype(BF)

    run_events(step, after)
    @pl.when(step == steps - 1)
    def _():
        s_inner, e_back = sinner_ref[...].astype(BF), eback_ref[...].astype(BF)
        middle = middle_ref[...]
        mixed_ref[...] = (alive * (middle + (acc2_ref[...] + dot(s_inner, up_s, 1, 0)))).astype(BF)
        shrink_up = dot(s_inner, dy_ref[...], 0, 0).astype(BF)
        expand_down = dot(e_back, second_ref[...], 0, 0).astype(BF)
        second_grad = acc3_ref[...] + dot(e_back, down_e, 1, 0)
        hat, scale = norm_parts(middle)
        mgrad = cot_ref[...].astype(F32) * alive + norm_back(hat, scale, gain_ref[...], second_grad)
        mgrad_ref[...] = mgrad
        low = mgrad.astype(BF)
        o_back = dot(low, up_o, 1, 1).astype(BF)
        output_up = dot(oinner_ref[...], low, 0, 0).astype(BF)
        for d in range(n_t):
            agrad = dot(low, wo_ref[d].reshape(width, cols), 1, 0)
            agrad = (agrad + dot(o_back, thin_ref[d, :, 3 * cols : 4 * cols], 1, 0)).astype(BF)
            for i in range(pairs):
                agrad_ref[d * pairs + i] = agrad[:, i * PAIR : (i + 1) * PAIR]
            grads_ref[d, :, :width] = expand_down
            grads_ref[d, :, width : 2 * width] = shrink_up
            grads_ref[d, :, 2 * width : 3 * width] = output_up
            grads_ref[d, :, at_od : at_od + cols] = dot(o_back, columns(d), 0, 0).astype(BF)
            grads_ref[d, :, at_id:] = rep_ref[4 * RANK :, : grads_ref.shape[2] - at_id]
        for g in both:
            g.finish()


ID_LANES = 128


def middle_both_ways(cap, x, att, cot, gain, rep, thin, wo_full, we_near, ws_near, we_land, ws_land, we, ws):
    n_dp, n_t = lax.axis_size("dp"), lax.axis_size("tensor")
    rows, width = x.shape
    depth, hid = we.shape
    cols = wo_full.shape[-1]
    sub = max(1, hid // 512)
    size = hid // sub
    late = list(reversed(range(n_t // 2, n_t)))
    grad_width = 3 * width + cols + 2 * hid + ID_LANES
    whole = lambda a: pl.BlockSpec(a.shape, lambda i: (0,) * len(a.shape))
    shape = jax.ShapeDtypeStruct
    full = shape((len(late), n_dp // 2, 2, depth, hid), BF)
    outs = [
        shape((rows, width), BF), shape((rows, width), F32), shape(att.shape, BF),
        shape((n_t, RANK, grad_width), BF),
    ]
    vmem = pltpu.VMEM
    return pl.pallas_call(
        functools.partial(middle_kernel, n_dp, n_t, cap, sub),
        grid=(n_t * sub,),
        in_specs=[whole(a) for a in (x, att, cot, gain, rep, thin, wo_full)]
        + [ANY] * 2 + [whole(we_land), whole(ws_land)] + [ANY] * 2,
        out_specs=[whole(a) for a in outs] + [ANY] * 2,
        out_shape=outs + [full, full],
        scratch_shapes=[
            vmem((rows, width), F32), vmem((rows, width), BF), vmem((rows, width), BF),
            vmem((rows, width), F32), vmem((rows, width), F32),
            vmem((rows, RANK), BF), vmem((RANK, rows), BF), vmem((rows, RANK), BF), vmem((RANK, rows), BF),
            vmem((rows, RANK), F32), vmem((rows, RANK), F32), vmem((rows, RANK), BF),
            vmem((3, n_dp // 2, 2, depth, size), BF), vmem((3, n_dp // 2, 2, depth, size), BF), DMA((3, 2)),
            *Gather.scratch(n_dp, late, late[:1]), *Gather.scratch(n_dp, late, late[:1]),
        ],
        compiler_params=params(collective_id=2, has_side_effects=True),
        name="middle_both_ways",
    )(x, att, cot, gain, rep, thin, wo_full, we_near, ws_near, we_land, ws_land, we, ws)


def sum_kernel(
    width, cols, hid, mid_ref, end_ref, entry_down, entry_up, output_down, output_up, expand_down, expand_up,
    shrink_down, shrink_up,
):
    outs = (entry_down, entry_up, output_down, output_up, expand_down, expand_up, shrink_down, shrink_up)

    @pl.when(pl.program_id(0) == 0)
    def _():
        for out in outs:
            out[...] = jnp.zeros_like(out)

    sources = range(mid_ref.shape[0])
    at_id = 3 * width + cols + 2 * hid
    chosen = [jnp.max(mid_ref[i, RANK // 2 :, at_id : at_id + 128].astype(F32)).astype(jnp.int32) for i in sources]
    for i in sources:
        a = chosen[i]
        take = lambda ref, at, size: ref[i, :, at : at + size].astype(F32)
        expand_down[a] += take(mid_ref, 0, width)
        shrink_up[a] += take(mid_ref, width, width)
        output_up[a] += take(mid_ref, 2 * width, width)
        output_down[a] += take(mid_ref, 3 * width, cols)
        expand_up[a] += take(mid_ref, 3 * width + cols, hid)
        shrink_down[a] += take(mid_ref, 3 * width + cols + hid, hid)
        for which in range(3):
            entry_up[a, which] += take(end_ref, which * cols, cols)
        entry_down[a] += take(end_ref, 3 * cols, width)


def sum_gradients(adapters, cols, hid, width, mid, end):
    shape = jax.ShapeDtypeStruct
    wide = shape((adapters, RANK, width), F32)
    flat = lambda a: a.reshape(a.shape[0], -1, *a.shape[-2:])
    mid, end = flat(mid), flat(end)
    outs = [
        wide, shape((adapters, 3, RANK, cols), F32), shape((adapters, RANK, cols), F32), wide,
        wide, shape((adapters, RANK, hid), F32), shape((adapters, RANK, hid), F32), wide,
    ]
    part = lambda a: pl.BlockSpec((None, *a.shape[1:]), lambda i: (i, 0, 0, 0))
    return pl.pallas_call(
        functools.partial(sum_kernel, width, cols, hid),
        grid=(mid.shape[0],),
        in_specs=[part(mid), part(end)],
        out_specs=[pl.BlockSpec(a.shape, lambda i, n=len(a.shape): (0,) * n) for a in outs],
        out_shape=outs,
        compiler_params=params(),
        name="sum_gradients",
    )(mid, end)


def local(
    tokens, cotangent, norm_first, norm_second, entry_weight, output_weight, expand_weight, shrink_weight,
    entry_down, entry_up, output_down, output_up, expand_down, expand_up, shrink_down, shrink_up,
    adapter_choice, clip_count,
):
    cap = adapter_choice.shape[0]
    rows, width = tokens.shape
    adapters = entry_down.shape[0]
    cols, hid = output_weight.shape[1], expand_weight.shape[1]
    gain_first, gain_second = norm_first.reshape(1, width), norm_second.reshape(1, width)
    flip = lambda a: a.transpose(0, 2, 1)
    w_entry = entry_weight.transpose(1, 0, 2).reshape(-1, cols)
    (
        att, lse, inner_t, thin, rep, q, k, v, k_far, v_far, normed, tok, cot, w_full, wo_full, we_near, ws_near,
        we_land, ws_land,
    ) = front_part(
        cap, adapter_choice, clip_count, gain_first,
        (flip(entry_down), output_up, flip(expand_down), shrink_up),
        (entry_up.transpose(0, 2, 1, 3), flip(output_down), expand_up, flip(shrink_down)),
        tokens, cotangent, w_entry, output_weight, expand_weight, shrink_weight,
    )
    mixed, mgrad, agrad, grads, _, _ = middle_both_ways(
        cap, tok, att, cot, gain_second, rep, thin, wo_full, we_near, ws_near, we_land, ws_land,
        expand_weight, shrink_weight,
    )
    mixed, mid_grads, token_grad, end_grads = back_part(
        cap, q, k, k_far, v, v_far, att, lse, agrad, gain_first, rep, thin, inner_t, grads, mixed, w_full, mgrad, tok,
        normed,
    )
    ed, eu, od, ou, xd, xu, sd, su = sum_gradients(adapters, cols, hid, width, mid_grads, end_grads)
    return (
        mixed, token_grad, flip(ed), eu.transpose(0, 2, 1, 3), flip(od), ou, flip(xd), xu, flip(sd), su,
    )


def solution(mesh):
    in_specs = (
        P(BOTH, None), P(BOTH, None), P(), P(),
        P("dp", None, "tensor"), P("dp", "tensor"), P("dp", "tensor"), P("dp", "tensor"),
        P(), P(None, None, None, "tensor"), P(None, "tensor", None), P(),
        P(), P(None, None, "tensor"), P(None, "tensor", None), P(), P("dp"), P("dp"),
    )
    out_specs = (
        P(BOTH, None), P(BOTH, None), P(), P(None, None, None, "tensor"), P(None, "tensor", None), P(),
        P(), P(None, None, "tensor"), P(None, "tensor", None), P(),
    )
    return jax.shard_map(local, mesh=mesh, in_specs=in_specs, out_specs=out_specs, check_vma=False)
```

```python
import functools

import jax
import jax.numpy as jnp
from jax import lax
from jax.experimental import pallas as pl
from jax.experimental.pallas import tpu as pltpu
from jax.sharding import PartitionSpec as P

HEAD_DIM = 64
PAIR = 2 * HEAD_DIM
RANK = 16
LOG2E = 1.4426950408889634
LN2 = 0.6931471805599453
F32, BF = jnp.float32, jnp.bfloat16
VMEM_LIMIT = 60 * 2**20


def dot(a, b, ca, cb):
    return lax.dot_general(a, b, (((ca,), (cb,)), ((), ())), preferred_element_type=F32)


def params(**more):
    return pltpu.CompilerParams(vmem_limit_bytes=VMEM_LIMIT, **more)


def merge_rows(block):
    return block.reshape(block.shape[0] * block.shape[1], block.shape[2])


def norm_parts(values):
    centre = jnp.mean(values, axis=-1, keepdims=True)
    shifted = values - centre
    scale = lax.rsqrt(jnp.mean(shifted * shifted, axis=-1, keepdims=True) + 1e-05)
    return shifted * scale, scale


def norm_back(hat, scale, gain, grad):
    inner = grad * gain
    mean_one = jnp.mean(inner, axis=-1, keepdims=True)
    mean_two = jnp.mean(inner * hat, axis=-1, keepdims=True)
    return scale * (inner - mean_one - hat * mean_two)


MESH = pl.DeviceIdType.MESH
BOTH = ("dp", "tensor")
ANY = pl.BlockSpec(memory_space=pl.ANY)
IN_VMEM = pl.BlockSpec(memory_space=pltpu.VMEM)
IN_SMEM = pl.BlockSpec(memory_space=pltpu.SMEM)
DMA = pltpu.SemaphoreType.DMA


class Place:
    def __init__(self, n_dp, n_t, cap):
        self.n_dp, self.n_t, self.cap = n_dp, n_t, cap
        self.dp, self.t = lax.axis_index("dp"), lax.axis_index("tensor")
        self.core, self.q = self.dp % 2, self.dp // 2
        self.n_q, self.n_hi = n_dp // 2, n_dp // 4
        self.lo, self.hi = self.q % 2, self.q // 2
        self.group = n_t // cap
        self.half = self.group // 2
        self.slot, block = self.t // self.group, self.t % self.group
        self.high, self.low = block // self.half, block % self.half
        self.stays = self.core == self.high
        self.sibling = (self.dp + 1 - 2 * self.core, self.t)
        self.partner = (self.dp - self.core + self.high, self.t - block + self.core * self.half + self.low)

    def along(self, d):
        return (self.t + d) % self.n_t

    def column(self, d, cols):
        return pl.ds(pl.multiple_of(((self.t + self.n_t - d) % self.n_t) * cols, cols), cols)

    def lo_q(self):
        return self.q + 1 - 2 * self.lo

    def hi_q(self, m, lo=None):
        return ((self.hi + m) % self.n_hi) * 2 + (self.lo if lo is None else lo)

    def device(self, q, core=None, t=None):
        return (q * 2 + (self.core if core is None else core), self.t if t is None else t)

    def mate(self, shift):
        block = (self.core * self.half + self.low + shift) % self.group
        return (self.dp - self.core + block // self.half, self.t - self.low + block % self.half)

    def gather_peers(self):
        return (
            [(self.dp, self.along(d)) for d in range(1, self.n_t)]
            + [self.sibling, self.device(self.lo_q())]
            + [self.device(self.hi_q(m)) for m in range(1, self.n_hi)]
        )

    def other_core_peers(self):
        return [(self.sibling[0], self.along(d)) for d in range(1, self.n_t)]


def greet(peers):
    barrier = pltpu.get_barrier_semaphore()
    for peer in peers:
        pl.semaphore_signal(barrier, inc=1, device_id=peer, device_id_type=MESH)
    pl.semaphore_wait(barrier, len(peers))


def remote(src, dst, send, recv, device):
    return pltpu.make_async_remote_copy(
        src_ref=src, dst_ref=dst, send_sem=send, recv_sem=recv, device_id=device, device_id_type=MESH
    )


class Gather:
    @staticmethod
    def keys(n_hi, ds, here):
        found = []
        for d in ds:
            found += [] if d in here else [("z", d)]
            found += [("x", d), ("s", d)]
            for m in range(1, n_hi):
                found += [("y", m, d), ("dy", m, d), ("dx", m, d)]
        return found

    @staticmethod
    def scratch(n_dp, ds, here=(0,)):
        count = len(Gather.keys(n_dp // 4, ds, here))
        return [DMA((count,)), DMA((count,)), DMA((len(here),))]

    def __init__(self, place, sources, full, ds, sems, spread=None, by_rows=True):
        self.place, self.sources, self.full, self.ds = place, sources, full, list(ds)
        self.send, self.recv, self.own = sems
        self.index = {k: i for i, k in enumerate(Gather.keys(place.n_hi, self.ds, sources))}
        self.spread, self.by_rows = spread, by_rows
        self.ms = range(1, place.n_hi)

    def block(self, d, q, half=None):
        ref = self.full.at[self.ds.index(d), q, self.place.core]
        if half is None:
            return ref
        rows, cols = self.full.shape[-2:]
        if self.by_rows:
            return ref.at[pl.ds(half * (rows // 2), rows // 2)]
        first = cols // 2 // 128 * 128
        return ref.at[:, pl.ds(half * first, cols - first if half else first)]

    def copy(self, key):
        p, kind, d = self.place, key[0], key[-1]
        i = self.index[key]
        if kind == "z":
            src = self.sources[0] if self.spread is None else self.spread(d)
            dst, device = self.block(d, p.q), (p.dp, p.along(d))
        elif kind == "s":
            src = dst = self.full.at[self.ds.index(d), :, p.core]
            device = p.sibling
        elif kind in "xy":
            src = self.sources[d] if d in self.sources else self.block(d, p.q)
            dst = self.block(d, p.q)
            device = p.device(p.lo_q() if kind == "x" else p.hi_q(key[1]))
        elif kind == "dy":
            src = dst = self.block(d, p.lo_q(), 0)
            device = p.device(p.hi_q(key[1]))
        else:
            src = dst = self.block(d, p.hi_q(p.n_hi - key[1]), 1)
            device = p.device(p.lo_q())
        return remote(src, dst, self.send.at[i], self.recv.at[i], device)

    def own_copy(self, d):
        i = list(self.sources).index(d)
        return pltpu.make_async_copy(self.sources[d], self.block(d, self.place.q), self.own.at[i])

    def along(self, d):
        self.copy(("z", d)).start()

    def relay(self, d):
        if d in self.sources:
            self.own_copy(d).start()
        else:
            self.copy(("z", d)).wait_recv()
        self.copy(("x", d)).start()
        for m in self.ms:
            self.copy(("y", m, d)).start()

    def diag(self, d):
        self.copy(("x", d)).wait_recv()
        for m in self.ms:
            self.copy(("dy", m, d)).start()
        for m in self.ms:
            self.copy(("y", m, d)).wait_recv()
            self.copy(("dx", m, d)).start()

    def share(self, d):
        if d in self.sources:
            self.own_copy(d).wait()
        for m in self.ms:
            self.copy(("dy", m, d)).wait_recv()
            self.copy(("dx", m, d)).wait_recv()
        self.copy(("s", d)).start()

    def done(self, d):
        self.copy(("s", d)).wait_recv()

    def finish(self):
        for key in self.index:
            self.copy(key).wait_send()


def run_events(step, batches):
    for i, batch in enumerate(batches):
        if batch:

            @pl.when(step == i)
            def _():
                for event in batch:
                    event()


def cut(names, letter):
    parts = [[]]
    for name in names:
        if name[0] == letter:
            parts.append([])
        else:
            parts[-1].append(name)
    return parts


def orders(n_t, pairs, sub, group):
    if (n_t, pairs, sub, group) == (4, 2, 2, 2):
        return FRONT, MIDDLE
    near = n_t // 2
    late = list(reversed(range(near, n_t)))
    name = lambda letters, d: letters + str(d)
    front = ["G", "T", "er0", "xr0", "hr0", "or0", "A"]
    for d in range(1, n_t):
        front += [name(g, d) for g in (("ea", "oa", "xa", "ha") if d < near else ("ea", "oa"))]
    front += ["X", "H", "C"]
    every = lambda g, d: [name(g + a, d) for a in ("rds" if d else "ds")]
    for d in range(n_t):
        front += every("e", d)
    front += ["W", "g", "N"]
    for d in range(n_t):
        front += [name("R", d), name("P", d)]
    for d in range(n_t):
        front += every("o", d) + (every("x", d) + every("h", d) if d < near else [])
    for d in range(n_t):
        front += [name("V", d)] + [name("K", d * pairs + i) for i in range(pairs)]
    middle = []
    for g in "xh":
        middle += [name(g + "r", late[0])] + [name(g + "a", d) for d in late[1:]]
    middle += ["I"]
    for i in range(n_t * sub):
        middle += [name("F", i)]
        if i == 0:
            for d in late:
                for g in "xh":
                    middle += every(g, d)[1 if d == late[0] else 0 :]
        if (i + 1) % sub == 0 and near <= (i + 1) // sub < n_t:
            middle += [name("B", late[(i + 1) // sub - near])]
    return front, middle


FRONT = (
    "G", "ea1", "hr0", "er0", "xr0", "T", "A", "ed0", "ea2", "ea3", "hd0", "es0", "er1", "W", "g", "ed1",
    "xd0", "oa3", "N", "es1", "or0", "oa2", "er2", "R0", "xa1", "P0", "ha1", "R1", "er3", "V0", "od0", "K0",
    "oa1", "xs0", "ed2", "ed3", "or2", "P1", "xr1", "K1", "es2", "hr1", "C", "V1", "K2", "hs0", "R2", "P2",
    "or1", "es3", "K3", "hd1", "od2", "R3", "or3", "X", "od1", "P3", "V2", "K4", "V3", "os0", "hs1", "od3",
    "os2", "xd1", "K5", "os1", "H", "os3", "K6", "xs1", "K7",
)
MIDDLE = (
    "xa2", "xr3", "I", "hr3", "F0", "xd3", "xr2", "ha2", "F1", "hd3", "F2", "xd2", "xs3", "hs3", "hr2", "F3",
    "B3", "xs2", "hd2", "F4", "hs2", "F5", "B2", "F6", "F7",
)
STEPS = {"a": Gather.along, "r": Gather.relay, "d": Gather.diag, "s": Gather.share}


def move(place, source, target, sems, begin, rows=None):
    if rows is not None:
        source, target = source.at[rows], target.at[rows]

    @pl.when(place.stays)
    def _():
        here = pltpu.make_async_copy(source, target, sems[2])
        here.start() if begin else here.wait()

    @pl.when(jnp.logical_not(place.stays))
    def _():
        there = remote(source, target, sems[0], sems[1], place.partner)
        there.start() if begin else there.wait()


def head_masks(shape):
    lane = lax.broadcasted_iota(jnp.int32, shape, 1)
    return lane < HEAD_DIM, lane >= HEAD_DIM


def ones_lanes(rows, count):
    lane = lax.broadcasted_iota(jnp.int32, (rows, PAIR), 1)
    return jnp.where(lane < count, 1.0, 0.0).astype(BF)


def attend(queries, keys, values, o_ref, lse_ref):
    rows, length = queries.shape[0], keys.shape[0]
    values = jnp.concatenate([values, ones_lanes(length, 1)], axis=1)
    zero = jnp.zeros_like(queries)
    outs, sums = [], []
    both = [dot(jnp.where(mask, queries, zero), keys, 1, 1) for mask in head_masks(queries.shape)]
    for scores in both:
        top = jnp.max(scores, axis=1, keepdims=True)
        probs = jnp.exp2(scores - top).astype(BF)
        mixed = dot(probs, values, 1, 0)
        total = mixed[:, PAIR : PAIR + 1]
        outs.append(mixed[:, :PAIR] / total)
        sums.append(top + jnp.log2(total))
    first, _ = head_masks((rows, PAIR))
    o_ref[...] = jnp.where(first, outs[0], outs[1]).astype(BF)
    lse_ref[...] = jnp.where(first, sums[0], sums[1])


def front_kernel(
    n_dp, n_t, cap,
    choice_ref, count_ref, gain_ref, ed_tab, ou_tab, xd_tab, su_tab, eu_tab, od_tab, xu_tab, sd_tab,
    tokens_ref, cot_ref, w_ref, wo_ref, we_ref, ws_ref,
    o_ref, lse_ref, inner_t_ref, thin_out, rep_out,
    q_out, k_out, v_out, k_far_out, v_far_out, normed_out, tok_out, cot_out, w_full, wo_full, we_full, ws_full,
    we_land, ws_land,
    q, k, v, k_far, v_far, tok, cot, normed, thin, rep, thin_send, stage, inner,
    tok_sems, cot_sems, thin_sends, thin_recvs, rep_sems, stage_sems, kv_sends, kv_recvs, keep_sems, kept_sems,
    land_sems, go_sem, *sems,
):
    p = Place(n_dp, n_t, cap)
    step, steps = pl.program_id(0), pl.num_programs(0)
    cols, hid = od_tab.shape[-1], xu_tab.shape[-1]
    pairs = cols // PAIR
    depth = w_ref.shape[0] // 3
    early = list(range(n_t // 2))
    entry = Gather(p, {0: w_ref}, w_full, range(n_t), sems[0:3])
    out_g = Gather(p, {0: wo_ref}, wo_full, range(n_t), sems[3:6])
    exp_g = Gather(p, {0: we_ref}, we_full, early, sems[6:9])
    shr_g = Gather(p, {0: ws_ref}, ws_full, early, sems[9:12])
    both = (exp_g, shr_g)
    tok_three = [tok_sems.at[i] for i in range(3)]
    cot_three = [cot_sems.at[i] for i in range(3)]

    def thin_targets():
        for s in range(cap):
            for low in range(p.half):
                to = s * p.group + p.core * p.half + low
                for core in range(2):
                    i = (s * p.half + low) * 2 + core
                    elsewhere = jnp.logical_or(core != p.core, to != p.t)
                    yield s, to, core, i, elsewhere

    def send_thin(near):
        for s, to, core, i, elsewhere in thin_targets():
            d = (to + n_t - p.t) % n_t

            @pl.when(jnp.logical_and(elsewhere, (to == p.t) == near))
            def _():
                remote(
                    thin_send.at[s], thin.at[d], thin_sends.at[i], thin_recvs.at[d], (p.dp - p.core + core, to)
                ).start()

    def send_adapters():
        for s in range(cap):
            a = choice_ref[s]
            for i in range(3):
                thin_send[s, :, i * cols : (i + 1) * cols] = eu_tab[a, i]
            thin_send[s, :, 3 * cols : 4 * cols] = od_tab[a]
            thin_send[s, :, 4 * cols : 4 * cols + hid] = xu_tab[a]
            thin_send[s, :, 4 * cols + hid :] = sd_tab[a]
        send_thin(True)

        @pl.when(p.stays)
        def _():
            a = choice_ref[p.slot]
            for i, table in enumerate((ed_tab, ou_tab, xd_tab, su_tab)):
                rep[i * RANK : (i + 1) * RANK] = table[a]
            row = lax.broadcasted_iota(jnp.int32, (RANK, rep.shape[1]), 0)
            alive = jnp.where(p.slot < count_ref[0], 1.0, 0.0)
            rep[4 * RANK :] = jnp.where(row < RANK // 2, alive, a.astype(F32)).astype(BF)
            remote(rep, rep, rep_sems.at[0], rep_sems.at[1], p.sibling).start()
            thin[0] = thin_send[p.slot]

    def take_near():
        @pl.when(jnp.logical_not(p.stays))
        def _():
            remote(rep, rep, rep_sems.at[0], rep_sems.at[1], p.sibling).wait_recv()
            remote(thin_send.at[0], thin.at[0], thin_sends.at[0], thin_recvs.at[0], p.sibling).wait_recv()

        rep_out[...] = rep[...]
        thin_out[0] = thin[0]

    def take_thin(d):
        remote(thin_send.at[0], thin.at[d], thin_sends.at[0], thin_recvs.at[d], p.sibling).wait_recv()
        thin_out[d] = thin[d]

    def load(d):
        return pltpu.make_async_copy(w_full.at[d], stage.at[d % 2], stage_sems.at[d % 2])

    def kept():
        return [pltpu.make_async_copy(tok, tok_out, keep_sems.at[0]), pltpu.make_async_copy(normed, normed_out, keep_sems.at[1])]

    def first_norm():
        hat, _ = norm_parts(tok[...].astype(F32))
        value = (hat * gain_ref[...]).astype(BF)
        normed[...] = value
        down = rep[:RANK]
        inner[...] = dot(value, down, 1, 1).astype(BF)
        inner_t_ref[...] = dot(down, value, 1, 1).astype(BF)
        for copy in kept():
            copy.start()

    def far_copy(d, which, m):
        source, target = ((k, k_far), (v, v_far))[which]
        device = p.mate(m)
        there = (d + device[1] + n_t - p.t) % n_t
        return remote(
            source.at[pl.ds(d * pairs, pairs)], target.at[m - 1, pl.ds(there * pairs, pairs)],
            kv_sends.at[d, which, m - 1], kv_recvs.at[there, which, m - 1], device,
        )

    def far_arrival(d, which, m):
        source, target = ((k, k_far), (v, v_far))[which]
        return remote(
            source.at[pl.ds(d * pairs, pairs)], target.at[m - 1, pl.ds(d * pairs, pairs)],
            kv_sends.at[d, which, m - 1], kv_recvs.at[d, which, m - 1], p.mate(m),
        )

    def project(d):
        load(d).wait()
        for which, out in ((1, k), (2, v), (0, q)):
            weights = stage[d % 2, :, :, which * depth : (which + 1) * depth].reshape(n_dp * depth, cols)
            part = dot(normed[...], weights, 1, 0)
            part = part + dot(inner[...], thin[d, :, which * cols : (which + 1) * cols], 1, 0)
            if which == 0:
                part = part * (HEAD_DIM**-0.5 * LOG2E)
            part = part.astype(BF)
            for i in range(pairs):
                out[d * pairs + i] = part[:, i * PAIR : (i + 1) * PAIR]
            if which:
                for m in range(1, p.group):
                    far_copy(d, which - 1, m).start()

    def copies_out(d):
        at = pl.ds(d * pairs, pairs)
        found = [(a.at[at], b.at[at]) for a, b in ((q, q_out), (k, k_out), (v, v_out))]
        for a, b in ((k_far, k_far_out), (v_far, v_far_out)):
            found += [(a.at[m, at], b.at[m, at]) for m in range(p.group - 1)]
        return [pltpu.make_async_copy(a, b, kept_sems.at[d, i]) for i, (a, b) in enumerate(found)]

    def arrive(d):
        for m in range(1, p.group):
            far_arrival(d, 0, m).wait_recv()
            far_arrival(d, 1, m).wait_recv()
        for copy in copies_out(d):
            copy.start()

    def land(i):
        source, target = ((we_ref, we_land), (ws_ref, ws_land))[i]
        return remote(source, target, land_sems.at[0, i], land_sems.at[1, i], (p.dp, p.along(n_t - 1)))

    def ready(d):
        if d:
            take_thin(d)
        entry.done(d)
        load(d).start()

    def go():
        @pl.when(jnp.logical_not(p.stays))
        def _():
            pl.semaphore_signal(go_sem, inc=1, device_id=p.sibling, device_id_type=MESH)

        @pl.when(p.stays)
        def _():
            pl.semaphore_wait(go_sem, 1)

    def arrived():
        move(p, tokens_ref, tok, tok_three, False)
        send_thin(False)

    def norm():
        take_near()
        first_norm()

    def opened():
        greet(p.gather_peers() + p.other_core_peers())

    gathers = {"e": entry, "x": exp_g, "h": shr_g, "o": out_g}
    plain = {
        "G": opened, "g": go, "W": arrived, "N": norm, "A": send_adapters,
        "T": lambda: move(p, tokens_ref, tok, tok_three, True), "C": lambda: move(p, cot_ref, cot, cot_three, True),
        "X": lambda: land(0).start(), "H": lambda: land(1).start(),
    }
    counted = {"R": ready, "P": project, "V": arrive}

    def event(name):
        if len(name) == 1:
            return plain[name]
        if len(name) == 2:
            return lambda: counted[name[0]](int(name[1]))
        return lambda: STEPS[name[1]](gathers[name[0]], int(name[2]))

    names = orders(n_t, pairs, max(1, hid // 512), p.group)[0]
    parts = cut(names, "K")
    closing = [event(name) for name in parts.pop()]
    first = ["P0" in part or sum(name[0] == "P" for name in part) > 1 for part in parts]
    single = {}
    before, after = [], []
    for i, part in enumerate(parts):
        places = [] if first[i] else [j for j, name in enumerate(part) if name[0] == "P"]
        at = places[0] if places else len(part)
        if places:
            single[i] = int(part[at][1])
        before.append([event(name) for name in part[:at]])
        after.append([event(name) for name in part[at + 1 :]])
    run_events(step, before)
    if single:
        chunk = sum(jnp.where(step == i, d, 0) for i, d in single.items())

        @pl.when(chunk > 0)
        def _():
            project(chunk)

    run_events(step, after)
    keys = jnp.concatenate([k[step]] + [k_far[m, step] for m in range(p.group - 1)], axis=0)
    values = jnp.concatenate([v[step]] + [v_far[m, step] for m in range(p.group - 1)], axis=0)
    attend(q[step], keys, values, o_ref, lse_ref)

    @pl.when(step == steps - 1)
    def _():
        for call in closing:
            call()
        for g in (exp_g, shr_g, out_g):
            for d in g.ds:
                g.done(d)
        for g in (entry, exp_g, shr_g, out_g):
            g.finish()
        for i in range(2):
            land(i).wait()
        move(p, cot_ref, cot, cot_three, False)
        keep_cot = pltpu.make_async_copy(cot, cot_out, keep_sems.at[2])
        keep_cot.start()

        @pl.when(p.stays)
        def _():
            remote(rep, rep, rep_sems.at[0], rep_sems.at[1], p.sibling).wait_send()

        for s, to, core, i, elsewhere in thin_targets():

            @pl.when(elsewhere)
            def _():
                remote(thin_send.at[s], thin.at[0], thin_sends.at[i], thin_recvs.at[0], p.sibling).wait_send()

        for copy in [keep_cot, *kept()]:
            copy.wait()
        for d in range(n_t):
            for m in range(1, p.group):
                far_copy(d, 0, m).wait_send()
                far_copy(d, 1, m).wait_send()
            for copy in copies_out(d):
                copy.wait()


def front_part(cap, choice, count, gain, rep_tables, thin_tables, tokens, cot, w, wo, we, ws):
    n_dp, n_t = lax.axis_size("dp"), lax.axis_size("tensor")
    rows, width = tokens.shape
    cols = wo.shape[-1]
    others = n_t // cap - 1
    count_pairs = width // PAIR
    early = n_t // 2
    thin_width = 4 * cols + 2 * we.shape[-1]
    shape, vmem = jax.ShapeDtypeStruct, pltpu.VMEM
    whole = lambda *s: pl.BlockSpec(s, lambda h: (0,) * len(s))
    pair = pl.BlockSpec((None, rows, PAIR), lambda h: (h, 0, 0))
    full = lambda n, a: shape((n, n_dp // 2, 2, *a.shape), BF)
    heads, far = (count_pairs, rows, PAIR), (others, count_pairs, rows, PAIR)
    small = [(RANK, rows), (n_t, RANK, thin_width), (5 * RANK, width)]
    return pl.pallas_call(
        functools.partial(front_kernel, n_dp, n_t, cap),
        grid=(count_pairs,),
        in_specs=[IN_SMEM, IN_SMEM] + [whole(*a.shape) for a in (gain, *rep_tables, *thin_tables)]
        + [ANY] * 2 + [whole(*a.shape) for a in (w, wo, we, ws)],
        out_specs=[pair, pair] + [whole(*s) for s in small] + [ANY] * 14,
        out_shape=[shape(heads, BF), shape(heads, F32)] + [shape(s, BF) for s in small]
        + [shape(heads, BF)] * 3 + [shape(far, BF)] * 2 + [shape((rows, width), BF)] * 3
        + [full(n_t, w), full(n_t, wo), full(early, we), full(early, ws), shape(we.shape, BF), shape(ws.shape, BF)],
        scratch_shapes=[
            vmem(heads, BF), vmem(heads, BF), vmem(heads, BF), vmem(far, BF), vmem(far, BF),
            vmem((rows, width), BF), vmem((rows, width), BF), vmem((rows, width), BF), vmem(small[1], BF), vmem(small[2], BF),
            vmem((cap, RANK, thin_width), BF),
            vmem((2, n_dp // 2, 2, *w.shape), BF), vmem((rows, RANK), BF),
            DMA((3,)), DMA((3,)), DMA((n_t,)), DMA((n_t,)), DMA((2,)), DMA((2,)),
            DMA((n_t, 2, others)), DMA((n_t, 2, others)), DMA((3,)), DMA((n_t, 3 + 2 * others)), DMA((2, 2)),
            pltpu.SemaphoreType.REGULAR,
            *Gather.scratch(n_dp, range(n_t)), *Gather.scratch(n_dp, range(n_t)),
            *Gather.scratch(n_dp, range(early)), *Gather.scratch(n_dp, range(early)),
        ],
        compiler_params=params(collective_id=0, has_side_effects=True),
        name="front_part",
    )(choice, count, gain, *rep_tables, *thin_tables, tokens, cot, w, wo, we, ws)


def split_lanes(column):
    column = -column
    high = column.astype(BF)
    rest = column - high.astype(F32)
    mid = rest.astype(BF)
    low = (rest - mid.astype(F32)).astype(BF)
    lane = lax.broadcasted_iota(jnp.int32, (column.shape[0], PAIR), 1)
    zero = jnp.zeros((column.shape[0], PAIR), BF)
    return jnp.where(lane == 0, high, jnp.where(lane == 1, mid, jnp.where(lane == 2, low, zero)))


def back_kernel(
    n_dp, n_t, cap, tiles,
    q_ref, k_ref, k_far, v_ref, v_far, o_ref, lse_ref, do_ref, gain_ref, rep_ref, thin_ref, inner_t_ref, grads_ref,
    mixed_ref, w_ref, mgrad_ref, tok_ref, normed_ref,
    mixed_out, mid_full, tgrad_out, end_full,
    grad, send, far, mixed, weights, mgrad, tok, normed, back_sum, row_sum, back_low, tgrad, end, sends, recvs, swap, swaps, load_sems,
    *sems,
):
    p = Place(n_dp, n_t, cap)
    step, steps = pl.program_id(0), pl.num_programs(0)
    rows = q_ref.shape[0]
    pairs = grad.shape[1] // n_t
    cols = w_ref.shape[-1]
    depth = w_ref.shape[-2] // 3
    width = tok_ref.shape[1]
    mid_g = Gather(
        p, {0: grads_ref.at[0]}, mid_full, range(n_t), sems[0:3],
        spread=lambda d: grads_ref.at[n_t - d], by_rows=False,
    )
    end_g = Gather(
        p, {0: end.at[0]}, end_full, range(n_t), sems[3:6], spread=lambda d: end.at[n_t - d], by_rows=False
    )
    swap_sems = [swap.at[i] for i in range(3)]
    loads = [
        pltpu.make_async_copy(src, dst, load_sems.at[i])
        for i, (src, dst) in enumerate(((w_ref, weights), (normed_ref, normed), (tok_ref, tok), (mgrad_ref, mgrad)))
    ]
    relay, diag, share = ((lambda d, f=f: lambda: f(d)) for f in (mid_g.relay, mid_g.diag, mid_g.share))
    start_swap = lambda: move(p, mixed_ref, mixed, swap_sems, True)
    start_loads = lambda: [copy.start() for copy in loads]

    def opening():
        greet(p.gather_peers() + p.other_core_peers())
        mid_g.relay(0)
        for d in range(1, n_t):
            mid_g.along(d)

    if n_t == 4:
        table = {
            0: [opening], 1: [diag(0), relay(1)], 2: [share(0), diag(1), relay(2), start_swap],
            3: [share(1), diag(2), relay(3)], 4: [share(2), diag(3), start_loads], 5: [share(3)],
        }
    else:
        table = {0: [opening, start_swap, start_loads, diag(0), share(0)]}
        for d in range(1, n_t):
            table[0] += [relay(d), diag(d), share(d)]
    run_events(step, [table.get(i, []) for i in range(max(table) + 1)])

    with_far = lambda near, far: jnp.concatenate([near[...]] + [far[m] for m in range(p.group - 1)], axis=0)
    keys = with_far(k_ref, k_far)
    length = keys.shape[0]
    ones = ones_lanes(length, 3)
    keys_more = jnp.concatenate([keys, ones], axis=1)
    values_more = jnp.concatenate([with_far(v_ref, v_far), ones], axis=1)
    queries, grad_out = q_ref[...], do_ref[...]
    zero = jnp.zeros_like(queries)
    product = grad_out.astype(F32) * o_ref[...].astype(F32)
    d_queries, both = [], [[], [], [], []]
    for head, mask in enumerate(head_masks(queries.shape)):
        query = jnp.where(mask, queries, zero)
        grad_head = jnp.where(mask, grad_out, zero)
        lse = lse_ref[:, head * HEAD_DIM : head * HEAD_DIM + 1]
        delta = jnp.sum(jnp.where(mask, product, 0.0), axis=1, keepdims=True)
        probs = jnp.exp2(dot(jnp.concatenate([query, split_lanes(lse)], axis=1), keys_more, 1, 1))
        slope = dot(jnp.concatenate([grad_head, split_lanes(delta)], axis=1), values_more, 1, 1)
        score_grad = (probs * slope).astype(BF)
        d_queries.append(dot(score_grad, keys, 1, 0))
        for kept, one in zip(both, (grad_head, probs.astype(BF), query, score_grad)):
            kept.append(one)
    grad_heads, probs, query, score_grad = [jnp.concatenate(kept, axis=0) for kept in both]
    d_values = dot(grad_heads, probs, 0, 0)
    d_keys = dot(query, score_grad, 0, 0)
    first, _ = head_masks((rows, PAIR))
    grad[0, step] = (jnp.where(first, d_queries[0], d_queries[1]) * HEAD_DIM**-0.5).astype(BF)
    d_keys = (d_keys * LN2).T.astype(BF)
    d_values = d_values.T.astype(BF)
    grad[1, step] = d_keys[:rows]
    grad[2, step] = d_values[:rows]

    def far_copy(i, m, h):
        device = p.mate(p.group - m)
        there = (h // pairs + device[1] + n_t - p.t) % n_t * pairs + h % pairs
        return remote(
            send.at[i, m - 1, h], far.at[i, m - 1, there], sends.at[i, m - 1, h], recvs.at[i, m - 1, there], device
        )

    for m in range(1, p.group):
        send[0, m - 1, step] = d_keys[m * rows : (m + 1) * rows]
        send[1, m - 1, step] = d_values[m * rows : (m + 1) * rows]
        far_copy(0, m, step).start()
        far_copy(1, m, step).start()

    @pl.when(step == steps - 1)
    def _():
        move(p, mixed_ref, mixed, swap_sems, False)
        keep = pltpu.make_async_copy(mixed, mixed_out, swap.at[3])
        keep.start()
        for i in range(2):
            for m in range(1, p.group):
                for h in range(n_t * pairs):
                    remote(
                        send.at[i, m - 1, h], far.at[i, m - 1, h], sends.at[i, m - 1, h], recvs.at[i, m - 1, h], p.sibling
                    ).wait_recv()

            @pl.loop(0, steps)
            def _(h):
                total = grad[1 + i, h].astype(F32)
                for m in range(p.group - 1):
                    total = total + far[i, m, h].astype(F32)
                grad[1 + i, h] = total.astype(BF)

        columns = lambda which, d, rows: jnp.concatenate(
            [grad[which, d * pairs + i, rows] for i in range(pairs)], axis=1
        )
        chunks = n_t * 3
        back_sum[...] = jnp.zeros_like(back_sum)

        @pl.loop(0, chunks)
        def _(j):
            d, at = j // 3, pl.ds(pl.multiple_of(j % 3 * cols, cols), cols)
            part = columns(j % 3, d, slice(None))
            back_sum[...] += dot(part, thin_ref[d, :, at], 1, 1)
            end[d, :, at] = dot(inner_t_ref[...], part, 1, 0).astype(BF)

        back_low[...] = back_sum[...].astype(BF)
        loads[1].wait()
        down_grad = dot(back_low[...], normed[...], 0, 0).astype(BF)
        for d in range(n_t):
            end[d, :, 3 * cols :] = down_grad
        end_g.relay(0)
        for d in range(1, n_t):
            end_g.along(d)
        for copy in (loads[0], *loads[2:]):
            copy.wait()

        def tile(n):
            start, count = tiles[n]
            rows = pl.ds(start, count)
            acc = row_sum.at[pl.ds(0, count)]
            acc[...] = dot(back_low[rows], rep_ref[:RANK], 1, 0)

            @pl.loop(0, chunks)
            def _(j):
                at = pl.ds(pl.multiple_of(j % 3 * depth, depth), depth)
                piece = weights[j // 3, :, :, at].reshape(width, cols)
                acc[...] += dot(columns(j % 3, j // 3, rows), piece, 1, 1)

            total = acc[...]
            hat, scale = norm_parts(tok[rows].astype(F32))
            tgrad[rows] = (mgrad[rows] + norm_back(hat, scale, gain_ref[...], total)).astype(BF)
            move(p, tgrad, tgrad_out, [swaps.at[n, i] for i in range(3)], True, rows)

        for n in range(len(tiles)):
            tile(n)
            if n == 0:
                end_g.diag(0)
                end_g.relay(1)
            if n == min(1, len(tiles) - 1):
                for d in range(2, n_t):
                    end_g.relay(d)
                end_g.share(0)
                end_g.diag(1)
        for d in range(2, n_t):
            end_g.diag(d)
            end_g.share(d - 1)
        end_g.share(n_t - 1)
        for d in range(n_t):
            mid_g.done(d)
            end_g.done(d)
        mid_g.finish()
        end_g.finish()
        for n, (start, count) in enumerate(tiles):
            move(p, tgrad, tgrad_out, [swaps.at[n, i] for i in range(3)], False, pl.ds(start, count))

        @pl.loop(0, steps)
        def _(h):
            for m in range(1, p.group):
                for i in range(2):
                    far_copy(i, m, h).wait_send()

        keep.wait()


def back_part(cap, q, k, k_far, v, v_far, o, lse, do, gain, rep, thin, inner_t, grads, mixed, w_full, mgrad, tok, normed):
    n_dp, n_t = lax.axis_size("dp"), lax.axis_size("tensor")
    heads, rows, _ = q.shape
    width, cols = tok.shape[1], w_full.shape[-1]
    others = k_far.shape[0]
    pair = pl.BlockSpec((None, rows, PAIR), lambda h: (h, 0, 0))
    far = pl.BlockSpec((others, None, rows, PAIR), lambda h: (0, h, 0, 0))
    whole = lambda a: pl.BlockSpec(a.shape, lambda h: (0,) * len(a.shape))
    shape, vmem = jax.ShapeDtypeStruct, pltpu.VMEM
    count = (2, others, heads)
    number = 3 if rows % 16 == 0 else 1
    size = rows // number // 16 * 16 if number > 1 else rows
    tiles = [(0, rows - size * (number - 1))]
    tiles += [(tiles[0][1] + size * i, size) for i in range(number - 1)]
    end_width = 3 * cols + width
    full = lambda n: shape((n_t, n_dp // 2, 2, RANK, n), BF)
    return pl.pallas_call(
        functools.partial(back_kernel, n_dp, n_t, cap, tiles),
        grid=(heads,),
        in_specs=[pair, pair, far, pair, far, pair, pair, pair]
        + [whole(a) for a in (gain, rep, thin, inner_t, grads)] + [ANY] * 5,
        out_specs=[ANY] * 4,
        out_shape=[shape(mixed.shape, BF), full(grads.shape[-1]), shape(tok.shape, BF), full(end_width)],
        scratch_shapes=[
            vmem((3, heads, rows, PAIR), BF), vmem((2, *k_far.shape), BF), vmem((2, *k_far.shape), BF),
            vmem(mixed.shape, BF), vmem(w_full.shape, BF), vmem(mgrad.shape, F32), vmem(tok.shape, BF),
            vmem(tok.shape, BF), vmem((rows, RANK), F32), vmem((tiles[0][1], width), F32), vmem((rows, RANK), BF),
            vmem(tok.shape, BF), vmem((n_t, RANK, end_width), BF),
            DMA(count), DMA(count), DMA((4,)), DMA((len(tiles), 3)), DMA((4,)),
            *Gather.scratch(n_dp, range(n_t)), *Gather.scratch(n_dp, range(n_t)),
        ],
        compiler_params=params(collective_id=1, has_side_effects=True),
        name="back_part",
    )(q, k, k_far, v, v_far, o, lse, do, gain, rep, thin, inner_t, grads, mixed, w_full, mgrad, tok, normed)


def gelu_parts(hidden):
    share = 0.5 * (1.0 + lax.erf(hidden * 0.7071067811865476))
    density = jnp.exp(-0.5 * hidden * hidden) * 0.3989422804014327
    return hidden * share, share + hidden * density


def middle_kernel(
    n_dp, n_t, cap, sub,
    x_ref, att_ref, cot_ref, gain_ref, rep_ref, thin_ref, wo_ref, we_near, ws_near, we_land, ws_land, we_ref, ws_ref,
    mixed_ref, mgrad_ref, agrad_ref, grads_ref, we_full, ws_full,
    middle_ref, second_ref, dy_ref, acc2_ref, acc3_ref, einner_ref, einner_t_ref, sback_ref, sback_t_ref,
    sinner_ref, eback_ref, oinner_ref, we_buf, ws_buf, buf_sems, *sems,
):
    p = Place(n_dp, n_t, cap)
    step, steps = pl.program_id(0), pl.num_programs(0)
    cols = wo_ref.shape[-1]
    width = x_ref.shape[1]
    hid = we_ref.shape[-1]
    size = hid // sub
    near = n_t // 2
    late = list(reversed(range(near, n_t)))
    exp_g = Gather(p, {n_t - 1: we_land}, we_full, late, sems[0:3], spread=lambda d: we_ref)
    shr_g = Gather(p, {n_t - 1: ws_land}, ws_full, late, sems[3:6], spread=lambda d: ws_ref)
    pairs = cols // PAIR
    both = (exp_g, shr_g)
    down_e, up_o, up_s = rep_ref[2 * RANK : 3 * RANK], rep_ref[RANK : 2 * RANK], rep_ref[3 * RANK : 4 * RANK]
    alive = rep_ref[4 * RANK : 4 * RANK + 1, 0:1].astype(F32)
    at_od, at_eu = 3 * width, 3 * width + cols
    at_sd, at_id = at_eu + hid, at_eu + 2 * hid

    def load(i):
        index, part = i // sub, i % sub
        at = pl.ds(part * size, size)
        pair = (we_near, ws_near) if index < near else (we_full, ws_full)
        index = index if index < near else index - near
        return [
            pltpu.make_async_copy(src.at[index, :, :, :, at], buf.at[i % 3], buf_sems.at[i % 3, j])
            for j, (src, buf) in enumerate(zip(pair, (we_buf, ws_buf)))
        ]

    gathers = {"x": exp_g, "h": shr_g}

    def bring(d):
        exp_g.done(d)
        shr_g.done(d)
        for i in range(sub):
            for copy in load((near + late.index(d)) * sub + i):
                copy.start()

    def event(name):
        if len(name) == 2:
            return lambda: bring(int(name[1]))
        return lambda: STEPS[name[1]](gathers[name[0]], int(name[2]))

    names = orders(n_t, pairs, sub, p.group)[1]
    begun = names.index("I")
    start = [event(name) for name in names[:begun]]
    opening, *after = [[event(name) for name in part] for part in cut(names[begun + 1 :], "F")]
    columns = lambda d: jnp.concatenate([att_ref[d * pairs + i] for i in range(pairs)], axis=1)

    @pl.when(step == 0)
    def _():
        greet(p.gather_peers())
        for call in start:
            call()
        for i in range(2):
            for copy in load(i):
                copy.start()
        branch, inner = 0.0, 0.0
        for d in range(n_t):
            att = columns(d)
            branch = branch + dot(att, wo_ref[d].reshape(width, cols), 1, 1)
            inner = inner + dot(att, thin_ref[d, :, 3 * cols : 4 * cols], 1, 1)
        inner = inner.astype(BF)
        oinner_ref[...] = inner
        middle = x_ref[...].astype(F32) + (branch + dot(inner, up_o, 1, 0))
        middle_ref[...] = middle
        hat, _ = norm_parts(middle)
        second = (hat * gain_ref[...]).astype(BF)
        second_ref[...] = second
        dy = (cot_ref[...].astype(F32) * alive).astype(BF)
        dy_ref[...] = dy
        einner_ref[...] = dot(second, down_e, 1, 1).astype(BF)
        einner_t_ref[...] = dot(down_e, second, 1, 1).astype(BF)
        sback_ref[...] = dot(dy, up_s, 1, 1).astype(BF)
        sback_t_ref[...] = dot(up_s, dy, 1, 1).astype(BF)
        acc2_ref[...] = jnp.zeros_like(acc2_ref)
        acc3_ref[...] = jnp.zeros_like(acc3_ref)
        sinner_ref[...] = jnp.zeros_like(sinner_ref)
        eback_ref[...] = jnp.zeros_like(eback_ref)

    run_events(step, [opening])
    for i in range(n_t * sub):

        @pl.when(step == i)
        def _():
            for copy in load(i):
                copy.wait()
            if i + 2 < near * sub:
                for copy in load(i + 2):
                    copy.start()

    buf = step % 3
    d, part = step // sub, step % sub
    d = jnp.where(d < near, d, n_t - 1 + near - d)
    we, ws = we_buf[buf].reshape(width, size), ws_buf[buf].reshape(width, size)
    at = pl.multiple_of(part * size, size)
    e_up = thin_ref[d, :, pl.ds(4 * cols + at, size)]
    s_down = thin_ref[d, :, pl.ds(4 * cols + hid + at, size)]
    hidden = dot(second_ref[...], we, 1, 0) + dot(einner_ref[...], e_up, 1, 0)
    value, slope = gelu_parts(hidden)
    act = value.astype(BF)
    acc2_ref[...] += dot(act, ws, 1, 1)
    sinner_ref[...] += dot(act, s_down, 1, 1)
    act_grad = dot(dy_ref[...], ws, 1, 0) + dot(sback_ref[...], s_down, 1, 0)
    hid_grad = (act_grad * slope).astype(BF)
    acc3_ref[...] += dot(hid_grad, we, 1, 1)
    eback_ref[...] += dot(hid_grad, e_up, 1, 1)
    grads_ref[d, :, pl.ds(at_eu + at, size)] = dot(einner_t_ref[...], hid_grad, 1, 0).astype(BF)
    grads_ref[d, :, pl.ds(at_sd + at, size)] = dot(sback_t_ref[...], act, 1, 0).astype(BF)

    run_events(step, after)
    @pl.when(step == steps - 1)
    def _():
        s_inner, e_back = sinner_ref[...].astype(BF), eback_ref[...].astype(BF)
        middle = middle_ref[...]
        mixed_ref[...] = (alive * (middle + (acc2_ref[...] + dot(s_inner, up_s, 1, 0)))).astype(BF)
        shrink_up = dot(s_inner, dy_ref[...], 0, 0).astype(BF)
        expand_down = dot(e_back, second_ref[...], 0, 0).astype(BF)
        second_grad = acc3_ref[...] + dot(e_back, down_e, 1, 0)
        hat, scale = norm_parts(middle)
        mgrad = cot_ref[...].astype(F32) * alive + norm_back(hat, scale, gain_ref[...], second_grad)
        mgrad_ref[...] = mgrad
        low = mgrad.astype(BF)
        o_back = dot(low, up_o, 1, 1).astype(BF)
        output_up = dot(oinner_ref[...], low, 0, 0).astype(BF)
        for d in range(n_t):
            agrad = dot(low, wo_ref[d].reshape(width, cols), 1, 0)
            agrad = (agrad + dot(o_back, thin_ref[d, :, 3 * cols : 4 * cols], 1, 0)).astype(BF)
            for i in range(pairs):
                agrad_ref[d * pairs + i] = agrad[:, i * PAIR : (i + 1) * PAIR]
            grads_ref[d, :, :width] = expand_down
            grads_ref[d, :, width : 2 * width] = shrink_up
            grads_ref[d, :, 2 * width : 3 * width] = output_up
            grads_ref[d, :, at_od : at_od + cols] = dot(o_back, columns(d), 0, 0).astype(BF)
            grads_ref[d, :, at_id:] = rep_ref[4 * RANK :, : grads_ref.shape[2] - at_id]
        for g in both:
            g.finish()


ID_LANES = 128


def middle_both_ways(cap, x, att, cot, gain, rep, thin, wo_full, we_near, ws_near, we_land, ws_land, we, ws):
    n_dp, n_t = lax.axis_size("dp"), lax.axis_size("tensor")
    rows, width = x.shape
    depth, hid = we.shape
    cols = wo_full.shape[-1]
    sub = max(1, hid // 512)
    size = hid // sub
    late = list(reversed(range(n_t // 2, n_t)))
    grad_width = 3 * width + cols + 2 * hid + ID_LANES
    whole = lambda a: pl.BlockSpec(a.shape, lambda i: (0,) * len(a.shape))
    shape = jax.ShapeDtypeStruct
    full = shape((len(late), n_dp // 2, 2, depth, hid), BF)
    outs = [
        shape((rows, width), BF), shape((rows, width), F32), shape(att.shape, BF),
        shape((n_t, RANK, grad_width), BF),
    ]
    vmem = pltpu.VMEM
    return pl.pallas_call(
        functools.partial(middle_kernel, n_dp, n_t, cap, sub),
        grid=(n_t * sub,),
        in_specs=[whole(a) for a in (x, att, cot, gain, rep, thin, wo_full)]
        + [ANY] * 2 + [whole(we_land), whole(ws_land)] + [ANY] * 2,
        out_specs=[whole(a) for a in outs] + [ANY] * 2,
        out_shape=outs + [full, full],
        scratch_shapes=[
            vmem((rows, width), F32), vmem((rows, width), BF), vmem((rows, width), BF),
            vmem((rows, width), F32), vmem((rows, width), F32),
            vmem((rows, RANK), BF), vmem((RANK, rows), BF), vmem((rows, RANK), BF), vmem((RANK, rows), BF),
            vmem((rows, RANK), F32), vmem((rows, RANK), F32), vmem((rows, RANK), BF),
            vmem((3, n_dp // 2, 2, depth, size), BF), vmem((3, n_dp // 2, 2, depth, size), BF), DMA((3, 2)),
            *Gather.scratch(n_dp, late, late[:1]), *Gather.scratch(n_dp, late, late[:1]),
        ],
        compiler_params=params(collective_id=2, has_side_effects=True),
        name="middle_both_ways",
    )(x, att, cot, gain, rep, thin, wo_full, we_near, ws_near, we_land, ws_land, we, ws)


def sum_kernel(
    width, cols, hid, mid_ref, end_ref, entry_down, entry_up, output_down, output_up, expand_down, expand_up,
    shrink_down, shrink_up,
):
    outs = (entry_down, entry_up, output_down, output_up, expand_down, expand_up, shrink_down, shrink_up)

    @pl.when(pl.program_id(0) == 0)
    def _():
        for out in outs:
            out[...] = jnp.zeros_like(out)

    sources = range(mid_ref.shape[0])
    at_id = 3 * width + cols + 2 * hid
    chosen = [jnp.max(mid_ref[i, RANK // 2 :, at_id : at_id + 128].astype(F32)).astype(jnp.int32) for i in sources]
    for i in sources:
        a = chosen[i]
        take = lambda ref, at, size: ref[i, :, at : at + size].astype(F32)
        expand_down[a] += take(mid_ref, 0, width)
        shrink_up[a] += take(mid_ref, width, width)
        output_up[a] += take(mid_ref, 2 * width, width)
        output_down[a] += take(mid_ref, 3 * width, cols)
        expand_up[a] += take(mid_ref, 3 * width + cols, hid)
        shrink_down[a] += take(mid_ref, 3 * width + cols + hid, hid)
        for which in range(3):
            entry_up[a, which] += take(end_ref, which * cols, cols)
        entry_down[a] += take(end_ref, 3 * cols, width)


def sum_gradients(adapters, cols, hid, width, mid, end):
    shape = jax.ShapeDtypeStruct
    wide = shape((adapters, RANK, width), F32)
    flat = lambda a: a.reshape(a.shape[0], -1, *a.shape[-2:])
    mid, end = flat(mid), flat(end)
    outs = [
        wide, shape((adapters, 3, RANK, cols), F32), shape((adapters, RANK, cols), F32), wide,
        wide, shape((adapters, RANK, hid), F32), shape((adapters, RANK, hid), F32), wide,
    ]
    part = lambda a: pl.BlockSpec((None, *a.shape[1:]), lambda i: (i, 0, 0, 0))
    return pl.pallas_call(
        functools.partial(sum_kernel, width, cols, hid),
        grid=(mid.shape[0],),
        in_specs=[part(mid), part(end)],
        out_specs=[pl.BlockSpec(a.shape, lambda i, n=len(a.shape): (0,) * n) for a in outs],
        out_shape=outs,
        compiler_params=params(),
        name="sum_gradients",
    )(mid, end)


def local(
    tokens, cotangent, norm_first, norm_second, entry_weight, output_weight, expand_weight, shrink_weight,
    entry_down, entry_up, output_down, output_up, expand_down, expand_up, shrink_down, shrink_up,
    adapter_choice, clip_count,
):
    cap = adapter_choice.shape[0]
    rows, width = tokens.shape
    adapters = entry_down.shape[0]
    cols, hid = output_weight.shape[1], expand_weight.shape[1]
    gain_first, gain_second = norm_first.reshape(1, width), norm_second.reshape(1, width)
    flip = lambda a: a.transpose(0, 2, 1)
    w_entry = entry_weight.transpose(1, 0, 2).reshape(-1, cols)
    (
        att, lse, inner_t, thin, rep, q, k, v, k_far, v_far, normed, tok, cot, w_full, wo_full, we_near, ws_near,
        we_land, ws_land,
    ) = front_part(
        cap, adapter_choice, clip_count, gain_first,
        (flip(entry_down), output_up, flip(expand_down), shrink_up),
        (entry_up.transpose(0, 2, 1, 3), flip(output_down), expand_up, flip(shrink_down)),
        tokens, cotangent, w_entry, output_weight, expand_weight, shrink_weight,
    )
    mixed, mgrad, agrad, grads, _, _ = middle_both_ways(
        cap, tok, att, cot, gain_second, rep, thin, wo_full, we_near, ws_near, we_land, ws_land,
        expand_weight, shrink_weight,
    )
    mixed, mid_grads, token_grad, end_grads = back_part(
        cap, q, k, k_far, v, v_far, att, lse, agrad, gain_first, rep, thin, inner_t, grads, mixed, w_full, mgrad, tok,
        normed,
    )
    ed, eu, od, ou, xd, xu, sd, su = sum_gradients(adapters, cols, hid, width, mid_grads, end_grads)
    return (
        mixed, token_grad, flip(ed), eu.transpose(0, 2, 1, 3), flip(od), ou, flip(xd), xu, flip(sd), su,
    )


def solution(mesh):
    in_specs = (
        P(BOTH, None), P(BOTH, None), P(), P(),
        P("dp", None, "tensor"), P("dp", "tensor"), P("dp", "tensor"), P("dp", "tensor"),
        P(), P(None, None, None, "tensor"), P(None, "tensor", None), P(),
        P(), P(None, None, "tensor"), P(None, "tensor", None), P(), P("dp"), P("dp"),
    )
    out_specs = (
        P(BOTH, None), P(BOTH, None), P(), P(None, None, None, "tensor"), P(None, "tensor", None), P(),
        P(), P(None, None, "tensor"), P(None, "tensor", None), P(),
    )
    return jax.shard_map(local, mesh=mesh, in_specs=in_specs, out_specs=out_specs, check_vma=False)
```

```python
import functools

import jax
import jax.numpy as jnp
from jax import lax
from jax.experimental import pallas as pl
from jax.experimental.pallas import tpu as pltpu
from jax.sharding import PartitionSpec as P

HEAD_DIM = 64
PAIR = 2 * HEAD_DIM
RANK = 16
LOG2E = 1.4426950408889634
LN2 = 0.6931471805599453
F32, BF = jnp.float32, jnp.bfloat16
VMEM_LIMIT = 60 * 2**20


def dot(a, b, ca, cb):
    return lax.dot_general(a, b, (((ca,), (cb,)), ((), ())), preferred_element_type=F32)


def params(**more):
    return pltpu.CompilerParams(vmem_limit_bytes=VMEM_LIMIT, **more)


def merge_rows(block):
    return block.reshape(block.shape[0] * block.shape[1], block.shape[2])


def norm_parts(values):
    centre = jnp.mean(values, axis=-1, keepdims=True)
    shifted = values - centre
    scale = lax.rsqrt(jnp.mean(shifted * shifted, axis=-1, keepdims=True) + 1e-05)
    return shifted * scale, scale


def norm_back(hat, scale, gain, grad):
    inner = grad * gain
    mean_one = jnp.mean(inner, axis=-1, keepdims=True)
    mean_two = jnp.mean(inner * hat, axis=-1, keepdims=True)
    return scale * (inner - mean_one - hat * mean_two)


MESH = pl.DeviceIdType.MESH
BOTH = ("dp", "tensor")
ANY = pl.BlockSpec(memory_space=pl.ANY)
IN_VMEM = pl.BlockSpec(memory_space=pltpu.VMEM)
IN_SMEM = pl.BlockSpec(memory_space=pltpu.SMEM)
DMA = pltpu.SemaphoreType.DMA


class Place:
    def __init__(self, n_dp, n_t, cap):
        self.n_dp, self.n_t, self.cap = n_dp, n_t, cap
        self.dp, self.t = lax.axis_index("dp"), lax.axis_index("tensor")
        self.core, self.q = self.dp % 2, self.dp // 2
        self.n_q, self.n_hi = n_dp // 2, n_dp // 4
        self.lo, self.hi = self.q % 2, self.q // 2
        self.group = n_t // cap
        self.half = self.group // 2
        self.slot, block = self.t // self.group, self.t % self.group
        self.high, self.low = block // self.half, block % self.half
        self.stays = self.core == self.high
        self.sibling = (self.dp + 1 - 2 * self.core, self.t)
        self.partner = (self.dp - self.core + self.high, self.t - block + self.core * self.half + self.low)

    def along(self, d):
        return (self.t + d) % self.n_t

    def column(self, d, cols):
        return pl.ds(pl.multiple_of(((self.t + self.n_t - d) % self.n_t) * cols, cols), cols)

    def lo_q(self):
        return self.q + 1 - 2 * self.lo

    def hi_q(self, m, lo=None):
        return ((self.hi + m) % self.n_hi) * 2 + (self.lo if lo is None else lo)

    def device(self, q, core=None, t=None):
        return (q * 2 + (self.core if core is None else core), self.t if t is None else t)

    def mate(self, shift):
        block = (self.core * self.half + self.low + shift) % self.group
        return (self.dp - self.core + block // self.half, self.t - self.low + block % self.half)

    def gather_peers(self):
        return (
            [(self.dp, self.along(d)) for d in range(1, self.n_t)]
            + [self.sibling, self.device(self.lo_q())]
            + [self.device(self.hi_q(m)) for m in range(1, self.n_hi)]
        )

    def other_core_peers(self):
        return [(self.sibling[0], self.along(d)) for d in range(1, self.n_t)]


def greet(peers):
    barrier = pltpu.get_barrier_semaphore()
    for peer in peers:
        pl.semaphore_signal(barrier, inc=1, device_id=peer, device_id_type=MESH)
    pl.semaphore_wait(barrier, len(peers))


def remote(src, dst, send, recv, device):
    return pltpu.make_async_remote_copy(
        src_ref=src, dst_ref=dst, send_sem=send, recv_sem=recv, device_id=device, device_id_type=MESH
    )


class Gather:
    @staticmethod
    def keys(n_hi, ds, here):
        found = []
        for d in ds:
            found += [] if d in here else [("z", d)]
            found += [("x", d), ("s", d)]
            for m in range(1, n_hi):
                found += [("y", m, d), ("dy", m, d), ("dx", m, d)]
        return found

    @staticmethod
    def scratch(n_dp, ds, here=(0,)):
        count = len(Gather.keys(n_dp // 4, ds, here))
        return [DMA((count,)), DMA((count,)), DMA((len(here),))]

    def __init__(self, place, sources, full, ds, sems, spread=None, by_rows=True):
        self.place, self.sources, self.full, self.ds = place, sources, full, list(ds)
        self.send, self.recv, self.own = sems
        self.index = {k: i for i, k in enumerate(Gather.keys(place.n_hi, self.ds, sources))}
        self.spread, self.by_rows = spread, by_rows
        self.ms = range(1, place.n_hi)

    def block(self, d, q, half=None):
        ref = self.full.at[self.ds.index(d), q, self.place.core]
        if half is None:
            return ref
        rows, cols = self.full.shape[-2:]
        if self.by_rows:
            return ref.at[pl.ds(half * (rows // 2), rows // 2)]
        first = cols // 2 // 128 * 128
        return ref.at[:, pl.ds(half * first, cols - first if half else first)]

    def copy(self, key):
        p, kind, d = self.place, key[0], key[-1]
        i = self.index[key]
        if kind == "z":
            src = self.sources[0] if self.spread is None else self.spread(d)
            dst, device = self.block(d, p.q), (p.dp, p.along(d))
        elif kind == "s":
            src = dst = self.full.at[self.ds.index(d), :, p.core]
            device = p.sibling
        elif kind in "xy":
            src = self.sources[d] if d in self.sources else self.block(d, p.q)
            dst = self.block(d, p.q)
            device = p.device(p.lo_q() if kind == "x" else p.hi_q(key[1]))
        elif kind == "dy":
            src = dst = self.block(d, p.lo_q(), 0)
            device = p.device(p.hi_q(key[1]))
        else:
            src = dst = self.block(d, p.hi_q(p.n_hi - key[1]), 1)
            device = p.device(p.lo_q())
        return remote(src, dst, self.send.at[i], self.recv.at[i], device)

    def own_copy(self, d):
        i = list(self.sources).index(d)
        return pltpu.make_async_copy(self.sources[d], self.block(d, self.place.q), self.own.at[i])

    def along(self, d):
        self.copy(("z", d)).start()

    def relay(self, d):
        if d in self.sources:
            self.own_copy(d).start()
        else:
            self.copy(("z", d)).wait_recv()
        self.copy(("x", d)).start()
        for m in self.ms:
            self.copy(("y", m, d)).start()

    def diag(self, d):
        self.copy(("x", d)).wait_recv()
        for m in self.ms:
            self.copy(("dy", m, d)).start()
        for m in self.ms:
            self.copy(("y", m, d)).wait_recv()
            self.copy(("dx", m, d)).start()

    def share(self, d):
        if d in self.sources:
            self.own_copy(d).wait()
        for m in self.ms:
            self.copy(("dy", m, d)).wait_recv()
            self.copy(("dx", m, d)).wait_recv()
        self.copy(("s", d)).start()

    def done(self, d):
        self.copy(("s", d)).wait_recv()

    def finish(self):
        for key in self.index:
            self.copy(key).wait_send()


def run_events(step, batches):
    for i, batch in enumerate(batches):
        if batch:

            @pl.when(step == i)
            def _():
                for event in batch:
                    event()


def cut(names, letter):
    parts = [[]]
    for name in names:
        if name[0] == letter:
            parts.append([])
        else:
            parts[-1].append(name)
    return parts


def orders(n_t, pairs, sub, group):
    if (n_t, pairs, sub, group) == (4, 2, 2, 2):
        return FRONT, MIDDLE
    near = n_t // 2
    late = list(reversed(range(near, n_t)))
    name = lambda letters, d: letters + str(d)
    front = ["G", "T", "er0", "xr0", "hr0", "or0", "A"]
    for d in range(1, n_t):
        front += [name(g, d) for g in (("ea", "oa", "xa", "ha") if d < near else ("ea", "oa"))]
    front += ["X", "H", "C"]
    every = lambda g, d: [name(g + a, d) for a in ("rds" if d else "ds")]
    for d in range(n_t):
        front += every("e", d)
    front += ["W", "g", "N"]
    for d in range(n_t):
        front += [name("R", d), name("P", d)]
    for d in range(n_t):
        front += every("o", d) + (every("x", d) + every("h", d) if d < near else [])
    for d in range(n_t):
        front += [name("V", d)] + [name("K", d * pairs + i) for i in range(pairs)]
    middle = []
    for g in "xh":
        middle += [name(g + "r", late[0])] + [name(g + "a", d) for d in late[1:]]
    middle += ["I"]
    for i in range(n_t * sub):
        middle += [name("F", i)]
        if i == 0:
            for d in late:
                for g in "xh":
                    middle += every(g, d)[1 if d == late[0] else 0 :]
        if (i + 1) % sub == 0 and near <= (i + 1) // sub < n_t:
            middle += [name("B", late[(i + 1) // sub - near])]
    return front, middle


FRONT = (
    "G", "ea1", "hr0", "er0", "xr0", "T", "A", "ed0", "ea2", "ea3", "hd0", "es0", "er1", "W", "g", "ed1",
    "xd0", "oa3", "N", "es1", "or0", "oa2", "er2", "R0", "xa1", "P0", "ha1", "R1", "er3", "V0", "od0", "K0",
    "oa1", "xs0", "ed2", "ed3", "or2", "P1", "xr1", "K1", "es2", "hr1", "C", "V1", "K2", "hs0", "R2", "P2",
    "or1", "es3", "K3", "hd1", "od2", "R3", "or3", "X", "od1", "P3", "V2", "K4", "V3", "os0", "hs1", "od3",
    "os2", "xd1", "K5", "os1", "H", "os3", "K6", "xs1", "K7",
)
MIDDLE = (
    "xa2", "xr3", "I", "hr3", "F0", "xd3", "xr2", "ha2", "F1", "hd3", "F2", "xd2", "xs3", "hs3", "hr2", "F3",
    "B3", "xs2", "hd2", "F4", "hs2", "F5", "B2", "F6", "F7",
)
STEPS = {"a": Gather.along, "r": Gather.relay, "d": Gather.diag, "s": Gather.share}


def move(place, source, target, sems, begin, rows=None):
    if rows is not None:
        source, target = source.at[rows], target.at[rows]

    @pl.when(place.stays)
    def _():
        here = pltpu.make_async_copy(source, target, sems[2])
        here.start() if begin else here.wait()

    @pl.when(jnp.logical_not(place.stays))
    def _():
        there = remote(source, target, sems[0], sems[1], place.partner)
        there.start() if begin else there.wait()


def head_masks(shape):
    lane = lax.broadcasted_iota(jnp.int32, shape, 1)
    return lane < HEAD_DIM, lane >= HEAD_DIM


def ones_lanes(rows, count):
    lane = lax.broadcasted_iota(jnp.int32, (rows, PAIR), 1)
    return jnp.where(lane < count, 1.0, 0.0).astype(BF)


def attend(queries, keys, values, o_ref, lse_ref):
    rows, length = queries.shape[0], keys.shape[0]
    values = jnp.concatenate([values, ones_lanes(length, 1)], axis=1)
    zero = jnp.zeros_like(queries)
    outs, sums = [], []
    both = [dot(jnp.where(mask, queries, zero), keys, 1, 1) for mask in head_masks(queries.shape)]
    for scores in both:
        top = jnp.max(scores, axis=1, keepdims=True)
        probs = jnp.exp2(scores - top).astype(BF)
        mixed = dot(probs, values, 1, 0)
        total = mixed[:, PAIR : PAIR + 1]
        outs.append(mixed[:, :PAIR] / total)
        sums.append(top + jnp.log2(total))
    first, _ = head_masks((rows, PAIR))
    o_ref[...] = jnp.where(first, outs[0], outs[1]).astype(BF)
    lse_ref[...] = jnp.where(first, sums[0], sums[1])


def front_kernel(
    n_dp, n_t, cap,
    choice_ref, count_ref, gain_ref, ed_tab, ou_tab, xd_tab, su_tab, eu_tab, od_tab, xu_tab, sd_tab,
    tokens_ref, cot_ref, w_ref, wo_ref, we_ref, ws_ref,
    o_ref, lse_ref, inner_t_ref, thin_out, rep_out,
    q_out, k_out, v_out, k_far_out, v_far_out, normed_out, tok_out, cot_out, w_full, wo_full, we_full, ws_full,
    we_land, ws_land,
    q, k, v, k_far, v_far, tok, cot, normed, thin, rep, thin_send, stage, inner,
    tok_sems, cot_sems, thin_sends, thin_recvs, rep_sems, stage_sems, kv_sends, kv_recvs, keep_sems, kept_sems,
    land_sems, go_sem, *sems,
):
    p = Place(n_dp, n_t, cap)
    step, steps = pl.program_id(0), pl.num_programs(0)
    cols, hid = od_tab.shape[-1], xu_tab.shape[-1]
    pairs = cols // PAIR
    depth = w_ref.shape[0] // 3
    early = list(range(n_t // 2))
    entry = Gather(p, {0: w_ref}, w_full, range(n_t), sems[0:3])
    out_g = Gather(p, {0: wo_ref}, wo_full, range(n_t), sems[3:6])
    exp_g = Gather(p, {0: we_ref}, we_full, early, sems[6:9])
    shr_g = Gather(p, {0: ws_ref}, ws_full, early, sems[9:12])
    both = (exp_g, shr_g)
    tok_three = [tok_sems.at[i] for i in range(3)]
    cot_three = [cot_sems.at[i] for i in range(3)]

    def thin_targets():
        for s in range(cap):
            for low in range(p.half):
                to = s * p.group + p.core * p.half + low
                for core in range(2):
                    i = (s * p.half + low) * 2 + core
                    elsewhere = jnp.logical_or(core != p.core, to != p.t)
                    yield s, to, core, i, elsewhere

    def send_thin(near):
        for s, to, core, i, elsewhere in thin_targets():
            d = (to + n_t - p.t) % n_t

            @pl.when(jnp.logical_and(elsewhere, (to == p.t) == near))
            def _():
                remote(
                    thin_send.at[s], thin.at[d], thin_sends.at[i], thin_recvs.at[d], (p.dp - p.core + core, to)
                ).start()

    def send_adapters():
        for s in range(cap):
            a = choice_ref[s]
            for i in range(3):
                thin_send[s, :, i * cols : (i + 1) * cols] = eu_tab[a, i]
            thin_send[s, :, 3 * cols : 4 * cols] = od_tab[a]
            thin_send[s, :, 4 * cols : 4 * cols + hid] = xu_tab[a]
            thin_send[s, :, 4 * cols + hid :] = sd_tab[a]
        send_thin(True)

        @pl.when(p.stays)
        def _():
            a = choice_ref[p.slot]
            for i, table in enumerate((ed_tab, ou_tab, xd_tab, su_tab)):
                rep[i * RANK : (i + 1) * RANK] = table[a]
            row = lax.broadcasted_iota(jnp.int32, (RANK, rep.shape[1]), 0)
            alive = jnp.where(p.slot < count_ref[0], 1.0, 0.0)
            rep[4 * RANK :] = jnp.where(row < RANK // 2, alive, a.astype(F32)).astype(BF)
            remote(rep, rep, rep_sems.at[0], rep_sems.at[1], p.sibling).start()
            thin[0] = thin_send[p.slot]

    def take_near():
        @pl.when(jnp.logical_not(p.stays))
        def _():
            remote(rep, rep, rep_sems.at[0], rep_sems.at[1], p.sibling).wait_recv()
            remote(thin_send.at[0], thin.at[0], thin_sends.at[0], thin_recvs.at[0], p.sibling).wait_recv()

        rep_out[...] = rep[...]
        thin_out[0] = thin[0]

    def take_thin(d):
        remote(thin_send.at[0], thin.at[d], thin_sends.at[0], thin_recvs.at[d], p.sibling).wait_recv()
        thin_out[d] = thin[d]

    def load(d):
        return pltpu.make_async_copy(w_full.at[d], stage.at[d % 2], stage_sems.at[d % 2])

    def kept():
        return [pltpu.make_async_copy(tok, tok_out, keep_sems.at[0]), pltpu.make_async_copy(normed, normed_out, keep_sems.at[1])]

    def first_norm():
        hat, _ = norm_parts(tok[...].astype(F32))
        value = (hat * gain_ref[...]).astype(BF)
        normed[...] = value
        down = rep[:RANK]
        inner[...] = dot(value, down, 1, 1).astype(BF)
        inner_t_ref[...] = dot(down, value, 1, 1).astype(BF)
        for copy in kept():
            copy.start()

    def far_copy(d, which, m):
        source, target = ((k, k_far), (v, v_far))[which]
        device = p.mate(m)
        there = (d + device[1] + n_t - p.t) % n_t
        return remote(
            source.at[pl.ds(d * pairs, pairs)], target.at[m - 1, pl.ds(there * pairs, pairs)],
            kv_sends.at[d, which, m - 1], kv_recvs.at[there, which, m - 1], device,
        )

    def far_arrival(d, which, m):
        source, target = ((k, k_far), (v, v_far))[which]
        return remote(
            source.at[pl.ds(d * pairs, pairs)], target.at[m - 1, pl.ds(d * pairs, pairs)],
            kv_sends.at[d, which, m - 1], kv_recvs.at[d, which, m - 1], p.mate(m),
        )

    def project(d):
        load(d).wait()
        for which, out in ((1, k), (2, v), (0, q)):
            weights = stage[d % 2, :, :, which * depth : (which + 1) * depth].reshape(n_dp * depth, cols)
            part = dot(normed[...], weights, 1, 0)
            part = part + dot(inner[...], thin[d, :, which * cols : (which + 1) * cols], 1, 0)
            if which == 0:
                part = part * (HEAD_DIM**-0.5 * LOG2E)
            part = part.astype(BF)
            for i in range(pairs):
                out[d * pairs + i] = part[:, i * PAIR : (i + 1) * PAIR]
            if which:
                for m in range(1, p.group):
                    far_copy(d, which - 1, m).start()

    def copies_out(d):
        at = pl.ds(d * pairs, pairs)
        found = [(a.at[at], b.at[at]) for a, b in ((q, q_out), (k, k_out), (v, v_out))]
        for a, b in ((k_far, k_far_out), (v_far, v_far_out)):
            found += [(a.at[m, at], b.at[m, at]) for m in range(p.group - 1)]
        return [pltpu.make_async_copy(a, b, kept_sems.at[d, i]) for i, (a, b) in enumerate(found)]

    def arrive(d):
        for m in range(1, p.group):
            far_arrival(d, 0, m).wait_recv()
            far_arrival(d, 1, m).wait_recv()
        for copy in copies_out(d):
            copy.start()

    def land(i):
        source, target = ((we_ref, we_land), (ws_ref, ws_land))[i]
        return remote(source, target, land_sems.at[0, i], land_sems.at[1, i], (p.dp, p.along(n_t - 1)))

    def ready(d):
        if d:
            take_thin(d)
        entry.done(d)
        load(d).start()

    def go():
        @pl.when(jnp.logical_not(p.stays))
        def _():
            pl.semaphore_signal(go_sem, inc=1, device_id=p.sibling, device_id_type=MESH)

        @pl.when(p.stays)
        def _():
            pl.semaphore_wait(go_sem, 1)

    def arrived():
        move(p, tokens_ref, tok, tok_three, False)
        send_thin(False)

    def norm():
        take_near()
        first_norm()

    def opened():
        greet(p.gather_peers() + p.other_core_peers())

    gathers = {"e": entry, "x": exp_g, "h": shr_g, "o": out_g}
    plain = {
        "G": opened, "g": go, "W": arrived, "N": norm, "A": send_adapters,
        "T": lambda: move(p, tokens_ref, tok, tok_three, True), "C": lambda: move(p, cot_ref, cot, cot_three, True),
        "X": lambda: land(0).start(), "H": lambda: land(1).start(),
    }
    counted = {"R": ready, "P": project, "V": arrive}

    def event(name):
        if len(name) == 1:
            return plain[name]
        if len(name) == 2:
            return lambda: counted[name[0]](int(name[1]))
        return lambda: STEPS[name[1]](gathers[name[0]], int(name[2]))

    names = orders(n_t, pairs, max(1, hid // 512), p.group)[0]
    parts = cut(names, "K")
    closing = [event(name) for name in parts.pop()]
    first = ["P0" in part or sum(name[0] == "P" for name in part) > 1 for part in parts]
    single = {}
    before, after = [], []
    for i, part in enumerate(parts):
        places = [] if first[i] else [j for j, name in enumerate(part) if name[0] == "P"]
        at = places[0] if places else len(part)
        if places:
            single[i] = int(part[at][1])
        before.append([event(name) for name in part[:at]])
        after.append([event(name) for name in part[at + 1 :]])
    run_events(step, before)
    if single:
        chunk = sum(jnp.where(step == i, d, 0) for i, d in single.items())

        @pl.when(chunk > 0)
        def _():
            project(chunk)

    run_events(step, after)
    keys = jnp.concatenate([k[step]] + [k_far[m, step] for m in range(p.group - 1)], axis=0)
    values = jnp.concatenate([v[step]] + [v_far[m, step] for m in range(p.group - 1)], axis=0)
    attend(q[step], keys, values, o_ref, lse_ref)

    @pl.when(step == steps - 1)
    def _():
        for call in closing:
            call()
        for g in (exp_g, shr_g, out_g):
            for d in g.ds:
                g.done(d)
        for g in (entry, exp_g, shr_g, out_g):
            g.finish()
        for i in range(2):
            land(i).wait()
        move(p, cot_ref, cot, cot_three, False)
        keep_cot = pltpu.make_async_copy(cot, cot_out, keep_sems.at[2])
        keep_cot.start()

        @pl.when(p.stays)
        def _():
            remote(rep, rep, rep_sems.at[0], rep_sems.at[1], p.sibling).wait_send()

        for s, to, core, i, elsewhere in thin_targets():

            @pl.when(elsewhere)
            def _():
                remote(thin_send.at[s], thin.at[0], thin_sends.at[i], thin_recvs.at[0], p.sibling).wait_send()

        for copy in [keep_cot, *kept()]:
            copy.wait()
        for d in range(n_t):
            for m in range(1, p.group):
                far_copy(d, 0, m).wait_send()
                far_copy(d, 1, m).wait_send()
            for copy in copies_out(d):
                copy.wait()


def front_part(cap, choice, count, gain, rep_tables, thin_tables, tokens, cot, w, wo, we, ws):
    n_dp, n_t = lax.axis_size("dp"), lax.axis_size("tensor")
    rows, width = tokens.shape
    cols = wo.shape[-1]
    others = n_t // cap - 1
    count_pairs = width // PAIR
    early = n_t // 2
    thin_width = 4 * cols + 2 * we.shape[-1]
    shape, vmem = jax.ShapeDtypeStruct, pltpu.VMEM
    whole = lambda *s: pl.BlockSpec(s, lambda h: (0,) * len(s))
    pair = pl.BlockSpec((None, rows, PAIR), lambda h: (h, 0, 0))
    full = lambda n, a: shape((n, n_dp // 2, 2, *a.shape), BF)
    heads, far = (count_pairs, rows, PAIR), (others, count_pairs, rows, PAIR)
    small = [(RANK, rows), (n_t, RANK, thin_width), (5 * RANK, width)]
    return pl.pallas_call(
        functools.partial(front_kernel, n_dp, n_t, cap),
        grid=(count_pairs,),
        in_specs=[IN_SMEM, IN_SMEM] + [whole(*a.shape) for a in (gain, *rep_tables, *thin_tables)]
        + [ANY] * 2 + [whole(*a.shape) for a in (w, wo, we, ws)],
        out_specs=[pair, pair] + [whole(*s) for s in small] + [ANY] * 14,
        out_shape=[shape(heads, BF), shape(heads, F32)] + [shape(s, BF) for s in small]
        + [shape(heads, BF)] * 3 + [shape(far, BF)] * 2 + [shape((rows, width), BF)] * 3
        + [full(n_t, w), full(n_t, wo), full(early, we), full(early, ws), shape(we.shape, BF), shape(ws.shape, BF)],
        scratch_shapes=[
            vmem(heads, BF), vmem(heads, BF), vmem(heads, BF), vmem(far, BF), vmem(far, BF),
            vmem((rows, width), BF), vmem((rows, width), BF), vmem((rows, width), BF), vmem(small[1], BF), vmem(small[2], BF),
            vmem((cap, RANK, thin_width), BF),
            vmem((2, n_dp // 2, 2, *w.shape), BF), vmem((rows, RANK), BF),
            DMA((3,)), DMA((3,)), DMA((n_t,)), DMA((n_t,)), DMA((2,)), DMA((2,)),
            DMA((n_t, 2, others)), DMA((n_t, 2, others)), DMA((3,)), DMA((n_t, 3 + 2 * others)), DMA((2, 2)),
            pltpu.SemaphoreType.REGULAR,
            *Gather.scratch(n_dp, range(n_t)), *Gather.scratch(n_dp, range(n_t)),
            *Gather.scratch(n_dp, range(early)), *Gather.scratch(n_dp, range(early)),
        ],
        compiler_params=params(collective_id=0, has_side_effects=True),
        name="front_part",
    )(choice, count, gain, *rep_tables, *thin_tables, tokens, cot, w, wo, we, ws)


def split_lanes(column):
    column = -column
    high = column.astype(BF)
    rest = column - high.astype(F32)
    mid = rest.astype(BF)
    low = (rest - mid.astype(F32)).astype(BF)
    lane = lax.broadcasted_iota(jnp.int32, (column.shape[0], PAIR), 1)
    zero = jnp.zeros((column.shape[0], PAIR), BF)
    return jnp.where(lane == 0, high, jnp.where(lane == 1, mid, jnp.where(lane == 2, low, zero)))


def back_kernel(
    n_dp, n_t, cap, tiles,
    q_ref, k_ref, k_far, v_ref, v_far, o_ref, lse_ref, do_ref, gain_ref, rep_ref, thin_ref, inner_t_ref, grads_ref,
    mixed_ref, w_ref, mgrad_ref, tok_ref, normed_ref,
    mixed_out, mid_full, tgrad_out, end_full,
    grad, send, far, mixed, weights, mgrad, tok, normed, back_sum, row_sum, back_low, tgrad, end, sends, recvs, swap, swaps, load_sems,
    *sems,
):
    p = Place(n_dp, n_t, cap)
    step, steps = pl.program_id(0), pl.num_programs(0)
    rows = q_ref.shape[0]
    pairs = grad.shape[1] // n_t
    cols = w_ref.shape[-1]
    depth = w_ref.shape[-2] // 3
    width = tok_ref.shape[1]
    mid_g = Gather(
        p, {0: grads_ref.at[0]}, mid_full, range(n_t), sems[0:3],
        spread=lambda d: grads_ref.at[n_t - d], by_rows=False,
    )
    end_g = Gather(
        p, {0: end.at[0]}, end_full, range(n_t), sems[3:6], spread=lambda d: end.at[n_t - d], by_rows=False
    )
    swap_sems = [swap.at[i] for i in range(3)]
    loads = [
        pltpu.make_async_copy(src, dst, load_sems.at[i])
        for i, (src, dst) in enumerate(((w_ref, weights), (normed_ref, normed), (tok_ref, tok), (mgrad_ref, mgrad)))
    ]
    relay, diag, share = ((lambda d, f=f: lambda: f(d)) for f in (mid_g.relay, mid_g.diag, mid_g.share))
    start_swap = lambda: move(p, mixed_ref, mixed, swap_sems, True)
    start_loads = lambda: [copy.start() for copy in loads]

    def opening():
        greet(p.gather_peers() + p.other_core_peers())
        mid_g.relay(0)
        for d in range(1, n_t):
            mid_g.along(d)

    if n_t == 4:
        table = {
            0: [opening], 1: [diag(0), relay(1)], 2: [share(0), diag(1), relay(2), start_swap],
            3: [share(1), diag(2), relay(3)], 4: [share(2), diag(3), start_loads], 5: [share(3)],
        }
    else:
        table = {0: [opening, start_swap, start_loads, diag(0), share(0)]}
        for d in range(1, n_t):
            table[0] += [relay(d), diag(d), share(d)]
    run_events(step, [table.get(i, []) for i in range(max(table) + 1)])

    with_far = lambda near, far: jnp.concatenate([near[...]] + [far[m] for m in range(p.group - 1)], axis=0)
    keys = with_far(k_ref, k_far)
    length = keys.shape[0]
    ones = ones_lanes(length, 3)
    keys_more = jnp.concatenate([keys, ones], axis=1)
    values_more = jnp.concatenate([with_far(v_ref, v_far), ones], axis=1)
    queries, grad_out = q_ref[...], do_ref[...]
    zero = jnp.zeros_like(queries)
    product = grad_out.astype(F32) * o_ref[...].astype(F32)
    d_queries, both = [], [[], [], [], []]
    for head, mask in enumerate(head_masks(queries.shape)):
        query = jnp.where(mask, queries, zero)
        grad_head = jnp.where(mask, grad_out, zero)
        lse = lse_ref[:, head * HEAD_DIM : head * HEAD_DIM + 1]
        delta = jnp.sum(jnp.where(mask, product, 0.0), axis=1, keepdims=True)
        probs = jnp.exp2(dot(jnp.concatenate([query, split_lanes(lse)], axis=1), keys_more, 1, 1))
        slope = dot(jnp.concatenate([grad_head, split_lanes(delta)], axis=1), values_more, 1, 1)
        score_grad = (probs * slope).astype(BF)
        d_queries.append(dot(score_grad, keys, 1, 0))
        for kept, one in zip(both, (grad_head, probs.astype(BF), query, score_grad)):
            kept.append(one)
    grad_heads, probs, query, score_grad = [jnp.concatenate(kept, axis=0) for kept in both]
    d_values = dot(grad_heads, probs, 0, 0)
    d_keys = dot(query, score_grad, 0, 0)
    first, _ = head_masks((rows, PAIR))
    grad[0, step] = (jnp.where(first, d_queries[0], d_queries[1]) * HEAD_DIM**-0.5).astype(BF)
    d_keys = (d_keys * LN2).T.astype(BF)
    d_values = d_values.T.astype(BF)
    grad[1, step] = d_keys[:rows]
    grad[2, step] = d_values[:rows]

    def far_copy(i, m, h):
        device = p.mate(p.group - m)
        there = (h // pairs + device[1] + n_t - p.t) % n_t * pairs + h % pairs
        return remote(
            send.at[i, m - 1, h], far.at[i, m - 1, there], sends.at[i, m - 1, h], recvs.at[i, m - 1, there], device
        )

    for m in range(1, p.group):
        send[0, m - 1, step] = d_keys[m * rows : (m + 1) * rows]
        send[1, m - 1, step] = d_values[m * rows : (m + 1) * rows]
        far_copy(0, m, step).start()
        far_copy(1, m, step).start()

    @pl.when(step == steps - 1)
    def _():
        move(p, mixed_ref, mixed, swap_sems, False)
        keep = pltpu.make_async_copy(mixed, mixed_out, swap.at[3])
        keep.start()
        for i in range(2):
            for m in range(1, p.group):
                for h in range(n_t * pairs):
                    remote(
                        send.at[i, m - 1, h], far.at[i, m - 1, h], sends.at[i, m - 1, h], recvs.at[i, m - 1, h], p.sibling
                    ).wait_recv()

            @pl.loop(0, steps)
            def _(h):
                total = grad[1 + i, h].astype(F32)
                for m in range(p.group - 1):
                    total = total + far[i, m, h].astype(F32)
                grad[1 + i, h] = total.astype(BF)

        columns = lambda which, d, rows: jnp.concatenate(
            [grad[which, d * pairs + i, rows] for i in range(pairs)], axis=1
        )
        chunks = n_t * 3
        back_sum[...] = jnp.zeros_like(back_sum)

        @pl.loop(0, chunks)
        def _(j):
            d, at = j // 3, pl.ds(pl.multiple_of(j % 3 * cols, cols), cols)
            part = columns(j % 3, d, slice(None))
            back_sum[...] += dot(part, thin_ref[d, :, at], 1, 1)
            end[d, :, at] = dot(inner_t_ref[...], part, 1, 0).astype(BF)

        back_low[...] = back_sum[...].astype(BF)
        loads[1].wait()
        down_grad = dot(back_low[...], normed[...], 0, 0).astype(BF)
        for d in range(n_t):
            end[d, :, 3 * cols :] = down_grad
        end_g.relay(0)
        for d in range(1, n_t):
            end_g.along(d)
        for copy in (loads[0], *loads[2:]):
            copy.wait()

        def tile(n):
            start, count = tiles[n]
            rows = pl.ds(start, count)
            acc = row_sum.at[pl.ds(0, count)]
            acc[...] = dot(back_low[rows], rep_ref[:RANK], 1, 0)

            @pl.loop(0, chunks)
            def _(j):
                at = pl.ds(pl.multiple_of(j % 3 * depth, depth), depth)
                piece = weights[j // 3, :, :, at].reshape(width, cols)
                acc[...] += dot(columns(j % 3, j // 3, rows), piece, 1, 1)

            total = acc[...]
            hat, scale = norm_parts(tok[rows].astype(F32))
            tgrad[rows] = (mgrad[rows] + norm_back(hat, scale, gain_ref[...], total)).astype(BF)
            move(p, tgrad, tgrad_out, [swaps.at[n, i] for i in range(3)], True, rows)

        for n in range(len(tiles)):
            tile(n)
            if n == 0:
                end_g.diag(0)
                end_g.relay(1)
            if n == min(1, len(tiles) - 1):
                for d in range(2, n_t):
                    end_g.relay(d)
                end_g.share(0)
                end_g.diag(1)
        for d in range(2, n_t):
            end_g.diag(d)
            end_g.share(d - 1)
        end_g.share(n_t - 1)
        for d in range(n_t):
            mid_g.done(d)
            end_g.done(d)
        mid_g.finish()
        end_g.finish()
        for n, (start, count) in enumerate(tiles):
            move(p, tgrad, tgrad_out, [swaps.at[n, i] for i in range(3)], False, pl.ds(start, count))

        @pl.loop(0, steps)
        def _(h):
            for m in range(1, p.group):
                for i in range(2):
                    far_copy(i, m, h).wait_send()

        keep.wait()


def back_part(cap, q, k, k_far, v, v_far, o, lse, do, gain, rep, thin, inner_t, grads, mixed, w_full, mgrad, tok, normed):
    n_dp, n_t = lax.axis_size("dp"), lax.axis_size("tensor")
    heads, rows, _ = q.shape
    width, cols = tok.shape[1], w_full.shape[-1]
    others = k_far.shape[0]
    pair = pl.BlockSpec((None, rows, PAIR), lambda h: (h, 0, 0))
    far = pl.BlockSpec((others, None, rows, PAIR), lambda h: (0, h, 0, 0))
    whole = lambda a: pl.BlockSpec(a.shape, lambda h: (0,) * len(a.shape))
    shape, vmem = jax.ShapeDtypeStruct, pltpu.VMEM
    count = (2, others, heads)
    number = 3 if rows % 16 == 0 else 1
    size = rows // number // 16 * 16 if number > 1 else rows
    tiles = [(0, rows - size * (number - 1))]
    tiles += [(tiles[0][1] + size * i, size) for i in range(number - 1)]
    end_width = 3 * cols + width
    full = lambda n: shape((n_t, n_dp // 2, 2, RANK, n), BF)
    return pl.pallas_call(
        functools.partial(back_kernel, n_dp, n_t, cap, tiles),
        grid=(heads,),
        in_specs=[pair, pair, far, pair, far, pair, pair, pair]
        + [whole(a) for a in (gain, rep, thin, inner_t, grads)] + [ANY] * 5,
        out_specs=[ANY] * 4,
        out_shape=[shape(mixed.shape, BF), full(grads.shape[-1]), shape(tok.shape, BF), full(end_width)],
        scratch_shapes=[
            vmem((3, heads, rows, PAIR), BF), vmem((2, *k_far.shape), BF), vmem((2, *k_far.shape), BF),
            vmem(mixed.shape, BF), vmem(w_full.shape, BF), vmem(mgrad.shape, F32), vmem(tok.shape, BF),
            vmem(tok.shape, BF), vmem((rows, RANK), F32), vmem((tiles[0][1], width), F32), vmem((rows, RANK), BF),
            vmem(tok.shape, BF), vmem((n_t, RANK, end_width), BF),
            DMA(count), DMA(count), DMA((4,)), DMA((len(tiles), 3)), DMA((4,)),
            *Gather.scratch(n_dp, range(n_t)), *Gather.scratch(n_dp, range(n_t)),
        ],
        compiler_params=params(collective_id=1, has_side_effects=True),
        name="back_part",
    )(q, k, k_far, v, v_far, o, lse, do, gain, rep, thin, inner_t, grads, mixed, w_full, mgrad, tok, normed)


def gelu_parts(hidden):
    share = 0.5 * (1.0 + lax.erf(hidden * 0.7071067811865476))
    density = jnp.exp(-0.5 * hidden * hidden) * 0.3989422804014327
    return hidden * share, share + hidden * density


def middle_kernel(
    n_dp, n_t, cap, sub,
    x_in, att_in, cot_in, gain_ref, rep_ref, thin_ref, wo_in, we_near, ws_near, we_land, ws_land, we_ref, ws_ref,
    mixed_out, mgrad_out, agrad_out, grads_ref, we_full, ws_full,
    middle_ref, second_ref, dy_ref, acc2_ref, acc3_ref, einner_ref, einner_t_ref, sback_ref, sback_t_ref,
    sinner_ref, eback_ref, oinner_ref, we_buf, ws_buf, x_ref, att_ref, cot_ref, wo_ref, mixed_ref, mgrad_ref, agrad_ref,
    buf_sems, in_sems, out_sems, *sems,
):
    p = Place(n_dp, n_t, cap)
    step, steps = pl.program_id(0), pl.num_programs(0)
    cols = wo_ref.shape[-1]
    width = x_ref.shape[1]
    hid = we_ref.shape[-1]
    size = hid // sub
    near = n_t // 2
    late = list(reversed(range(near, n_t)))
    exp_g = Gather(p, {n_t - 1: we_land}, we_full, late, sems[0:3], spread=lambda d: we_ref)
    shr_g = Gather(p, {n_t - 1: ws_land}, ws_full, late, sems[3:6], spread=lambda d: ws_ref)
    pairs = cols // PAIR
    both = (exp_g, shr_g)
    down_e, up_o, up_s = rep_ref[2 * RANK : 3 * RANK], rep_ref[RANK : 2 * RANK], rep_ref[3 * RANK : 4 * RANK]
    alive = rep_ref[4 * RANK : 4 * RANK + 1, 0:1].astype(F32)
    at_od, at_eu = 3 * width, 3 * width + cols
    at_sd, at_id = at_eu + hid, at_eu + 2 * hid

    def load(i):
        index, part = i // sub, i % sub
        at = pl.ds(part * size, size)
        pair = (we_near, ws_near) if index < near else (we_full, ws_full)
        index = index if index < near else index - near
        return [
            pltpu.make_async_copy(src.at[index, :, :, :, at], buf.at[i % 3], buf_sems.at[i % 3, j])
            for j, (src, buf) in enumerate(zip(pair, (we_buf, ws_buf)))
        ]

    inputs = [
        pltpu.make_async_copy(src, dst, in_sems.at[i])
        for i, (src, dst) in enumerate(((att_in, att_ref), (wo_in, wo_ref), (x_in, x_ref), (cot_in, cot_ref)))
    ]
    outputs = [
        pltpu.make_async_copy(src, dst, out_sems.at[i])
        for i, (src, dst) in enumerate(((mixed_ref, mixed_out), (mgrad_ref, mgrad_out), (agrad_ref, agrad_out)))
    ]
    gathers = {"x": exp_g, "h": shr_g}

    def bring(d):
        exp_g.done(d)
        shr_g.done(d)
        for i in range(sub):
            for copy in load((near + late.index(d)) * sub + i):
                copy.start()

    def event(name):
        if len(name) == 2:
            return lambda: bring(int(name[1]))
        return lambda: STEPS[name[1]](gathers[name[0]], int(name[2]))

    names = orders(n_t, pairs, sub, p.group)[1]
    begun = names.index("I")
    start = [event(name) for name in names[:begun]]
    opening, *after = [[event(name) for name in part] for part in cut(names[begun + 1 :], "F")]
    columns = lambda d: jnp.concatenate([att_ref[d * pairs + i] for i in range(pairs)], axis=1)

    @pl.when(step == 0)
    def _():
        for copy in inputs:
            copy.start()
        for i in range(2):
            for copy in load(i):
                copy.start()
        greet(p.gather_peers())
        for call in start:
            call()
        for copy in inputs:
            copy.wait()
        branch, inner = 0.0, 0.0
        for d in range(n_t):
            att = columns(d)
            branch = branch + dot(att, wo_ref[d].reshape(width, cols), 1, 1)
            inner = inner + dot(att, thin_ref[d, :, 3 * cols : 4 * cols], 1, 1)
        inner = inner.astype(BF)
        oinner_ref[...] = inner
        middle = x_ref[...].astype(F32) + (branch + dot(inner, up_o, 1, 0))
        middle_ref[...] = middle
        hat, _ = norm_parts(middle)
        second = (hat * gain_ref[...]).astype(BF)
        second_ref[...] = second
        dy = (cot_ref[...].astype(F32) * alive).astype(BF)
        dy_ref[...] = dy
        einner_ref[...] = dot(second, down_e, 1, 1).astype(BF)
        einner_t_ref[...] = dot(down_e, second, 1, 1).astype(BF)
        sback_ref[...] = dot(dy, up_s, 1, 1).astype(BF)
        sback_t_ref[...] = dot(up_s, dy, 1, 1).astype(BF)
        acc2_ref[...] = jnp.zeros_like(acc2_ref)
        acc3_ref[...] = jnp.zeros_like(acc3_ref)
        sinner_ref[...] = jnp.zeros_like(sinner_ref)
        eback_ref[...] = jnp.zeros_like(eback_ref)

    run_events(step, [opening])
    for i in range(n_t * sub):

        @pl.when(step == i)
        def _():
            for copy in load(i):
                copy.wait()
            if i + 2 < near * sub:
                for copy in load(i + 2):
                    copy.start()

    buf = step % 3
    d, part = step // sub, step % sub
    d = jnp.where(d < near, d, n_t - 1 + near - d)
    we, ws = we_buf[buf].reshape(width, size), ws_buf[buf].reshape(width, size)
    at = pl.multiple_of(part * size, size)
    e_up = thin_ref[d, :, pl.ds(4 * cols + at, size)]
    s_down = thin_ref[d, :, pl.ds(4 * cols + hid + at, size)]
    hidden = dot(second_ref[...], we, 1, 0) + dot(einner_ref[...], e_up, 1, 0)
    value, slope = gelu_parts(hidden)
    act = value.astype(BF)
    acc2_ref[...] += dot(act, ws, 1, 1)
    sinner_ref[...] += dot(act, s_down, 1, 1)
    act_grad = dot(dy_ref[...], ws, 1, 0) + dot(sback_ref[...], s_down, 1, 0)
    hid_grad = (act_grad * slope).astype(BF)
    acc3_ref[...] += dot(hid_grad, we, 1, 1)
    eback_ref[...] += dot(hid_grad, e_up, 1, 1)
    grads_ref[d, :, pl.ds(at_eu + at, size)] = dot(einner_t_ref[...], hid_grad, 1, 0).astype(BF)
    grads_ref[d, :, pl.ds(at_sd + at, size)] = dot(sback_t_ref[...], act, 1, 0).astype(BF)

    run_events(step, after)
    @pl.when(step == steps - 1)
    def _():
        s_inner, e_back = sinner_ref[...].astype(BF), eback_ref[...].astype(BF)
        middle = middle_ref[...]
        mixed_ref[...] = (alive * (middle + (acc2_ref[...] + dot(s_inner, up_s, 1, 0)))).astype(BF)
        outputs[0].start()
        shrink_up = dot(s_inner, dy_ref[...], 0, 0).astype(BF)
        expand_down = dot(e_back, second_ref[...], 0, 0).astype(BF)
        second_grad = acc3_ref[...] + dot(e_back, down_e, 1, 0)
        hat, scale = norm_parts(middle)
        mgrad = cot_ref[...].astype(F32) * alive + norm_back(hat, scale, gain_ref[...], second_grad)
        mgrad_ref[...] = mgrad
        outputs[1].start()
        low = mgrad.astype(BF)
        o_back = dot(low, up_o, 1, 1).astype(BF)
        output_up = dot(oinner_ref[...], low, 0, 0).astype(BF)
        for d in range(n_t):
            agrad = dot(low, wo_ref[d].reshape(width, cols), 1, 0)
            agrad = (agrad + dot(o_back, thin_ref[d, :, 3 * cols : 4 * cols], 1, 0)).astype(BF)
            for i in range(pairs):
                agrad_ref[d * pairs + i] = agrad[:, i * PAIR : (i + 1) * PAIR]
        outputs[2].start()
        for d in range(n_t):
            grads_ref[d, :, :width] = expand_down
            grads_ref[d, :, width : 2 * width] = shrink_up
            grads_ref[d, :, 2 * width : 3 * width] = output_up
            grads_ref[d, :, at_od : at_od + cols] = dot(o_back, columns(d), 0, 0).astype(BF)
            grads_ref[d, :, at_id:] = rep_ref[4 * RANK :, : grads_ref.shape[2] - at_id]
        for g in both:
            g.finish()
        for copy in outputs:
            copy.wait()


ID_LANES = 128


def middle_both_ways(cap, x, att, cot, gain, rep, thin, wo_full, we_near, ws_near, we_land, ws_land, we, ws):
    n_dp, n_t = lax.axis_size("dp"), lax.axis_size("tensor")
    rows, width = x.shape
    depth, hid = we.shape
    cols = wo_full.shape[-1]
    sub = max(1, hid // 512)
    size = hid // sub
    late = list(reversed(range(n_t // 2, n_t)))
    grad_width = 3 * width + cols + 2 * hid + ID_LANES
    whole = lambda a: pl.BlockSpec(a.shape, lambda i: (0,) * len(a.shape))
    shape = jax.ShapeDtypeStruct
    full = shape((len(late), n_dp // 2, 2, depth, hid), BF)
    outs = [
        shape((rows, width), BF), shape((rows, width), F32), shape(att.shape, BF),
        shape((n_t, RANK, grad_width), BF),
    ]
    vmem = pltpu.VMEM
    return pl.pallas_call(
        functools.partial(middle_kernel, n_dp, n_t, cap, sub),
        grid=(n_t * sub,),
        in_specs=[ANY] * 3 + [whole(a) for a in (gain, rep, thin)]
        + [ANY] * 3 + [whole(we_land), whole(ws_land)] + [ANY] * 2,
        out_specs=[ANY] * 3 + [whole(outs[3])] + [ANY] * 2,
        out_shape=outs + [full, full],
        scratch_shapes=[
            vmem((rows, width), F32), vmem((rows, width), BF), vmem((rows, width), BF),
            vmem((rows, width), F32), vmem((rows, width), F32),
            vmem((rows, RANK), BF), vmem((RANK, rows), BF), vmem((rows, RANK), BF), vmem((RANK, rows), BF),
            vmem((rows, RANK), F32), vmem((rows, RANK), F32), vmem((rows, RANK), BF),
            vmem((3, n_dp // 2, 2, depth, size), BF), vmem((3, n_dp // 2, 2, depth, size), BF),
            vmem(x.shape, BF), vmem(att.shape, BF), vmem(cot.shape, BF), vmem(wo_full.shape, BF),
            vmem(x.shape, BF), vmem(x.shape, F32), vmem(att.shape, BF), DMA((3, 2)), DMA((4,)), DMA((3,)),
            *Gather.scratch(n_dp, late, late[:1]), *Gather.scratch(n_dp, late, late[:1]),
        ],
        compiler_params=params(collective_id=2, has_side_effects=True),
        name="middle_both_ways",
    )(x, att, cot, gain, rep, thin, wo_full, we_near, ws_near, we_land, ws_land, we, ws)


def sum_kernel(
    width, cols, hid, mid_ref, end_ref, entry_down, entry_up, output_down, output_up, expand_down, expand_up,
    shrink_down, shrink_up,
):
    outs = (entry_down, entry_up, output_down, output_up, expand_down, expand_up, shrink_down, shrink_up)

    @pl.when(pl.program_id(0) == 0)
    def _():
        for out in outs:
            out[...] = jnp.zeros_like(out)

    sources = range(mid_ref.shape[0])
    at_id = 3 * width + cols + 2 * hid
    chosen = [jnp.max(mid_ref[i, RANK // 2 :, at_id : at_id + 128].astype(F32)).astype(jnp.int32) for i in sources]
    for i in sources:
        a = chosen[i]
        take = lambda ref, at, size: ref[i, :, at : at + size].astype(F32)
        expand_down[a] += take(mid_ref, 0, width)
        shrink_up[a] += take(mid_ref, width, width)
        output_up[a] += take(mid_ref, 2 * width, width)
        output_down[a] += take(mid_ref, 3 * width, cols)
        expand_up[a] += take(mid_ref, 3 * width + cols, hid)
        shrink_down[a] += take(mid_ref, 3 * width + cols + hid, hid)
        for which in range(3):
            entry_up[a, which] += take(end_ref, which * cols, cols)
        entry_down[a] += take(end_ref, 3 * cols, width)


def sum_gradients(adapters, cols, hid, width, mid, end):
    shape = jax.ShapeDtypeStruct
    wide = shape((adapters, RANK, width), F32)
    flat = lambda a: a.reshape(a.shape[0], -1, *a.shape[-2:])
    mid, end = flat(mid), flat(end)
    outs = [
        wide, shape((adapters, 3, RANK, cols), F32), shape((adapters, RANK, cols), F32), wide,
        wide, shape((adapters, RANK, hid), F32), shape((adapters, RANK, hid), F32), wide,
    ]
    part = lambda a: pl.BlockSpec((None, *a.shape[1:]), lambda i: (i, 0, 0, 0))
    return pl.pallas_call(
        functools.partial(sum_kernel, width, cols, hid),
        grid=(mid.shape[0],),
        in_specs=[part(mid), part(end)],
        out_specs=[pl.BlockSpec(a.shape, lambda i, n=len(a.shape): (0,) * n) for a in outs],
        out_shape=outs,
        compiler_params=params(),
        name="sum_gradients",
    )(mid, end)


def local(
    tokens, cotangent, norm_first, norm_second, entry_weight, output_weight, expand_weight, shrink_weight,
    entry_down, entry_up, output_down, output_up, expand_down, expand_up, shrink_down, shrink_up,
    adapter_choice, clip_count,
):
    cap = adapter_choice.shape[0]
    rows, width = tokens.shape
    adapters = entry_down.shape[0]
    cols, hid = output_weight.shape[1], expand_weight.shape[1]
    gain_first, gain_second = norm_first.reshape(1, width), norm_second.reshape(1, width)
    flip = lambda a: a.transpose(0, 2, 1)
    w_entry = entry_weight.transpose(1, 0, 2).reshape(-1, cols)
    (
        att, lse, inner_t, thin, rep, q, k, v, k_far, v_far, normed, tok, cot, w_full, wo_full, we_near, ws_near,
        we_land, ws_land,
    ) = front_part(
        cap, adapter_choice, clip_count, gain_first,
        (flip(entry_down), output_up, flip(expand_down), shrink_up),
        (entry_up.transpose(0, 2, 1, 3), flip(output_down), expand_up, flip(shrink_down)),
        tokens, cotangent, w_entry, output_weight, expand_weight, shrink_weight,
    )
    mixed, mgrad, agrad, grads, _, _ = middle_both_ways(
        cap, tok, att, cot, gain_second, rep, thin, wo_full, we_near, ws_near, we_land, ws_land,
        expand_weight, shrink_weight,
    )
    mixed, mid_grads, token_grad, end_grads = back_part(
        cap, q, k, k_far, v, v_far, att, lse, agrad, gain_first, rep, thin, inner_t, grads, mixed, w_full, mgrad, tok,
        normed,
    )
    ed, eu, od, ou, xd, xu, sd, su = sum_gradients(adapters, cols, hid, width, mid_grads, end_grads)
    return (
        mixed, token_grad, flip(ed), eu.transpose(0, 2, 1, 3), flip(od), ou, flip(xd), xu, flip(sd), su,
    )


def solution(mesh):
    in_specs = (
        P(BOTH, None), P(BOTH, None), P(), P(),
        P("dp", None, "tensor"), P("dp", "tensor"), P("dp", "tensor"), P("dp", "tensor"),
        P(), P(None, None, None, "tensor"), P(None, "tensor", None), P(),
        P(), P(None, None, "tensor"), P(None, "tensor", None), P(), P("dp"), P("dp"),
    )
    out_specs = (
        P(BOTH, None), P(BOTH, None), P(), P(None, None, None, "tensor"), P(None, "tensor", None), P(),
        P(), P(None, None, "tensor"), P(None, "tensor", None), P(),
    )
    return jax.shard_map(local, mesh=mesh, in_specs=in_specs, out_specs=out_specs, check_vma=False)
```
